128 devices in a mesh: fsdp: 32 (over z, y, x_hi), ctx: 2 (over core), tp: 2 (over x_lo).
Axes of the slice: x: 4 (x_hi: 2, x_lo: 2; x = x_hi * 2 + x_lo), y: 4, z: 4, core: 2. Of those that a mesh axis runs over, the one named last changes fastest.
Arguments:
- tokens: bfloat16 [8192, 512], P(('fsdp', 'ctx')), may hold values from -16 to 16
- positions: int32 [8192], P(('fsdp', 'ctx')), may hold values from 0 to 2047, as said below
- cotangent: bfloat16 [8192, 512], P(('fsdp', 'ctx')), may hold values from -16 to 16
- ln1_gain: bfloat16 [1, 512], P(None, 'fsdp'), may hold values from 0.099609375 to 1.8984375
- ln1_bias: bfloat16 [1, 512], P(None, 'fsdp'), may hold values from -2 to 2
- ln2_gain: bfloat16 [1, 512], P(None, 'fsdp'), may hold values from 0.099609375 to 1.8984375
- ln2_bias: bfloat16 [1, 512], P(None, 'fsdp'), may hold values from -2 to 2
- qkv_weight: bfloat16 [1, 3, 512, 512], P(None, None, 'fsdp', 'tp'), may hold values from -0.25 to 0.25
- qkv_bias: bfloat16 [1, 3, 8, 64], P(None, None, 'tp', 'fsdp'), may hold values from -2 to 2
- out_weight: bfloat16 [1, 512, 512], P(None, 'tp', 'fsdp'), may hold values from -0.75 to 0.75
- out_bias: bfloat16 [1, 512], P(None, 'fsdp'), may hold values from -2 to 2
- up_weight: bfloat16 [1, 512, 2048], P(None, 'fsdp', 'tp'), may hold values from -0.25 to 0.25
- up_bias: bfloat16 [1, 32, 64], P(None, 'tp', 'fsdp'), may hold values from -2 to 2
- down_weight: bfloat16 [1, 2048, 512], P(None, 'tp', 'fsdp'), may hold values from -0.125 to 0.125
- down_bias: bfloat16 [1, 512], P(None, 'fsdp'), may hold values from -2 to 2
Outputs:
- output: bfloat16 [8192, 512], P(('fsdp', 'ctx'))
- grad_input: float32 [8192, 512], P(('fsdp', 'ctx'))
- grad_ln1_gain: float32 [1, 512], P(None, 'fsdp')
- grad_ln1_bias: float32 [1, 512], P(None, 'fsdp')
- grad_ln2_gain: float32 [1, 512], P(None, 'fsdp')
- grad_ln2_bias: float32 [1, 512], P(None, 'fsdp')
- grad_qkv_weight: float32 [1, 3, 512, 512], P(None, None, 'fsdp', 'tp')
- grad_qkv_bias: float32 [1, 3, 8, 64], P(None, None, 'tp', 'fsdp')
- grad_out_weight: float32 [1, 512, 512], P(None, 'tp', 'fsdp')
- grad_out_bias: float32 [1, 512], P(None, 'fsdp')
- grad_up_weight: float32 [1, 512, 2048], P(None, 'fsdp', 'tp')
- grad_up_bias: float32 [1, 32, 64], P(None, 'tp', 'fsdp')
- grad_down_weight: float32 [1, 2048, 512], P(None, 'tp', 'fsdp')
- grad_down_bias: float32 [1, 512], P(None, 'fsdp')
The draws below stay inside these ranges and needn't reach their ends.
Inputs may be any that keep to these rules, and one draw needn't show every extreme that they name: Each sequence of 256 tokens begins inside a document whose positions count up by one from some start, and from some token at or after 3 * 64 may begin a second document whose positions count up from 0.
All inputs are finite; a program needn't handle non-finite values.
Results may differ from the reference program's by a relative error of at most 0.025.
Values may be sent and summed in bfloat16 or wider, within the bound.
A program may use at most 64 MiB of HBM per device.

```python
import math
import jax
import jax.numpy as jnp
from jax import lax

D = 512
HEADS = 8
HD = 64
FF = 2048
MAXPOS = 2048
ROT = 16
LAYERS = 1
LEN = 256
TOKENS = 8192


def draw_positions(key, part):
    key = jax.random.fold_in(key, 11)
    seq_count = TOKENS // LEN
    key_start, key_split, key_pick = jax.random.split(key, 3)
    offsets = jax.random.randint(key_start, (seq_count,), 0, MAXPOS - LEN + 1)
    splits = jax.random.randint(key_split, (seq_count,), 3 * LEN // 4, LEN + 1)
    chosen = jax.random.randint(key_pick, (), 0, seq_count)
    following = (chosen + 1) % seq_count
    seq_rows = jnp.arange(seq_count)
    offsets = jnp.where(seq_rows == chosen, MAXPOS - LEN, offsets)
    splits = jnp.where(seq_rows == chosen, LEN, splits)
    offsets = jnp.where((seq_rows == following) & (seq_rows != chosen), 0, offsets)
    places = jnp.arange(LEN)
    counted = jnp.where(places[None, :] < splits[:, None], offsets[:, None] + places[None, :], places[None, :] - splits[:, None])
    return counted.reshape(TOKENS).astype(jnp.int32)


def with_spikes(drawn, stream_key, source, target, parts, factor):
    owner, partner = [(jnp.arange(drawn.shape[position]) // (drawn.shape[position] // parts)).reshape([-1 if axis == position else 1 for axis in range(drawn.ndim)]) for position in (source, target)]
    chosen = jax.random.permutation(stream_key, parts)[partner]
    strong = (owner == chosen) | (owner == (partner + parts // 2) % parts)
    return jnp.where(strong, factor * drawn, drawn)


def level_of(key, shape, shards, smallest, top_value):
    gain, own = 1.0, jax.random.fold_in(key, 6)
    for position, blocks in shards:
        draws = jnp.exp(jax.random.uniform(jax.random.fold_in(own, position), (blocks,), jnp.float32, smallest / len(shards), top_value / len(shards)))
        gain = gain * jnp.repeat(draws, shape[position] // blocks).reshape([-1 if axis == position else 1 for axis in range(len(shape))])
    return gain


def scatter_about(key, dims, spread, bound, cuts=(), kind=jnp.bfloat16):
    entries = jax.random.normal(key, dims, jnp.float32) * spread
    if len(cuts) > 0:
        entries = level_of(key, dims, cuts, -0.22, 0.18) * entries
    return jnp.clip(entries, min=-bound, max=bound).astype(kind)


def heavy_noise(key, extent, width, limit, pieces, heavy, kind=jnp.bfloat16):
    entries = width * jax.random.normal(key, extent, jnp.float32)
    if pieces:
        entries = entries * level_of(key, extent, pieces, -0.22, 0.18)
    return jnp.clip(with_spikes(entries, jax.random.fold_in(key, 3), *heavy), -limit, limit).astype(kind)


def setup_inputs(seed: int = 0) -> dict:
    key_of = jax.random.split(jax.random.key(seed), 16)
    tokens = heavy_noise(key_of[0], (TOKENS, D), 1.0, 16.0, ((0, 64),), (0, 1, 64, 4.0))
    positions = draw_positions(jax.random.fold_in(key_of[15], 71), 0)
    cotangent = heavy_noise(key_of[2], (TOKENS, D), 1.0, 16.0, ((0, 64),), (0, 1, 64, 4.0))
    ln1_gain = jnp.clip(1.0 + 0.18 * jax.random.normal(key_of[3], (LAYERS, D), jnp.float32), 0.099609375, 1.8984375).astype(jnp.bfloat16)
    ln1_bias = scatter_about(key_of[4], (LAYERS, D), 0.3, 2.0, ((1, 32),))
    ln2_gain = jnp.clip(1.0 + 0.18 * jax.random.normal(key_of[5], (LAYERS, D), jnp.float32), 0.099609375, 1.8984375).astype(jnp.bfloat16)
    ln2_bias = scatter_about(key_of[6], (LAYERS, D), 0.3, 2.0, ((1, 32),))
    qkv_weight = scatter_about(key_of[7], (LAYERS, 3, D, HEADS * HD), D ** -0.5, 0.25, ((2, 32), (3, 2)))
    qkv_bias = scatter_about(key_of[8], (LAYERS, 3, HEADS, HD), 0.3, 2.0, ((2, 2), (3, 32)))
    out_weight = scatter_about(key_of[9], (LAYERS, HEADS * HD, D), HD ** -0.5, 0.75, ((1, 2), (2, 32)))
    out_bias = scatter_about(key_of[10], (LAYERS, D), 0.3, 2.0, ((1, 32),))
    up_weight = scatter_about(key_of[11], (LAYERS, D, FF), D ** -0.5, 0.25, ((1, 32), (2, 2)))
    up_bias = scatter_about(key_of[12], (LAYERS, FF // HD, HD), 0.3, 2.0, ((1, 2), (2, 32)))
    down_weight = scatter_about(key_of[13], (LAYERS, FF, D), FF ** -0.5, 0.125, ((1, 2), (2, 32)))
    down_bias = scatter_about(key_of[14], (LAYERS, D), 0.3, 2.0, ((1, 32),))
    return dict(tokens=tokens, positions=positions, cotangent=cotangent, ln1_gain=ln1_gain, ln1_bias=ln1_bias, ln2_gain=ln2_gain, ln2_bias=ln2_bias, qkv_weight=qkv_weight, qkv_bias=qkv_bias, out_weight=out_weight, out_bias=out_bias, up_weight=up_weight, up_bias=up_bias, down_weight=down_weight, down_bias=down_bias)


EPS = 1e-05
BASE = 10000.0
MASKED = -1e+30

@jax.custom_vjp
def low(v):
    return lax.optimization_barrier(v.astype(jnp.bfloat16)).astype(jnp.float32)

@jax.custom_vjp
def low_back(v):
    return v

def low_keep(v):
    return (low(v), None)

def low_pass(kept, grad):
    return (grad,)

def back_keep(v):
    return (v, None)

def back_low(kept, grad):
    return (low(grad),)
low.defvjp(low_keep, low_pass)
low_back.defvjp(back_keep, back_low)

def layer_norm(inputs, scale_vec, shift_vec):
    row_mean = lax.optimization_barrier(jnp.mean(inputs, axis=-1, keepdims=True))
    centered = inputs - row_mean
    moment = lax.optimization_barrier(jnp.mean(centered * centered, axis=-1, keepdims=True))
    return centered * lax.rsqrt(moment + EPS) * scale_vec + shift_vec

def turn_tables(places):
    half_rot = ROT // 2
    freq_index = jnp.arange(half_rot, dtype=jnp.float32)
    inverse = BASE ** (-2.0 * freq_index / ROT)
    angles = places.astype(jnp.float32)[..., None] * inverse
    return (jnp.cos(angles), jnp.sin(angles))

def rotate(inputs, cos_table, sin_table):
    half_rot = ROT // 2
    cos_heads = cos_table[..., None, :]
    sin_heads = sin_table[..., None, :]
    low_part = inputs[..., :half_rot]
    high_part = inputs[..., half_rot:ROT]
    return jnp.concatenate([low_part * cos_heads - high_part * sin_heads, high_part * cos_heads + low_part * sin_heads, inputs[..., ROT:]], axis=-1)

def attend(item):
    query_heads, key_heads, value_heads, visible = item
    score_scale = 1.0 / math.sqrt(HD)
    highest = lax.Precision.HIGHEST
    scores = low_back(score_scale * jnp.einsum('shd,thd->hst', query_heads, key_heads, precision=highest))
    scores = jnp.where(visible[None], scores, MASKED)
    row_max = lax.optimization_barrier(jnp.max(scores, axis=-1, keepdims=True))
    exp_scores = jnp.exp(scores - row_max)
    soft_probs = exp_scores / lax.optimization_barrier(jnp.sum(exp_scores, axis=-1, keepdims=True))
    return jnp.einsum('hst,thd->shd', low(soft_probs), value_heads, precision=highest)

def layer(residual, weights, cos_table, sin_table, visible):
    gain_one, shift_one, gain_two, shift_two, w_qkv, b_qkv, w_out, b_out, w_up, b_up, w_down, b_down = weights
    highest = lax.Precision.HIGHEST
    group_count = residual.shape[0]
    seq_len = residual.shape[1]
    normed = low(layer_norm(residual, gain_one, shift_one))
    mlp_input = low(layer_norm(residual, gain_two, shift_two))
    projected = low_back(jnp.einsum('psd,cdf->cpsf', normed, w_qkv, precision=highest) + b_qkv.reshape(3, 1, 1, HEADS * HD))
    head_shape = (group_count, seq_len, HEADS, HD)
    query_heads = low(rotate(projected[0].reshape(head_shape), cos_table, sin_table))
    key_heads = low(rotate(projected[1].reshape(head_shape), cos_table, sin_table))
    value_heads = low(projected[2].reshape(head_shape))
    attended = lax.map(jax.checkpoint(attend), (query_heads, key_heads, value_heads, visible))
    attended = low(low_back(attended.reshape(group_count, seq_len, HEADS * HD)))
    pre_act = low_back(jnp.einsum('psd,df->psf', mlp_input, w_up, precision=highest) + b_up.reshape(FF))
    activated = low(jax.nn.gelu(pre_act, approximate=False))
    attn_branch = jnp.einsum('psf,fd->psd', attended, w_out, precision=highest) + b_out
    mlp_branch = jnp.einsum('psf,fd->psd', activated, w_down, precision=highest) + b_down
    return residual + low_back(attn_branch + mlp_branch)

def forward(block_in, block_pos, params):
    seq_index = jnp.arange(LEN, dtype=jnp.int32)
    doc_start = seq_index[None, :] - block_pos
    visible = (seq_index[None, None, :] <= seq_index[None, :, None]) & (seq_index[None, None, :] >= doc_start[:, :, None])
    cos_table, sin_table = turn_tables(block_pos)
    residual = block_in
    for layer_at in range(LAYERS):
        residual = layer(residual, tuple((stacked[layer_at] for stacked in params)), cos_table, sin_table, visible)
    return residual

def reference(tokens, positions, cotangent, ln1_gain, ln1_bias, ln2_gain, ln2_bias, qkv_weight, qkv_bias, out_weight, out_bias, up_weight, up_bias, down_weight, down_bias):
    params = tuple((stacked.astype(jnp.float32) for stacked in (ln1_gain, ln1_bias, ln2_gain, ln2_bias, qkv_weight, qkv_bias, out_weight, out_bias, up_weight, up_bias, down_weight, down_bias)))
    seq_count = TOKENS // LEN
    per_group = math.gcd(seq_count, max(1, 4096 // LEN))
    group_count = seq_count // per_group
    inputs = tokens.astype(jnp.float32).reshape(group_count, per_group, LEN, D)
    places = positions.reshape(group_count, per_group, LEN)
    cot_groups = cotangent.astype(jnp.float32).reshape(group_count, per_group, LEN, D)

    def step_group(totals, item):
        block_in, block_pos, block_cot = item
        result, pull = jax.vjp(lambda x_in, weights: forward(x_in, block_pos, weights), block_in, params)
        grad_in, grad_weights = pull(block_cot)
        return (jax.tree.map(jnp.add, totals, grad_weights), (result, grad_in))
    zeros_tree = jax.tree.map(jnp.zeros_like, params)
    totals, (results, grad_ins) = lax.scan(step_group, zeros_tree, (inputs, places, cot_groups))
    output = results.reshape(TOKENS, D).astype(jnp.bfloat16)
    grad_input = grad_ins.reshape(TOKENS, D)
    return (output, grad_input, totals[0], totals[1], totals[2], totals[3], totals[4], totals[5], totals[6], totals[7], totals[8], totals[9], totals[10], totals[11])
```

```python
import math

import jax
import jax.numpy as jnp
import numpy as np
from jax import lax
from jax.experimental import pallas as pl
from jax.experimental.pallas import tpu as pltpu
from jax.sharding import PartitionSpec as P

HD = 64
ROT = 16
EPS = 1e-05
BASE = 10000.0
MASKED = -1e30
SCALE = 1.0 / math.sqrt(HD)
INV_ROOT_TWO = 1.0 / math.sqrt(2.0)
INV_ROOT_TWO_PI = 1.0 / math.sqrt(2.0 * math.pi)
MESH = pl.DeviceIdType.MESH
F32 = jnp.float32
BF16 = jnp.bfloat16

UP = slice(0, 256)
QK = slice(256, 384)
DN = slice(384, 640)
VO = slice(640, 768)
HALF = (slice(0, 384), slice(384, 768))

M_XW, M_XE = 0, 1
M_POS = 2
M_TOK = 5
M_COT = 8
M_AG1 = 12
M_AGE1 = 18
M_AG2 = 21
M_AGE2 = 27
M_OUT = 30
M_DX = 34
M_RS1 = 38
M_RSE1 = 44
M_RS2 = 47
M_RSE2 = 53
M_FIN = 56
M_FINE = 59
M_ALL = 66


def dot_nn(left, right):
    return lax.dot_general(left, right, (((1,), (0,)), ((), ())), preferred_element_type=F32)


def dot_nt(left, right):
    return lax.dot_general(left, right, (((1,), (1,)), ((), ())), preferred_element_type=F32)


def dot_tn(left, right):
    return lax.dot_general(left, right, (((0,), (0,)), ((), ())), preferred_element_type=F32)


def iota(shape, dim):
    return lax.broadcasted_iota(jnp.int32, shape, dim)


def turn_partner(pair):
    lane = iota(pair.shape, 1) % HD
    return jnp.where(
        lane < ROT // 2, pltpu.roll(pair, pair.shape[1] - ROT // 2, 1), pltpu.roll(pair, ROT // 2, 1)
    )


def kernel(
    tok_in, pos_in, cot_in, gain1, shift1, gain2, shift2, qkv_w, qkv_b, out_w, out_b, up_w, up_b, down_w, down_b,
    out_o, gin_o, gg1_o, gb1_o, gg2_o, gb2_o, gqkvw_o, gqkvb_o, goutw_o, gbias_o, gupw_o, gupb_o, gdownw_o,
    W, XS, E, XE, TK, CT, PS, SM,
    NRM, RSQ, NB, MB, NTR, MTR, BTR, COS, SIN, PCOL,
    GC, GVZ, ATZ, PO, RO, SO, XO, PD, RD, SD, XD,
    GS, RA1, RB1, SA, SB, RA2, RB2, EG, RE1, SE, RE2, FB, XR, FE, XF,
    ss, rs,
):
    place = lax.axis_index("fsdp")
    z, y, xh = place // 8, (place // 2) % 4, place % 2
    c = lax.axis_index("ctx")
    t = lax.axis_index("tp")
    ox, oc, ot = 1 - xh, 1 - c, 1 - t

    def dev(xx, cc, tt, zz=z, yy=y):
        return {"fsdp": zz * 8 + yy * 2 + xx, "ctx": cc, "tp": tt}

    def zdev(k):
        return dev(xh, c, t, zz=(z + k) % 4)

    def ydev(k):
        return dev(xh, c, t, yy=(y + k) % 4)

    def send(number, src, dst, where):
        copy = pltpu.make_async_remote_copy(
            src_ref=src, dst_ref=dst, send_sem=ss.at[number], recv_sem=rs.at[number],
            device_id=where, device_id_type=MESH,
        )
        copy.start()
        return copy

    sent = []

    def track(copy):
        sent.append(copy)
        return copy

    barrier = pltpu.get_barrier_semaphore()
    group = [
        dev(xh, oc, t), dev(ox, c, t), dev(ox, c, ot), dev(ox, oc, t), dev(xh, c, ot), dev(xh, oc, ot), dev(ox, oc, ot)
    ]
    peers = group + [zdev(k) for k in (1, 2, 3)] + [ydev(k) for k in (1, 2, 3)]
    for peer in peers:
        pl.semaphore_signal(barrier, inc=1, device_id=peer, device_id_type=MESH)

    def cut(xx):
        lanes = pl.ds(pl.multiple_of(xx * 128, 128), 128)
        q_pair, k_pair, v_pair, o_pair = (
            ref[:, lanes].astype(F32) for ref in (qkv_w.at[0], qkv_w.at[1], qkv_w.at[2], out_w)
        )
        low = iota((16, 128), 1) < HD
        first = c == 0

        def halves(a, b):
            a_low = jnp.where(first, a, pltpu.roll(a, HD, 1))
            b_high = jnp.where(first, pltpu.roll(b, HD, 1), b)
            return jnp.where(low, a_low, b_high).astype(BF16)

        wide = pl.ds(pl.multiple_of((xx * 2 + c) * 256, 256), 256)
        return up_w[:, wide], halves(q_pair, k_pair), down_w[:, wide], halves(v_pair, o_pair)

    for target, xx in ((XS, ox), (W.at[z, y, xh], xh)):
        up_cut, qk_cut, down_cut, vo_cut = cut(xx)
        target[:, UP] = up_cut
        target[:, QK] = qk_cut
        target[:, DN] = down_cut
        target[:, VO] = vo_cut

    SM[...] = jnp.zeros((16, 128), F32)
    for row, ref in enumerate((gain1, shift1, gain2, shift2, out_b, down_b)):
        SM[row : row + 1, 0:16] = ref[...].astype(F32)
    for which in range(3):
        SM[8 + 2 * which : 10 + 2 * which, 0:4] = qkv_b[which].astype(F32)
    SM[6:8, 0:16] = up_b[...].astype(F32)
    SM[14:16, 0:16] = up_b[...].astype(F32)

    row16, lane16 = iota((16, 128), 0), iota((16, 128), 1)

    def placed(xx):
        raw = SM[...]
        head = xx * 2 + c

        def column(lane):
            return jnp.sum(jnp.where(lane16 == lane, raw, 0.0), axis=1, keepdims=True)

        spread = pltpu.roll(raw, 16 * (y * 2 + xh), 1)
        low = lane16 < HD
        hit = (lane16 % HD) == 2 * place + row16 % 2
        qkv = jnp.where(low != ((row16 == 10) | (row16 == 11)), column(head), 0.0)
        up_first = jnp.where(low, column(4 * head), column(4 * head + 1))
        up_second = jnp.where(low, column(4 * head + 2), column(4 * head + 3))
        bias = jnp.where(row16 < 8, up_first, jnp.where(row16 < 14, qkv, up_second))
        return jnp.where(row16 < 6, spread, jnp.where(hit, bias, 0.0))

    XE[0] = placed(ox).astype(BF16)
    XE[1] = placed(xh).astype(BF16)

    TK[xh, c] = tok_in[...]
    CT[xh, c] = cot_in[...]
    PS[xh, c] = pos_in[...]

    pl.semaphore_wait(barrier, len(peers))

    xw = track(send(M_XW, XS, W.at[z, y, xh], dev(ox, c, t)))
    xe = track(send(M_XE, XE.at[0], XE.at[2], dev(ox, c, t)))
    across = dev(ox, c, ot)
    core = dev(xh, oc, t)
    tok_across = track(send(M_TOK, tok_in, TK.at[xh, c], across))
    tok_core = track(send(M_TOK + 1, tok_in, TK.at[xh, c], core))
    pos_copies = [
        track(send(M_POS + i, pos_in, PS.at[xh, c], where))
        for i, where in enumerate((core, dev(ox, c, t), dev(ox, oc, t)))
    ]
    cot_across = track(send(M_COT, cot_in, CT.at[xh, c], across))
    cot_core = track(send(M_COT + 1, cot_in, CT.at[xh, c], core))

    xw.wait_recv()
    ag1 = []
    for k in (2, 1, 3):
        here = W.at[z, y, :, :, HALF[0]]
        ag1.append(track(send(M_AG1 + k - 1, here, here, zdev(k))))
        here = W.at[z, y, :, :, HALF[1]]
        ag1.append(track(send(M_AG1 + 3 + k - 1, here, here, ydev(k))))
    xe.wait_recv()
    E[z, y] = (XE[1].astype(F32) + XE[2].astype(F32)).astype(BF16)
    for k in (2, 1, 3):
        ag1.append(track(send(M_AGE1 + k - 1, E.at[z, y], E.at[z, y], zdev(k))))
    tok_across.wait_recv()
    tok_pass = track(send(M_TOK + 2, TK.at[ox, c], TK.at[ox, c], core))
    for copy in ag1:
        copy.wait_recv()
    ag2 = []
    age2 = []
    for k in (2, 1, 3):
        age2.append(track(send(M_AGE2 + k - 1, E.at[:, y], E.at[:, y], ydev(k))))
    for k in (2, 1, 3):
        here = W.at[:, y, :, :, HALF[0]]
        ag2.append(track(send(M_AG2 + k - 1, here, here, ydev(k))))
        here = W.at[z, :, :, :, HALF[1]]
        ag2.append(track(send(M_AG2 + 3 + k - 1, here, here, zdev(k))))
    cot_across.wait_recv()
    cot_pass = track(send(M_COT + 2, CT.at[ox, c], CT.at[ox, c], core))
    tok_core.wait_recv()
    tok_pass.wait_recv()

    for s in range(2):
        rows = TK[s].reshape(256, 512).astype(F32)
        centered = rows - jnp.mean(rows, axis=1, keepdims=True)
        moment = jnp.mean(centered * centered, axis=1, keepdims=True)
        rsq = lax.rsqrt(moment + EPS)
        NRM[s] = centered * rsq
        RSQ[s] = jnp.broadcast_to(rsq, (256, 128))

    for copy in pos_copies:
        copy.wait_recv()
    row8 = iota((8, 128), 0)
    inverse = jnp.zeros((8, 128), F32)
    for r in range(ROT // 2):
        inverse = jnp.where(row8 == r, float(np.float32(BASE ** (-2.0 * r / ROT))), inverse)
    ones, zeros = jnp.ones((48, 128), F32), jnp.zeros((48, 128), F32)
    for s in range(2):
        for b in range(2):
            places = PS[s, b].astype(F32)
            angle = jnp.broadcast_to(places, (8, 128)) * inverse
            cos, sin = jnp.cos(angle), jnp.sin(angle)
            part = pl.ds(b * 128, 128)
            COS[s, part] = jnp.concatenate([cos, cos, ones, cos, cos, ones], axis=0).T
            SIN[s, part] = jnp.concatenate([-sin, sin, zeros, -sin, sin, zeros], axis=0).T
            PCOL[s, part] = jnp.broadcast_to(places, (128, 128)).T

    cot_core.wait_recv()
    cot_pass.wait_recv()
    bias_grad = jnp.zeros((1, 512), F32)
    for s in range(2):
        grad = CT[s].reshape(256, 512)
        BTR[:, s * 256 : (s + 1) * 256] = grad.T
        bias_grad = bias_grad + jnp.sum(grad.astype(F32), axis=0, keepdims=True)

    for copy in age2:
        copy.wait_recv()
    per_z = []
    for zz in range(4):
        total = E[zz, 0].astype(F32)
        for yy in range(1, 4):
            total = total + E[zz, yy].astype(F32)
        per_z.append(total)
    vectors = jnp.concatenate(per_z, axis=1)
    all_z = per_z[0] + per_z[1] + per_z[2] + per_z[3]
    g1, b1, g2, b2 = (vectors[r : r + 1] for r in range(4))
    b_branch = vectors[4:5] + vectors[5:6]
    b_up = jnp.concatenate([all_z[6:7] + all_z[7:8], all_z[14:15] + all_z[15:16]], axis=1)
    b_qk = all_z[8:9] + all_z[9:10] + all_z[10:11] + all_z[11:12]
    b_v = (all_z[12:13] + all_z[13:14])[:, :HD]

    for s in range(2):
        n = NRM[s]
        normed = (n * g1 + b1).astype(BF16)
        mlp_input = (n * g2 + b2).astype(BF16)
        NB[s] = normed
        MB[s] = mlp_input
        NTR[:, s * 256 : (s + 1) * 256] = normed.T
        MTR[:, s * 256 : (s + 1) * 256] = mlp_input.T

    for copy in ag2:
        copy.wait_recv()

    gb_up = jnp.zeros((1, 256), F32)
    gb_qk = jnp.zeros((1, 128), F32)
    gb_v = jnp.zeros((1, HD), F32)
    for s in range(2):
        part = slice(s * 256, (s + 1) * 256)
        normed, mlp_input, branch_grad = NB[s], MB[s], CT[s].reshape(256, 512)
        w_up = W[:, :, :, :, UP].reshape(512, 256)
        w_down = W[:, :, :, :, DN].reshape(512, 256)
        w_qk = W[:, :, :, :, QK].reshape(512, 128)
        w_vo = W[:, :, :, :, VO].reshape(512, 128)
        pre_act = dot_nn(mlp_input, w_up) + b_up
        phi = 0.5 * (1.0 + lax.erf(pre_act * INV_ROOT_TWO))
        density = jnp.exp(-0.5 * pre_act * pre_act) * INV_ROOT_TWO_PI
        activated = (pre_act * phi).astype(BF16)
        grad_pre = (dot_nn(branch_grad, w_down) * (phi + pre_act * density)).astype(BF16)
        gb_up = gb_up + jnp.sum(grad_pre.astype(F32), axis=0, keepdims=True)
        GC[part, UP] = grad_pre
        GC[part, DN] = activated

        cos, sin = COS[s], SIN[s]
        qk = dot_nn(normed, w_qk) + b_qk
        qk = (qk * cos + turn_partner(qk) * sin).astype(BF16)
        query, key = qk[:, :HD], qk[:, HD:]
        value = (dot_nn(normed, w_vo)[:, :HD] + b_v).astype(BF16)
        grad_att = dot_nn(branch_grad, w_vo)[:, HD:].astype(BF16)
        row, col = iota((256, 256), 0), iota((256, 256), 1)
        start = row.astype(F32) - jnp.concatenate([PCOL[s], PCOL[s]], axis=1)
        visible = (col <= row) & (col.astype(F32) >= start)
        scores = jnp.where(visible, dot_nt(query, key) * SCALE, MASKED)
        exps = jnp.exp(scores - jnp.max(scores, axis=1, keepdims=True))
        probs = exps / jnp.sum(exps, axis=1, keepdims=True)
        probs_low = probs.astype(BF16)
        attended = dot_nn(probs_low, value).astype(BF16)
        grad_probs = dot_nt(grad_att, value)
        row_dot = jnp.sum(probs * grad_probs, axis=1, keepdims=True)
        grad_scores = (probs * (grad_probs - row_dot)).astype(BF16)
        grad_query = dot_nn(grad_scores, key) * SCALE
        grad_key = dot_tn(grad_scores, query) * SCALE
        grad_value = dot_tn(probs_low, grad_att).astype(BF16)
        grad_qk = jnp.concatenate([grad_query, grad_key], axis=1)
        grad_qk = (grad_qk * cos - turn_partner(grad_qk) * sin).astype(BF16)
        gb_qk = gb_qk + jnp.sum(grad_qk.astype(F32), axis=0, keepdims=True)
        gb_v = gb_v + jnp.sum(grad_value.astype(F32), axis=0, keepdims=True)
        blank = jnp.zeros((256, HD), BF16)
        GC[part, QK] = grad_qk
        GVZ[part] = jnp.concatenate([grad_value, blank], axis=1)
        ATZ[part] = jnp.concatenate([blank, attended], axis=1)
        branch = dot_nt(activated, w_down) + dot_nt(ATZ[part], w_vo)
        PO[s] = branch.astype(BF16).reshape(2, 128, 512)

    out_core = track(send(M_OUT, PO.at[:, oc], RO, core))

    GS[:, :, :, UP] = dot_nn(MTR[...], GC[:, UP]).astype(BF16).reshape(4, 4, 32, 256)
    GS[:, :, :, QK] = dot_nn(NTR[...], GC[:, QK]).astype(BF16).reshape(4, 4, 32, 128)
    rs1 = []
    for k in (2, 1, 3):
        rs1.append(track(send(M_RS1 + k - 1, GS.at[:, (y + k) % 4, :, HALF[0]], RA1.at[k - 1], ydev(k))))
    GS[:, :, :, DN] = dot_nn(BTR[...], GC[:, DN]).astype(BF16).reshape(4, 4, 32, 256)
    grad_vo = dot_nn(NTR[...], GVZ[...]) + dot_nn(BTR[...], ATZ[...])
    GS[:, :, :, VO] = grad_vo.astype(BF16).reshape(4, 4, 32, 128)
    for k in (2, 1, 3):
        rs1.append(track(send(M_RS1 + 3 + k - 1, GS.at[(z + k) % 4, :, :, HALF[1]], RB1.at[k - 1], zdev(k))))

    out_core.wait_recv()
    SO[...] = (PO[:, c].astype(F32) + RO[...].astype(F32)).astype(BF16)
    out_copies = [
        track(send(M_OUT + 1, SO.at[ox], XO.at[0], dev(ox, c, ot))),
        track(send(M_OUT + 2, SO.at[ox], XO.at[1], dev(ox, c, t))),
        track(send(M_OUT + 3, SO.at[xh], XO.at[2], dev(xh, c, ot))),
    ]

    totals = [jnp.zeros((1, 512), F32) for _ in range(4)]
    for s in range(2):
        part = slice(s * 256, (s + 1) * 256)
        w_up = W[:, :, :, :, UP].reshape(512, 256)
        w_qk = W[:, :, :, :, QK].reshape(512, 128)
        w_vo = W[:, :, :, :, VO].reshape(512, 128)
        n = NRM[s]
        grad_mlp = dot_nt(GC[part, UP], w_up)
        grad_normed = dot_nt(GC[part, QK], w_qk) + dot_nt(GVZ[part], w_vo)
        for i, term in enumerate((grad_normed * n, grad_normed, grad_mlp * n, grad_mlp)):
            totals[i] = totals[i] + jnp.sum(term, axis=0, keepdims=True)
        joined = grad_normed * g1 + grad_mlp * g2
        mean_one = jnp.mean(joined, axis=1, keepdims=True)
        mean_two = jnp.mean(joined * n, axis=1, keepdims=True)
        term = RSQ[s][:, :1] * (joined - mean_one - n * mean_two)
        PD[s] = term.astype(BF16).reshape(2, 128, 512)
    dx_core = track(send(M_DX, PD.at[:, oc], RD, core))

    up_rows = jnp.concatenate([gb_up[:, :128], gb_up[:, 128:]], axis=0)
    v_row = jnp.concatenate([gb_v, jnp.zeros((1, 128 - HD), F32)], axis=1)
    for zz in range(4):
        lanes = slice(zz * 128, (zz + 1) * 128)
        pieces = [total[:, lanes] for total in totals] + [bias_grad[:, lanes], gb_qk, v_row, up_rows]
        EG[zz] = jnp.concatenate(pieces + [jnp.zeros((7, 128), F32)], axis=0).astype(BF16)
    rse1 = [track(send(M_RSE1 + k - 1, EG, RE1.at[k - 1], ydev(k))) for k in (2, 1, 3)]

    dx_core.wait_recv()
    SD[...] = (PD[:, c].astype(F32) + RD[...].astype(F32)).astype(BF16)
    dx_copies = [
        track(send(M_DX + 1, SD.at[ox], XD.at[0], dev(ox, c, ot))),
        track(send(M_DX + 2, SD.at[ox], XD.at[1], dev(ox, c, t))),
        track(send(M_DX + 3, SD.at[xh], XD.at[2], dev(xh, c, ot))),
    ]

    for copy in rs1:
        copy.wait_recv()

    def summed(own, received):
        total = own.astype(F32)
        for k in range(3):
            total = total + received[k].astype(F32)
        return total

    SA[...] = summed(GS[:, y, :, HALF[0]], RA1).astype(BF16)
    rs2 = [track(send(M_RS2 + k - 1, SA.at[(z + k) % 4], RA2.at[k - 1], zdev(k))) for k in (2, 1, 3)]
    SB[...] = summed(GS[z, :, :, HALF[1]], RB1).astype(BF16)
    rs2 += [track(send(M_RS2 + 3 + k - 1, SB.at[(y + k) % 4], RB2.at[k - 1], ydev(k))) for k in (2, 1, 3)]
    for copy in rse1:
        copy.wait_recv()
    SE[...] = summed(EG[...], RE1).astype(BF16)
    rse2 = [track(send(M_RSE2 + k - 1, SE.at[(z + k) % 4], RE2.at[k - 1], zdev(k))) for k in (2, 1, 3)]

    def over_chips(own, received):
        return (own.astype(F32) + received[2].astype(F32)) + (received[0].astype(F32) + received[1].astype(F32))

    for copy in out_copies:
        copy.wait_recv()
    out_o[...] = (tok_in[...].astype(F32) + (over_chips(SO[xh], XO) + b_branch)).astype(BF16)
    for copy in dx_copies:
        copy.wait_recv()
    gin_o[...] = cot_in[...].astype(F32) + over_chips(SD[xh], XD)

    for copy in rs2:
        copy.wait_recv()
    FB[:, :, HALF[0]] = summed(SA[z], RA2).astype(BF16).reshape(2, 16, 384)
    FB[:, :, HALF[1]] = summed(SB[y], RB2).astype(BF16).reshape(2, 16, 384)
    fin = [
        track(send(M_FIN, FB.at[ox], XR.at[xh, c], dev(ox, c, t))),
        track(send(M_FIN + 1, FB.at[ox], XR.at[xh, c], dev(ox, oc, t))),
        track(send(M_FIN + 2, FB.at[xh], XR.at[xh, c], dev(xh, oc, t))),
    ]
    XR[xh, c] = FB[xh]
    for copy in rse2:
        copy.wait_recv()
    FE[...] = summed(SE[z], RE2).astype(BF16)
    fine = [track(send(M_FINE + i, FE, XF.at[t, xh, c], where)) for i, where in enumerate(group)]
    XF[t, xh, c] = FE[...]

    for copy in fin:
        copy.wait_recv()
    for xx in range(2):
        both = [XR[xx, 0].astype(F32), XR[xx, 1].astype(F32)]
        lanes = slice(xx * 128, (xx + 1) * 128)
        low = iota((16, 128), 1) < HD

        def join(first, second):
            return jnp.where(low, first, pltpu.roll(second, HD, 1)), jnp.where(low, pltpu.roll(first, HD, 1), second)

        q_new, k_new = join(both[0][:, QK], both[1][:, QK])
        v_new, o_new = join(both[0][:, VO], both[1][:, VO])
        gqkvw_o[0, :, lanes] = q_new
        gqkvw_o[1, :, lanes] = k_new
        gqkvw_o[2, :, lanes] = v_new
        goutw_o[:, lanes] = o_new
        for cc in range(2):
            wide = slice((xx * 2 + cc) * 256, (xx * 2 + cc + 1) * 256)
            gupw_o[:, wide] = both[cc][:, UP]
            gdownw_o[:, wide] = both[cc][:, DN]

    for copy in fine:
        copy.wait_recv()
    tiles = [[[XF[tt, xx, cc].astype(F32) for cc in range(2)] for xx in range(2)] for tt in range(2)]
    whole = jnp.zeros((16, 128), F32)
    for tt in range(2):
        for xx in range(2):
            for cc in range(2):
                whole = whole + tiles[tt][xx][cc]
    whole = jnp.where(row16 == 4, tiles[0][0][0], whole)
    whole = pltpu.roll(whole, (128 - 16 * (y * 2 + xh)) % 128, 1)
    for row, ref in enumerate((gg1_o, gb1_o, gg2_o, gb2_o, gbias_o)):
        ref[...] = whole[row : row + 1, 0:16]
    j4, h4 = iota((2, 4), 0), iota((2, 4), 1)
    j16, h16 = iota((2, 16), 0), iota((2, 16), 1)
    new_qkv = [jnp.zeros((2, 4), F32) for _ in range(3)]
    new_up = jnp.zeros((2, 16), F32)
    for xx in range(2):
        for cc in range(2):
            head = xx * 2 + cc
            tile = jnp.where(t == 0, tiles[0][xx][cc], tiles[1][xx][cc])
            for j in range(2):
                low_col = jnp.sum(jnp.where(lane16 == 2 * place + j, tile, 0.0), axis=1, keepdims=True)
                high_col = jnp.sum(jnp.where(lane16 == HD + 2 * place + j, tile, 0.0), axis=1, keepdims=True)
                spot = (j4 == j) & (h4 == head)
                for which, item in enumerate((low_col[5:6], high_col[5:6], low_col[6:7])):
                    new_qkv[which] = jnp.where(spot, item, new_qkv[which])
                for u, item in enumerate((low_col[7:8], high_col[7:8], low_col[8:9], high_col[8:9])):
                    new_up = jnp.where((j16 == j) & (h16 == head * 4 + u), item, new_up)
    for which in range(3):
        gqkvb_o[which] = new_qkv[which]
    gupb_o[...] = new_up

    for copy in sent:
        copy.wait_send()


def body(
    tokens, positions, cotangent, ln1_gain, ln1_bias, ln2_gain, ln2_bias, qkv_weight, qkv_bias, out_weight, out_bias,
    up_weight, up_bias, down_weight, down_bias,
):
    vmem = pl.BlockSpec(memory_space=pltpu.VMEM)
    shape = jax.ShapeDtypeStruct
    row = shape((1, 16), F32)
    operands = (
        tokens, positions.reshape(1, 128), cotangent, ln1_gain, ln1_bias, ln2_gain, ln2_bias, qkv_weight[0],
        qkv_bias[0].transpose(0, 2, 1), out_weight[0].T, out_bias, up_weight[0], up_bias[0].T, down_weight[0].T,
        down_bias,
    )
    outs = (
        shape((128, 512), BF16), shape((128, 512), F32), row, row, row, row, shape((3, 16, 256), F32),
        shape((3, 2, 4), F32), shape((16, 256), F32), row, shape((16, 1024), F32), shape((2, 16), F32),
        shape((16, 1024), F32),
    )
    scratch = [
        ((4, 4, 2, 16, 768), BF16), ((16, 768), BF16), ((4, 4, 16, 128), BF16), ((3, 16, 128), BF16),
        ((2, 2, 128, 512), BF16), ((2, 2, 128, 512), BF16), ((2, 2, 1, 128), jnp.int32), ((16, 128), F32),
        ((2, 256, 512), F32), ((2, 256, 128), F32), ((2, 256, 512), BF16), ((2, 256, 512), BF16),
        ((512, 512), BF16), ((512, 512), BF16), ((512, 512), BF16),
        ((2, 256, 128), F32), ((2, 256, 128), F32), ((2, 256, 128), F32),
        ((512, 768), BF16), ((512, 128), BF16), ((512, 128), BF16),
        ((2, 2, 128, 512), BF16), ((2, 128, 512), BF16), ((2, 128, 512), BF16), ((3, 128, 512), BF16),
        ((2, 2, 128, 512), BF16), ((2, 128, 512), BF16), ((2, 128, 512), BF16), ((3, 128, 512), BF16),
        ((4, 4, 32, 768), BF16), ((3, 4, 32, 384), BF16), ((3, 4, 32, 384), BF16), ((4, 32, 384), BF16),
        ((4, 32, 384), BF16), ((3, 32, 384), BF16), ((3, 32, 384), BF16),
        ((4, 16, 128), BF16), ((3, 4, 16, 128), BF16), ((4, 16, 128), BF16), ((3, 16, 128), BF16),
        ((2, 16, 768), BF16), ((2, 2, 16, 768), BF16), ((16, 128), BF16), ((2, 2, 2, 16, 128), BF16),
    ]
    results = pl.pallas_call(
        kernel,
        out_shape=outs,
        in_specs=[vmem] * len(operands),
        out_specs=[vmem] * len(outs),
        scratch_shapes=[pltpu.VMEM(*item) for item in scratch]
        + [pltpu.SemaphoreType.DMA((M_ALL,)), pltpu.SemaphoreType.DMA((M_ALL,))],
        compiler_params=pltpu.CompilerParams(
            collective_id=0, has_side_effects=True, vmem_limit_bytes=48 * 1024 * 1024
        ),
    )(*operands)
    (
        output, grad_input, grad_gain1, grad_shift1, grad_gain2, grad_shift2, grad_qkv, grad_qkv_bias, grad_out,
        grad_bias, grad_up, grad_up_bias, grad_down,
    ) = results
    return (
        output, grad_input, grad_gain1, grad_shift1, grad_gain2, grad_shift2, grad_qkv[None],
        grad_qkv_bias.transpose(0, 2, 1)[None], grad_out.T[None], grad_bias, grad_up[None], grad_up_bias.T[None],
        grad_down.T[None], grad_bias,
    )


def solution(mesh):
    row = P(None, "fsdp")
    tokens = P(("fsdp", "ctx"), None)
    qkv, qkv_bias = P(None, None, "fsdp", "tp"), P(None, None, "tp", "fsdp")
    fanned, spread = P(None, "tp", "fsdp"), P(None, "fsdp", "tp")
    in_specs = (
        tokens, P(("fsdp", "ctx")), tokens, row, row, row, row, qkv, qkv_bias, fanned, row, spread, fanned, fanned, row
    )
    out_specs = (
        tokens, tokens, row, row, row, row, qkv, qkv_bias, fanned, row, spread, fanned, fanned, row
    )
    return jax.shard_map(body, mesh=mesh, in_specs=in_specs, out_specs=out_specs, check_vma=False)
```

```python
import math

import jax
import jax.numpy as jnp
import numpy as np
from jax import lax
from jax.experimental import pallas as pl
from jax.experimental.pallas import tpu as pltpu
from jax.sharding import PartitionSpec as P

HD = 64
ROT = 16
EPS = 1e-05
BASE = 10000.0
MASKED = -1e30
SCALE = 1.0 / math.sqrt(HD)
INV_ROOT_TWO = 1.0 / math.sqrt(2.0)
INV_ROOT_TWO_PI = 1.0 / math.sqrt(2.0 * math.pi)
MESH = pl.DeviceIdType.MESH
F32 = jnp.float32
BF16 = jnp.bfloat16
GRANT = int(62 * 1024 * 1024)

UP = slice(0, 256)
QK = slice(256, 384)
DN = slice(384, 640)
VO = slice(640, 768)
HALF = (slice(0, 384), slice(384, 768))

M_XW, M_XE = 0, 1
M_POS = 2
M_TOK = 5
M_COT = 8
M_AG1 = 12
M_AGE1 = 18
M_AG2 = 21
M_AGE2 = 27
M_OUT = 30
M_DX = 34
M_RS1 = 38
M_RSE1 = 44
M_RS2 = 47
M_RSE2 = 53
M_FIN = 56
M_FINE = 59
M_ALL = 66


def dot_nn(left, right):
    return lax.dot_general(left, right, (((1,), (0,)), ((), ())), preferred_element_type=F32)


def dot_nt(left, right):
    return lax.dot_general(left, right, (((1,), (1,)), ((), ())), preferred_element_type=F32)


def dot_tn(left, right):
    return lax.dot_general(left, right, (((0,), (0,)), ((), ())), preferred_element_type=F32)


def iota(shape, dim):
    return lax.broadcasted_iota(jnp.int32, shape, dim)


def turn_partner(pair):
    lane = iota(pair.shape, 1) % HD
    return jnp.where(
        lane < ROT // 2, pltpu.roll(pair, pair.shape[1] - ROT // 2, 1), pltpu.roll(pair, ROT // 2, 1)
    )


def kernel(
    tok_in, pos_in, cot_in, gain1_in, shift1_in, gain2_in, shift2_in, qkv_w_in, qkv_b_in, out_w_in, out_b_in, up_w_in,
    up_b_in, down_w_in, down_b_in,
    out_o, gin_o, gg1_o, gb1_o, gg2_o, gb2_o, gqkvw_o, gqkvb_o, goutw_o, gbias_o, gupw_o, gupb_o, gdownw_o,
    gain1, shift1, gain2, shift2, qkv_w, qkv_b, out_w, out_b, up_w, up_b, down_w, down_b,
    W, XS, E, XE, TK, CT, PS, SM,
    NRM, RSQ, NB, MB, NTR, MTR, BTR, COS, SIN, PCOL,
    GC, GVZ, ATZ, PO, RO, SO, XO, PD, RD, SD, XD,
    GS, RA1, RB1, SA, SB, RA2, RB2, EG, RE1, SE, RE2, FB, XR, FE, XF,
    ss, rs, ls,
):
    place = lax.axis_index("fsdp")
    z, y, xh = place // 8, (place // 2) % 4, place % 2
    c = lax.axis_index("ctx")
    t = lax.axis_index("tp")
    ox, oc, ot = 1 - xh, 1 - c, 1 - t

    def dev(xx, cc, tt, zz=z, yy=y):
        return {"fsdp": zz * 8 + yy * 2 + xx, "ctx": cc, "tp": tt}

    def zdev(k):
        return dev(xh, c, t, zz=(z + k) % 4)

    def ydev(k):
        return dev(xh, c, t, yy=(y + k) % 4)

    def send(number, src, dst, where):
        copy = pltpu.make_async_remote_copy(
            src_ref=src, dst_ref=dst, send_sem=ss.at[number], recv_sem=rs.at[number],
            device_id=where, device_id_type=MESH,
        )
        copy.start()
        return copy

    sent = []

    def track(copy):
        sent.append(copy)
        return copy

    barrier = pltpu.get_barrier_semaphore()
    group = [
        dev(xh, oc, t), dev(ox, c, t), dev(ox, c, ot), dev(ox, oc, t), dev(xh, c, ot), dev(xh, oc, ot), dev(ox, oc, ot)
    ]
    peers = group + [zdev(k) for k in (1, 2, 3)] + [ydev(k) for k in (1, 2, 3)]
    for peer in peers:
        pl.semaphore_signal(barrier, inc=1, device_id=peer, device_id_type=MESH)

    loads = []
    for i, (src, dst) in enumerate((
        (qkv_w_in, qkv_w), (out_w_in, out_w), (up_w_in, up_w), (down_w_in, down_w), (gain1_in, gain1),
        (shift1_in, shift1), (gain2_in, gain2), (shift2_in, shift2), (out_b_in, out_b), (down_b_in, down_b),
        (qkv_b_in, qkv_b), (up_b_in, up_b), (pos_in, PS.at[xh, c]), (tok_in, TK.at[xh, c]), (cot_in, CT.at[xh, c]),
    )):
        loads.append(pltpu.make_async_copy(src, dst, ls.at[i]))
        loads[-1].start()
    for load in loads[:4]:
        load.wait()

    def cut(xx):
        lanes = pl.ds(pl.multiple_of(xx * 128, 128), 128)
        q_pair, k_pair, v_pair, o_pair = (
            ref[:, lanes].astype(F32) for ref in (qkv_w.at[0], qkv_w.at[1], qkv_w.at[2], out_w)
        )
        low = iota((16, 128), 1) < HD
        first = c == 0

        def halves(a, b):
            a_low = jnp.where(first, a, pltpu.roll(a, HD, 1))
            b_high = jnp.where(first, pltpu.roll(b, HD, 1), b)
            return jnp.where(low, a_low, b_high).astype(BF16)

        wide = pl.ds(pl.multiple_of((xx * 2 + c) * 256, 256), 256)
        return up_w[:, wide], halves(q_pair, k_pair), down_w[:, wide], halves(v_pair, o_pair)

    for target, xx in ((XS, ox), (W.at[z, y, xh], xh)):
        up_cut, qk_cut, down_cut, vo_cut = cut(xx)
        target[:, UP] = up_cut
        target[:, QK] = qk_cut
        target[:, DN] = down_cut
        target[:, VO] = vo_cut

    for load in loads[4:12]:
        load.wait()
    SM[...] = jnp.zeros((16, 128), F32)
    for row, ref in enumerate((gain1, shift1, gain2, shift2, out_b, down_b)):
        SM[row : row + 1, 0:16] = ref[...].astype(F32)
    for which in range(3):
        SM[8 + 2 * which : 10 + 2 * which, 0:4] = qkv_b[which].astype(F32)
    SM[6:8, 0:16] = up_b[...].astype(F32)
    SM[14:16, 0:16] = up_b[...].astype(F32)

    row16, lane16 = iota((16, 128), 0), iota((16, 128), 1)

    def placed(xx):
        raw = SM[...]
        head = xx * 2 + c

        def column(lane):
            return jnp.sum(jnp.where(lane16 == lane, raw, 0.0), axis=1, keepdims=True)

        spread = pltpu.roll(raw, 16 * (y * 2 + xh), 1)
        low = lane16 < HD
        hit = (lane16 % HD) == 2 * place + row16 % 2
        qkv = jnp.where(low != ((row16 == 10) | (row16 == 11)), column(head), 0.0)
        up_first = jnp.where(low, column(4 * head), column(4 * head + 1))
        up_second = jnp.where(low, column(4 * head + 2), column(4 * head + 3))
        bias = jnp.where(row16 < 8, up_first, jnp.where(row16 < 14, qkv, up_second))
        return jnp.where(row16 < 6, spread, jnp.where(hit, bias, 0.0))

    XE[0] = placed(ox).astype(BF16)
    XE[1] = placed(xh).astype(BF16)

    pl.semaphore_wait(barrier, len(peers))

    xw = track(send(M_XW, XS, W.at[z, y, xh], dev(ox, c, t)))
    xe = track(send(M_XE, XE.at[0], XE.at[2], dev(ox, c, t)))
    across = dev(ox, c, ot)
    core = dev(xh, oc, t)
    tok_across = track(send(M_TOK, tok_in, TK.at[xh, c], across))
    tok_core = track(send(M_TOK + 1, tok_in, TK.at[xh, c], core))
    pos_copies = [
        track(send(M_POS + i, pos_in, PS.at[xh, c], where))
        for i, where in enumerate((core, dev(ox, c, t), dev(ox, oc, t)))
    ]
    cot_across = track(send(M_COT, cot_in, CT.at[xh, c], across))
    cot_core = track(send(M_COT + 1, cot_in, CT.at[xh, c], core))

    xw.wait_recv()
    ag1 = []
    for k in (2, 1, 3):
        here = W.at[z, y, :, :, HALF[0]]
        ag1.append(track(send(M_AG1 + k - 1, here, here, zdev(k))))
        here = W.at[z, y, :, :, HALF[1]]
        ag1.append(track(send(M_AG1 + 3 + k - 1, here, here, ydev(k))))
    xe.wait_recv()
    E[z, y] = (XE[1].astype(F32) + XE[2].astype(F32)).astype(BF16)
    for k in (2, 1, 3):
        ag1.append(track(send(M_AGE1 + k - 1, E.at[z, y], E.at[z, y], zdev(k))))
    tok_across.wait_recv()
    tok_pass = track(send(M_TOK + 2, TK.at[ox, c], TK.at[ox, c], core))
    for copy in ag1:
        copy.wait_recv()
    ag2 = []
    age2 = []
    for k in (2, 1, 3):
        age2.append(track(send(M_AGE2 + k - 1, E.at[:, y], E.at[:, y], ydev(k))))
    for k in (2, 1, 3):
        here = W.at[:, y, :, :, HALF[0]]
        ag2.append(track(send(M_AG2 + k - 1, here, here, ydev(k))))
        here = W.at[z, :, :, :, HALF[1]]
        ag2.append(track(send(M_AG2 + 3 + k - 1, here, here, zdev(k))))
    cot_across.wait_recv()
    cot_pass = track(send(M_COT + 2, CT.at[ox, c], CT.at[ox, c], core))
    for load in loads[12:]:
        load.wait()
    tok_core.wait_recv()
    tok_pass.wait_recv()

    for s in range(2):
        rows = TK[s].reshape(256, 512).astype(F32)
        centered = rows - jnp.mean(rows, axis=1, keepdims=True)
        moment = jnp.mean(centered * centered, axis=1, keepdims=True)
        rsq = lax.rsqrt(moment + EPS)
        NRM[s] = centered * rsq
        RSQ[s] = jnp.broadcast_to(rsq, (256, 128))

    for copy in pos_copies:
        copy.wait_recv()
    row8 = iota((8, 128), 0)
    inverse = jnp.zeros((8, 128), F32)
    for r in range(ROT // 2):
        inverse = jnp.where(row8 == r, float(np.float32(BASE ** (-2.0 * r / ROT))), inverse)
    ones, zeros = jnp.ones((48, 128), F32), jnp.zeros((48, 128), F32)
    for s in range(2):
        for b in range(2):
            places = PS[s, b].astype(F32)
            angle = jnp.broadcast_to(places, (8, 128)) * inverse
            cos, sin = jnp.cos(angle), jnp.sin(angle)
            part = pl.ds(b * 128, 128)
            COS[s, part] = jnp.concatenate([cos, cos, ones, cos, cos, ones], axis=0).T
            SIN[s, part] = jnp.concatenate([-sin, sin, zeros, -sin, sin, zeros], axis=0).T
            PCOL[s, part] = jnp.broadcast_to(places, (128, 128)).T

    cot_core.wait_recv()
    cot_pass.wait_recv()
    bias_grad = jnp.zeros((1, 512), F32)
    for s in range(2):
        grad = CT[s].reshape(256, 512)
        BTR[:, s * 256 : (s + 1) * 256] = grad.T
        bias_grad = bias_grad + jnp.sum(grad.astype(F32), axis=0, keepdims=True)

    for copy in age2:
        copy.wait_recv()
    per_z = []
    for zz in range(4):
        total = E[zz, 0].astype(F32)
        for yy in range(1, 4):
            total = total + E[zz, yy].astype(F32)
        per_z.append(total)
    vectors = jnp.concatenate(per_z, axis=1)
    all_z = per_z[0] + per_z[1] + per_z[2] + per_z[3]
    g1, b1, g2, b2 = (vectors[r : r + 1] for r in range(4))
    b_branch = vectors[4:5] + vectors[5:6]
    b_up = jnp.concatenate([all_z[6:7] + all_z[7:8], all_z[14:15] + all_z[15:16]], axis=1)
    b_qk = all_z[8:9] + all_z[9:10] + all_z[10:11] + all_z[11:12]
    b_v = (all_z[12:13] + all_z[13:14])[:, :HD]

    for s in range(2):
        n = NRM[s]
        normed = (n * g1 + b1).astype(BF16)
        mlp_input = (n * g2 + b2).astype(BF16)
        NB[s] = normed
        MB[s] = mlp_input
        NTR[:, s * 256 : (s + 1) * 256] = normed.T
        MTR[:, s * 256 : (s + 1) * 256] = mlp_input.T

    for copy in ag2:
        copy.wait_recv()

    gb_up = jnp.zeros((1, 256), F32)
    gb_qk = jnp.zeros((1, 128), F32)
    gb_v = jnp.zeros((1, HD), F32)
    for s in range(2):
        part = slice(s * 256, (s + 1) * 256)
        normed, mlp_input, branch_grad = NB[s], MB[s], CT[s].reshape(256, 512)
        w_up = W[:, :, :, :, UP].reshape(512, 256)
        w_down = W[:, :, :, :, DN].reshape(512, 256)
        w_qk = W[:, :, :, :, QK].reshape(512, 128)
        w_vo = W[:, :, :, :, VO].reshape(512, 128)
        pre_act = dot_nn(mlp_input, w_up) + b_up
        phi = 0.5 * (1.0 + lax.erf(pre_act * INV_ROOT_TWO))
        density = jnp.exp(-0.5 * pre_act * pre_act) * INV_ROOT_TWO_PI
        activated = (pre_act * phi).astype(BF16)
        grad_pre = (dot_nn(branch_grad, w_down) * (phi + pre_act * density)).astype(BF16)
        gb_up = gb_up + jnp.sum(grad_pre.astype(F32), axis=0, keepdims=True)
        GC[part, UP] = grad_pre
        GC[part, DN] = activated

        cos, sin = COS[s], SIN[s]
        qk = dot_nn(normed, w_qk) + b_qk
        qk = (qk * cos + turn_partner(qk) * sin).astype(BF16)
        query, key = qk[:, :HD], qk[:, HD:]
        value = (dot_nn(normed, w_vo)[:, :HD] + b_v).astype(BF16)
        grad_att = dot_nn(branch_grad, w_vo)[:, HD:].astype(BF16)
        row, col = iota((256, 256), 0), iota((256, 256), 1)
        start = row.astype(F32) - jnp.concatenate([PCOL[s], PCOL[s]], axis=1)
        visible = (col <= row) & (col.astype(F32) >= start)
        scores = jnp.where(visible, dot_nt(query, key) * SCALE, MASKED)
        exps = jnp.exp(scores - jnp.max(scores, axis=1, keepdims=True))
        probs = exps / jnp.sum(exps, axis=1, keepdims=True)
        probs_low = probs.astype(BF16)
        attended = dot_nn(probs_low, value).astype(BF16)
        grad_probs = dot_nt(grad_att, value)
        row_dot = jnp.sum(probs * grad_probs, axis=1, keepdims=True)
        grad_scores = (probs * (grad_probs - row_dot)).astype(BF16)
        grad_query = dot_nn(grad_scores, key) * SCALE
        grad_key = dot_tn(grad_scores, query) * SCALE
        grad_value = dot_tn(probs_low, grad_att).astype(BF16)
        grad_qk = jnp.concatenate([grad_query, grad_key], axis=1)
        grad_qk = (grad_qk * cos - turn_partner(grad_qk) * sin).astype(BF16)
        gb_qk = gb_qk + jnp.sum(grad_qk.astype(F32), axis=0, keepdims=True)
        gb_v = gb_v + jnp.sum(grad_value.astype(F32), axis=0, keepdims=True)
        blank = jnp.zeros((256, HD), BF16)
        GC[part, QK] = grad_qk
        GVZ[part] = jnp.concatenate([grad_value, blank], axis=1)
        ATZ[part] = jnp.concatenate([blank, attended], axis=1)
        branch = dot_nt(activated, w_down) + dot_nt(ATZ[part], w_vo)
        PO[s] = branch.astype(BF16).reshape(2, 128, 512)

    out_core = track(send(M_OUT, PO.at[:, oc], RO, core))

    GS[:, :, :, UP] = dot_nn(MTR[...], GC[:, UP]).astype(BF16).reshape(4, 4, 32, 256)
    GS[:, :, :, QK] = dot_nn(NTR[...], GC[:, QK]).astype(BF16).reshape(4, 4, 32, 128)
    rs1 = []
    for k in (2, 1, 3):
        rs1.append(track(send(M_RS1 + k - 1, GS.at[:, (y + k) % 4, :, HALF[0]], RA1.at[k - 1], ydev(k))))
    GS[:, :, :, DN] = dot_nn(BTR[...], GC[:, DN]).astype(BF16).reshape(4, 4, 32, 256)
    grad_vo = dot_nn(NTR[...], GVZ[...]) + dot_nn(BTR[...], ATZ[...])
    GS[:, :, :, VO] = grad_vo.astype(BF16).reshape(4, 4, 32, 128)
    for k in (2, 1, 3):
        rs1.append(track(send(M_RS1 + 3 + k - 1, GS.at[(z + k) % 4, :, :, HALF[1]], RB1.at[k - 1], zdev(k))))

    out_core.wait_recv()
    SO[...] = (PO[:, c].astype(F32) + RO[...].astype(F32)).astype(BF16)
    out_copies = [
        track(send(M_OUT + 1, SO.at[ox], XO.at[0], dev(ox, c, ot))),
        track(send(M_OUT + 2, SO.at[ox], XO.at[1], dev(ox, c, t))),
        track(send(M_OUT + 3, SO.at[xh], XO.at[2], dev(xh, c, ot))),
    ]

    totals = [jnp.zeros((1, 512), F32) for _ in range(4)]
    for s in range(2):
        part = slice(s * 256, (s + 1) * 256)
        w_up = W[:, :, :, :, UP].reshape(512, 256)
        w_qk = W[:, :, :, :, QK].reshape(512, 128)
        w_vo = W[:, :, :, :, VO].reshape(512, 128)
        n = NRM[s]
        grad_mlp = dot_nt(GC[part, UP], w_up)
        grad_normed = dot_nt(GC[part, QK], w_qk) + dot_nt(GVZ[part], w_vo)
        for i, term in enumerate((grad_normed * n, grad_normed, grad_mlp * n, grad_mlp)):
            totals[i] = totals[i] + jnp.sum(term, axis=0, keepdims=True)
        joined = grad_normed * g1 + grad_mlp * g2
        mean_one = jnp.mean(joined, axis=1, keepdims=True)
        mean_two = jnp.mean(joined * n, axis=1, keepdims=True)
        term = RSQ[s][:, :1] * (joined - mean_one - n * mean_two)
        PD[s] = term.astype(BF16).reshape(2, 128, 512)
    dx_core = track(send(M_DX, PD.at[:, oc], RD, core))

    up_rows = jnp.concatenate([gb_up[:, :128], gb_up[:, 128:]], axis=0)
    v_row = jnp.concatenate([gb_v, jnp.zeros((1, 128 - HD), F32)], axis=1)
    for zz in range(4):
        lanes = slice(zz * 128, (zz + 1) * 128)
        pieces = [total[:, lanes] for total in totals] + [bias_grad[:, lanes], gb_qk, v_row, up_rows]
        EG[zz] = jnp.concatenate(pieces + [jnp.zeros((7, 128), F32)], axis=0).astype(BF16)
    rse1 = [track(send(M_RSE1 + k - 1, EG, RE1.at[k - 1], ydev(k))) for k in (2, 1, 3)]

    dx_core.wait_recv()
    SD[...] = (PD[:, c].astype(F32) + RD[...].astype(F32)).astype(BF16)
    dx_copies = [
        track(send(M_DX + 1, SD.at[ox], XD.at[0], dev(ox, c, ot))),
        track(send(M_DX + 2, SD.at[ox], XD.at[1], dev(ox, c, t))),
        track(send(M_DX + 3, SD.at[xh], XD.at[2], dev(xh, c, ot))),
    ]

    for copy in rs1:
        copy.wait_recv()

    def summed(own, received):
        total = own.astype(F32)
        for k in range(3):
            total = total + received[k].astype(F32)
        return total

    SA[...] = summed(GS[:, y, :, HALF[0]], RA1).astype(BF16)
    rs2 = [track(send(M_RS2 + k - 1, SA.at[(z + k) % 4], RA2.at[k - 1], zdev(k))) for k in (2, 1, 3)]
    SB[...] = summed(GS[z, :, :, HALF[1]], RB1).astype(BF16)
    rs2 += [track(send(M_RS2 + 3 + k - 1, SB.at[(y + k) % 4], RB2.at[k - 1], ydev(k))) for k in (2, 1, 3)]
    for copy in rse1:
        copy.wait_recv()
    SE[...] = summed(EG[...], RE1).astype(BF16)
    rse2 = [track(send(M_RSE2 + k - 1, SE.at[(z + k) % 4], RE2.at[k - 1], zdev(k))) for k in (2, 1, 3)]

    def over_chips(own, received):
        return (own.astype(F32) + received[2].astype(F32)) + (received[0].astype(F32) + received[1].astype(F32))

    for copy in out_copies:
        copy.wait_recv()
    out_o[...] = (TK[xh, c].astype(F32) + (over_chips(SO[xh], XO) + b_branch)).astype(BF16)
    for copy in dx_copies:
        copy.wait_recv()
    gin_o[...] = CT[xh, c].astype(F32) + over_chips(SD[xh], XD)

    for copy in rs2:
        copy.wait_recv()
    FB[:, :, HALF[0]] = summed(SA[z], RA2).astype(BF16).reshape(2, 16, 384)
    FB[:, :, HALF[1]] = summed(SB[y], RB2).astype(BF16).reshape(2, 16, 384)
    fin = [
        track(send(M_FIN, FB.at[ox], XR.at[xh, c], dev(ox, c, t))),
        track(send(M_FIN + 1, FB.at[ox], XR.at[xh, c], dev(ox, oc, t))),
        track(send(M_FIN + 2, FB.at[xh], XR.at[xh, c], dev(xh, oc, t))),
    ]
    XR[xh, c] = FB[xh]
    for copy in rse2:
        copy.wait_recv()
    FE[...] = summed(SE[z], RE2).astype(BF16)
    fine = [track(send(M_FINE + i, FE, XF.at[t, xh, c], where)) for i, where in enumerate(group)]
    XF[t, xh, c] = FE[...]

    for copy in fin:
        copy.wait_recv()
    for xx in range(2):
        both = [XR[xx, 0].astype(F32), XR[xx, 1].astype(F32)]
        lanes = slice(xx * 128, (xx + 1) * 128)
        low = iota((16, 128), 1) < HD

        def join(first, second):
            return jnp.where(low, first, pltpu.roll(second, HD, 1)), jnp.where(low, pltpu.roll(first, HD, 1), second)

        q_new, k_new = join(both[0][:, QK], both[1][:, QK])
        v_new, o_new = join(both[0][:, VO], both[1][:, VO])
        gqkvw_o[0, :, lanes] = q_new
        gqkvw_o[1, :, lanes] = k_new
        gqkvw_o[2, :, lanes] = v_new
        goutw_o[:, lanes] = o_new
        for cc in range(2):
            wide = slice((xx * 2 + cc) * 256, (xx * 2 + cc + 1) * 256)
            gupw_o[:, wide] = both[cc][:, UP]
            gdownw_o[:, wide] = both[cc][:, DN]

    for copy in fine:
        copy.wait_recv()
    tiles = [[[XF[tt, xx, cc].astype(F32) for cc in range(2)] for xx in range(2)] for tt in range(2)]
    whole = jnp.zeros((16, 128), F32)
    for tt in range(2):
        for xx in range(2):
            for cc in range(2):
                whole = whole + tiles[tt][xx][cc]
    whole = jnp.where(row16 == 4, tiles[0][0][0], whole)
    whole = pltpu.roll(whole, (128 - 16 * (y * 2 + xh)) % 128, 1)
    for row, ref in enumerate((gg1_o, gb1_o, gg2_o, gb2_o, gbias_o)):
        ref[...] = whole[row : row + 1, 0:16]
    j4, h4 = iota((2, 4), 0), iota((2, 4), 1)
    j16, h16 = iota((2, 16), 0), iota((2, 16), 1)
    new_qkv = [jnp.zeros((2, 4), F32) for _ in range(3)]
    new_up = jnp.zeros((2, 16), F32)
    for xx in range(2):
        for cc in range(2):
            head = xx * 2 + cc
            tile = jnp.where(t == 0, tiles[0][xx][cc], tiles[1][xx][cc])
            for j in range(2):
                low_col = jnp.sum(jnp.where(lane16 == 2 * place + j, tile, 0.0), axis=1, keepdims=True)
                high_col = jnp.sum(jnp.where(lane16 == HD + 2 * place + j, tile, 0.0), axis=1, keepdims=True)
                spot = (j4 == j) & (h4 == head)
                for which, item in enumerate((low_col[5:6], high_col[5:6], low_col[6:7])):
                    new_qkv[which] = jnp.where(spot, item, new_qkv[which])
                for u, item in enumerate((low_col[7:8], high_col[7:8], low_col[8:9], high_col[8:9])):
                    new_up = jnp.where((j16 == j) & (h16 == head * 4 + u), item, new_up)
    for which in range(3):
        gqkvb_o[which] = new_qkv[which]
    gupb_o[...] = new_up
    for copy in sent:
        copy.wait_send()


def place_results(*refs):
    ins, outs, sems = refs[:13], refs[13:27], refs[27]
    copies = [pltpu.make_async_copy(src, dst, sems.at[i]) for i, (src, dst) in enumerate(zip(ins + (ins[9],), outs))]
    for copy in copies:
        copy.start()
    for copy in copies:
        copy.wait()


def body(
    tokens, positions, cotangent, ln1_gain, ln1_bias, ln2_gain, ln2_bias, qkv_weight, qkv_bias, out_weight, out_bias,
    up_weight, up_bias, down_weight, down_bias,
):
    shape = jax.ShapeDtypeStruct
    row = shape((1, 16), F32)
    operands = (
        tokens, positions.reshape(1, 128), cotangent, ln1_gain, ln1_bias, ln2_gain, ln2_bias, qkv_weight[0],
        qkv_bias[0].transpose(0, 2, 1), out_weight[0].T, out_bias, up_weight[0], up_bias[0].T, down_weight[0].T,
        down_bias,
    )
    outs = (
        shape((128, 512), BF16), shape((128, 512), F32), row, row, row, row, shape((3, 16, 256), F32),
        shape((3, 2, 4), F32), shape((16, 256), F32), row, shape((16, 1024), F32), shape((2, 16), F32),
        shape((16, 1024), F32),
    )
    scratch = [
        *[((1, 16), BF16)] * 4, ((3, 16, 256), BF16), ((3, 2, 4), BF16), ((16, 256), BF16), ((1, 16), BF16),
        ((16, 1024), BF16), ((2, 16), BF16), ((16, 1024), BF16), ((1, 16), BF16),
        ((4, 4, 2, 16, 768), BF16), ((16, 768), BF16), ((4, 4, 16, 128), BF16), ((3, 16, 128), BF16),
        ((2, 2, 128, 512), BF16), ((2, 2, 128, 512), BF16), ((2, 2, 1, 128), jnp.int32), ((16, 128), F32),
        ((2, 256, 512), F32), ((2, 256, 128), F32), ((2, 256, 512), BF16), ((2, 256, 512), BF16),
        ((512, 512), BF16), ((512, 512), BF16), ((512, 512), BF16),
        ((2, 256, 128), F32), ((2, 256, 128), F32), ((2, 256, 128), F32),
        ((512, 768), BF16), ((512, 128), BF16), ((512, 128), BF16),
        ((2, 2, 128, 512), BF16), ((2, 128, 512), BF16), ((2, 128, 512), BF16), ((3, 128, 512), BF16),
        ((2, 2, 128, 512), BF16), ((2, 128, 512), BF16), ((2, 128, 512), BF16), ((3, 128, 512), BF16),
        ((4, 4, 32, 768), BF16), ((3, 4, 32, 384), BF16), ((3, 4, 32, 384), BF16), ((4, 32, 384), BF16),
        ((4, 32, 384), BF16), ((3, 32, 384), BF16), ((3, 32, 384), BF16),
        ((4, 16, 128), BF16), ((3, 4, 16, 128), BF16), ((4, 16, 128), BF16), ((3, 16, 128), BF16),
        ((2, 16, 768), BF16), ((2, 2, 16, 768), BF16), ((16, 128), BF16), ((2, 2, 2, 16, 128), BF16),
    ]
    results = pl.pallas_call(
        kernel,
        out_shape=outs,
        in_specs=[pl.BlockSpec(memory_space=pl.ANY)] * len(operands),
        out_specs=[pl.BlockSpec(memory_space=pltpu.VMEM)] * len(outs),
        scratch_shapes=[pltpu.VMEM(*item) for item in scratch]
        + [pltpu.SemaphoreType.DMA((M_ALL,)), pltpu.SemaphoreType.DMA((M_ALL,)), pltpu.SemaphoreType.DMA((15,))],
        compiler_params=pltpu.CompilerParams(
            collective_id=0, has_side_effects=True, vmem_limit_bytes=GRANT
        ),
    )(*operands)
    results = pl.pallas_call(
        place_results,
        out_shape=outs + (row,),
        in_specs=[pl.BlockSpec(memory_space=pltpu.VMEM)] * 13,
        out_specs=[pl.BlockSpec(memory_space=pl.ANY)] * 14,
        scratch_shapes=[pltpu.SemaphoreType.DMA((14,))],
        compiler_params=pltpu.CompilerParams(vmem_limit_bytes=GRANT),
    )(*results)
    (
        output, grad_input, grad_gain1, grad_shift1, grad_gain2, grad_shift2, grad_qkv, grad_qkv_bias, grad_out,
        grad_bias, grad_up, grad_up_bias, grad_down, grad_bias_again,
    ) = results
    return (
        output, grad_input, grad_gain1, grad_shift1, grad_gain2, grad_shift2, grad_qkv[None],
        grad_qkv_bias.transpose(0, 2, 1)[None], grad_out.T[None], grad_bias, grad_up[None], grad_up_bias.T[None],
        grad_down.T[None], grad_bias_again,
    )


def solution(mesh):
    row = P(None, "fsdp")
    tokens = P(("fsdp", "ctx"), None)
    qkv, qkv_bias = P(None, None, "fsdp", "tp"), P(None, None, "tp", "fsdp")
    fanned, spread = P(None, "tp", "fsdp"), P(None, "fsdp", "tp")
    in_specs = (
        tokens, P(("fsdp", "ctx")), tokens, row, row, row, row, qkv, qkv_bias, fanned, row, spread, fanned, fanned, row
    )
    out_specs = (
        tokens, tokens, row, row, row, row, qkv, qkv_bias, fanned, row, spread, fanned, fanned, row
    )
    return jax.shard_map(body, mesh=mesh, in_specs=in_specs, out_specs=out_specs, check_vma=False)
```

```python
import math

import jax
import jax.numpy as jnp
import numpy as np
from jax import lax
from jax.experimental import pallas as pl
from jax.experimental.pallas import tpu as pltpu
from jax.sharding import PartitionSpec as P

HD = 64
ROT = 16
EPS = 1e-05
BASE = 10000.0
MASKED = -1e30
SCALE = 1.0 / math.sqrt(HD)
INV_ROOT_TWO = 1.0 / math.sqrt(2.0)
INV_ROOT_TWO_PI = 1.0 / math.sqrt(2.0 * math.pi)
MESH = pl.DeviceIdType.MESH
F32 = jnp.float32
BF16 = jnp.bfloat16
GRANT = int(62 * 1024 * 1024)

UP = slice(0, 256)
QK = slice(256, 384)
DN = slice(384, 640)
VO = slice(640, 768)
HALF = (slice(0, 384), slice(384, 768))

PARTS = ((0, UP), (1, DN), (0, QK), (1, VO))

M_XW, M_XE = 0, 1
M_POS = 2
M_TOK = 5
M_COT = 8
M_AG1 = 12
M_AGE1 = 18
M_AG2 = 21
M_AGE2 = 33
M_OUT = 36
M_DX = 40
M_RS1 = 46
M_RSE1 = 58
M_RS2 = 61
M_RSE2 = 73
M_FIN = 76
M_FINE = 79
M_ALL = 86


def dot_nn(left, right):
    return lax.dot_general(left, right, (((1,), (0,)), ((), ())), preferred_element_type=F32)


def dot_nt(left, right):
    return lax.dot_general(left, right, (((1,), (1,)), ((), ())), preferred_element_type=F32)


def dot_tn(left, right):
    return lax.dot_general(left, right, (((0,), (0,)), ((), ())), preferred_element_type=F32)


def iota(shape, dim):
    return lax.broadcasted_iota(jnp.int32, shape, dim)


def turn_partner(pair):
    lane = iota(pair.shape, 1) % HD
    return jnp.where(
        lane < ROT // 2, pltpu.roll(pair, pair.shape[1] - ROT // 2, 1), pltpu.roll(pair, ROT // 2, 1)
    )


def kernel(
    tok_in, pos_in, cot_in, gain1_in, shift1_in, gain2_in, shift2_in, qkv_w_in, qkv_b_in, out_w_in, out_b_in, up_w_in,
    up_b_in, down_w_in, down_b_in,
    out_o, gin_o, gg1_o, gb1_o, gg2_o, gb2_o, gqkvw_o, gqkvb_o, goutw_o, gbias_o, gupw_o, gupb_o, gdownw_o,
    gain1, shift1, gain2, shift2, qkv_w, qkv_b, out_w, out_b, up_w, up_b, down_w, down_b,
    W, XS, E, XE, TK, CT, PS, SM,
    NRM, RSQ, NB, MB, NTR, MTR, BTR, COS, SIN, PCOL,
    GC, GVZ, ATZ, PO, RO, SO, XO, TO, PD, RD, SD, XD, TD,
    GS, RA1, RB1, SA, SB, RA2, RB2, EG, RE1, SE, RE2, FB, XR, FE, XF,
    ss, rs, ls,
):
    place = lax.axis_index("fsdp")
    z, y, xh = place // 8, (place // 2) % 4, place % 2
    c = lax.axis_index("ctx")
    t = lax.axis_index("tp")
    ox, oc, ot = 1 - xh, 1 - c, 1 - t

    def dev(xx, cc, tt, zz=z, yy=y):
        return {"fsdp": zz * 8 + yy * 2 + xx, "ctx": cc, "tp": tt}

    def zdev(k):
        return dev(xh, c, t, zz=(z + k) % 4)

    def ydev(k):
        return dev(xh, c, t, yy=(y + k) % 4)

    def send(number, src, dst, where):
        copy = pltpu.make_async_remote_copy(
            src_ref=src, dst_ref=dst, send_sem=ss.at[number], recv_sem=rs.at[number],
            device_id=where, device_id_type=MESH,
        )
        copy.start()
        return copy

    sent = []

    def track(copy):
        sent.append(copy)
        return copy

    barrier = pltpu.get_barrier_semaphore()
    group = [
        dev(xh, oc, t), dev(ox, c, t), dev(ox, c, ot), dev(ox, oc, t), dev(xh, c, ot), dev(xh, oc, ot), dev(ox, oc, ot)
    ]
    peers = group + [zdev(k) for k in (1, 2, 3)] + [ydev(k) for k in (1, 2, 3)]
    for peer in peers:
        pl.semaphore_signal(barrier, inc=1, device_id=peer, device_id_type=MESH)

    loads = []
    for i, (src, dst) in enumerate((
        (qkv_w_in, qkv_w), (out_w_in, out_w), (up_w_in, up_w), (down_w_in, down_w), (gain1_in, gain1),
        (shift1_in, shift1), (gain2_in, gain2), (shift2_in, shift2), (out_b_in, out_b), (down_b_in, down_b),
        (qkv_b_in, qkv_b), (up_b_in, up_b), (pos_in, PS.at[xh, c]), (tok_in, TK.at[xh, c]), (cot_in, CT.at[xh, c]),
    )):
        loads.append(pltpu.make_async_copy(src, dst, ls.at[i]))
        loads[-1].start()
    for load in loads[:4]:
        load.wait()

    def cut(xx):
        lanes = pl.ds(pl.multiple_of(xx * 128, 128), 128)
        q_pair, k_pair, v_pair, o_pair = (
            ref[:, lanes].astype(F32) for ref in (qkv_w.at[0], qkv_w.at[1], qkv_w.at[2], out_w)
        )
        low = iota((16, 128), 1) < HD
        first = c == 0

        def halves(a, b):
            a_low = jnp.where(first, a, pltpu.roll(a, HD, 1))
            b_high = jnp.where(first, pltpu.roll(b, HD, 1), b)
            return jnp.where(low, a_low, b_high).astype(BF16)

        wide = pl.ds(pl.multiple_of((xx * 2 + c) * 256, 256), 256)
        return up_w[:, wide], halves(q_pair, k_pair), down_w[:, wide], halves(v_pair, o_pair)

    for target, xx in ((XS, ox), (W.at[z, y, xh], xh)):
        up_cut, qk_cut, down_cut, vo_cut = cut(xx)
        target[:, UP] = up_cut
        target[:, QK] = qk_cut
        target[:, DN] = down_cut
        target[:, VO] = vo_cut

    for load in loads[4:12]:
        load.wait()
    SM[...] = jnp.zeros((16, 128), F32)
    for row, ref in enumerate((gain1, shift1, gain2, shift2, out_b, down_b)):
        SM[row : row + 1, 0:16] = ref[...].astype(F32)
    for which in range(3):
        SM[8 + 2 * which : 10 + 2 * which, 0:4] = qkv_b[which].astype(F32)
    SM[6:8, 0:16] = up_b[...].astype(F32)
    SM[14:16, 0:16] = up_b[...].astype(F32)

    row16, lane16 = iota((16, 128), 0), iota((16, 128), 1)

    def placed(xx):
        raw = SM[...]
        head = xx * 2 + c

        def column(lane):
            return jnp.sum(jnp.where(lane16 == lane, raw, 0.0), axis=1, keepdims=True)

        spread = pltpu.roll(raw, 16 * (y * 2 + xh), 1)
        low = lane16 < HD
        hit = (lane16 % HD) == 2 * place + row16 % 2
        qkv = jnp.where(low != ((row16 == 10) | (row16 == 11)), column(head), 0.0)
        up_first = jnp.where(low, column(4 * head), column(4 * head + 1))
        up_second = jnp.where(low, column(4 * head + 2), column(4 * head + 3))
        bias = jnp.where(row16 < 8, up_first, jnp.where(row16 < 14, qkv, up_second))
        return jnp.where(row16 < 6, spread, jnp.where(hit, bias, 0.0))

    XE[0] = placed(ox).astype(BF16)
    XE[1] = placed(xh).astype(BF16)

    pl.semaphore_wait(barrier, len(peers))

    xw = track(send(M_XW, XS, W.at[z, y, xh], dev(ox, c, t)))
    xe = track(send(M_XE, XE.at[0], XE.at[2], dev(ox, c, t)))
    across = dev(ox, c, ot)
    core = dev(xh, oc, t)
    tok_across = track(send(M_TOK, tok_in, TK.at[xh, c], across))
    tok_core = track(send(M_TOK + 1, tok_in, TK.at[xh, c], core))
    pos_copies = [
        track(send(M_POS + i, pos_in, PS.at[xh, c], where))
        for i, where in enumerate((core, dev(ox, c, t), dev(ox, oc, t)))
    ]
    cot_across = track(send(M_COT, cot_in, CT.at[xh, c], across))
    cot_core = track(send(M_COT + 1, cot_in, CT.at[xh, c], core))

    xw.wait_recv()
    ag1 = []
    for k in (2, 1, 3):
        here = W.at[z, y, :, :, HALF[0]]
        ag1.append(track(send(M_AG1 + k - 1, here, here, zdev(k))))
        here = W.at[z, y, :, :, HALF[1]]
        ag1.append(track(send(M_AG1 + 3 + k - 1, here, here, ydev(k))))
    xe.wait_recv()
    E[z, y] = (XE[1].astype(F32) + XE[2].astype(F32)).astype(BF16)
    for k in (2, 1, 3):
        ag1.append(track(send(M_AGE1 + k - 1, E.at[z, y], E.at[z, y], zdev(k))))
    tok_across.wait_recv()
    tok_pass = track(send(M_TOK + 2, TK.at[ox, c], TK.at[ox, c], core))
    for copy in ag1:
        copy.wait_recv()
    ag2 = []
    age2 = []
    for k in (2, 1, 3):
        age2.append(track(send(M_AGE2 + k - 1, E.at[:, y], E.at[:, y], ydev(k))))
    for part, (route, columns) in enumerate(PARTS):
        for k in (2, 1, 3):
            here = (W.at[:, y, :, :, columns], W.at[z, :, :, :, columns])[route]
            number = M_AG2 + 3 * part + k - 1
            ag2.append(track(send(number, here, here, (ydev, zdev)[route](k))))
    cot_across.wait_recv()
    cot_pass = track(send(M_COT + 2, CT.at[ox, c], CT.at[ox, c], core))
    for load in loads[12:]:
        load.wait()
    tok_core.wait_recv()
    tok_pass.wait_recv()

    for s in range(2):
        rows = TK[s].reshape(256, 512).astype(F32)
        centered = rows - jnp.mean(rows, axis=1, keepdims=True)
        moment = jnp.mean(centered * centered, axis=1, keepdims=True)
        rsq = lax.rsqrt(moment + EPS)
        NRM[s] = centered * rsq
        RSQ[s] = jnp.broadcast_to(rsq, (256, 128))

    for copy in pos_copies:
        copy.wait_recv()
    row8 = iota((8, 128), 0)
    inverse = jnp.zeros((8, 128), F32)
    for r in range(ROT // 2):
        inverse = jnp.where(row8 == r, float(np.float32(BASE ** (-2.0 * r / ROT))), inverse)
    ones, zeros = jnp.ones((48, 128), F32), jnp.zeros((48, 128), F32)
    for s in range(2):
        for b in range(2):
            places = PS[s, b].astype(F32)
            angle = jnp.broadcast_to(places, (8, 128)) * inverse
            cos, sin = jnp.cos(angle), jnp.sin(angle)
            part = pl.ds(b * 128, 128)
            COS[s, part] = jnp.concatenate([cos, cos, ones, cos, cos, ones], axis=0).T
            SIN[s, part] = jnp.concatenate([-sin, sin, zeros, -sin, sin, zeros], axis=0).T
            PCOL[s, part] = jnp.broadcast_to(places, (128, 128)).T

    cot_core.wait_recv()
    cot_pass.wait_recv()
    bias_grad = jnp.zeros((1, 512), F32)
    for s in range(2):
        grad = CT[s].reshape(256, 512)
        BTR[:, s * 256 : (s + 1) * 256] = grad.T
        bias_grad = bias_grad + jnp.sum(grad.astype(F32), axis=0, keepdims=True)

    for copy in age2:
        copy.wait_recv()
    per_z = []
    for zz in range(4):
        total = E[zz, 0].astype(F32)
        for yy in range(1, 4):
            total = total + E[zz, yy].astype(F32)
        per_z.append(total)
    vectors = jnp.concatenate(per_z, axis=1)
    all_z = per_z[0] + per_z[1] + per_z[2] + per_z[3]
    g1, b1, g2, b2 = (vectors[r : r + 1] for r in range(4))
    b_branch = vectors[4:5] + vectors[5:6]
    b_up = jnp.concatenate([all_z[6:7] + all_z[7:8], all_z[14:15] + all_z[15:16]], axis=1)
    b_qk = all_z[8:9] + all_z[9:10] + all_z[10:11] + all_z[11:12]
    b_v = (all_z[12:13] + all_z[13:14])[:, :HD]

    for s in range(2):
        n = NRM[s]
        normed = (n * g1 + b1).astype(BF16)
        mlp_input = (n * g2 + b2).astype(BF16)
        NB[s] = normed
        MB[s] = mlp_input
        NTR[:, s * 256 : (s + 1) * 256] = normed.T
        MTR[:, s * 256 : (s + 1) * 256] = mlp_input.T

    for copy in ag2[:6]:
        copy.wait_recv()

    def columns_of(columns, width):
        return W[:, :, :, :, columns].reshape(512, width)

    gb_up = jnp.zeros((1, 256), F32)
    for s in range(2):
        part = slice(s * 256, (s + 1) * 256)
        branch_grad = CT[s].reshape(256, 512)
        pre_act = dot_nn(MB[s], columns_of(UP, 256)) + b_up
        phi = 0.5 * (1.0 + lax.erf(pre_act * INV_ROOT_TWO))
        density = jnp.exp(-0.5 * pre_act * pre_act) * INV_ROOT_TWO_PI
        grad_hidden = dot_nn(branch_grad, columns_of(DN, 256))
        grad_pre = (grad_hidden * (phi + pre_act * density)).astype(BF16)
        gb_up = gb_up + jnp.sum(grad_pre.astype(F32), axis=0, keepdims=True)
        GC[part, UP] = grad_pre
        GC[part, DN] = (pre_act * phi).astype(BF16)

    rs1 = []

    def first_ring(part):
        route, columns = PARTS[part]
        for k in (2, 1, 3):
            src = (GS.at[:, (y + k) % 4, :, columns], GS.at[(z + k) % 4, :, :, columns])[route]
            dst = (RA1, RB1)[route].at[k - 1, :, :, local(columns)]
            rs1.append(track(send(M_RS1 + 3 * part + k - 1, src, dst, (ydev, zdev)[route](k))))

    def local(columns):
        return slice(columns.start % 384, (columns.stop - 1) % 384 + 1)

    GS[:, :, :, UP] = dot_nn(MTR[...], GC[:, UP]).astype(BF16).reshape(4, 4, 32, 256)
    first_ring(0)
    GS[:, :, :, DN] = dot_nn(BTR[...], GC[:, DN]).astype(BF16).reshape(4, 4, 32, 256)
    first_ring(1)

    for copy in ag2[6:]:
        copy.wait_recv()
    gb_qk = jnp.zeros((1, 128), F32)
    gb_v = jnp.zeros((1, HD), F32)
    for s in range(2):
        part = slice(s * 256, (s + 1) * 256)
        normed, branch_grad = NB[s], CT[s].reshape(256, 512)
        w_vo = columns_of(VO, 128)
        cos, sin = COS[s], SIN[s]
        qk = dot_nn(normed, columns_of(QK, 128)) + b_qk
        qk = (qk * cos + turn_partner(qk) * sin).astype(BF16)
        query, key = qk[:, :HD], qk[:, HD:]
        value = (dot_nn(normed, w_vo)[:, :HD] + b_v).astype(BF16)
        grad_att = dot_nn(branch_grad, w_vo)[:, HD:].astype(BF16)
        row, col = iota((256, 256), 0), iota((256, 256), 1)
        start = row.astype(F32) - jnp.concatenate([PCOL[s], PCOL[s]], axis=1)
        visible = (col <= row) & (col.astype(F32) >= start)
        scores = jnp.where(visible, dot_nt(query, key) * SCALE, MASKED)
        exps = jnp.exp(scores - jnp.max(scores, axis=1, keepdims=True))
        probs = exps / jnp.sum(exps, axis=1, keepdims=True)
        probs_low = probs.astype(BF16)
        attended = dot_nn(probs_low, value).astype(BF16)
        grad_probs = dot_nt(grad_att, value)
        row_dot = jnp.sum(probs * grad_probs, axis=1, keepdims=True)
        grad_scores = (probs * (grad_probs - row_dot)).astype(BF16)
        grad_query = dot_nn(grad_scores, key) * SCALE
        grad_key = dot_tn(grad_scores, query) * SCALE
        grad_value = dot_tn(probs_low, grad_att).astype(BF16)
        grad_qk = jnp.concatenate([grad_query, grad_key], axis=1)
        grad_qk = (grad_qk * cos - turn_partner(grad_qk) * sin).astype(BF16)
        gb_qk = gb_qk + jnp.sum(grad_qk.astype(F32), axis=0, keepdims=True)
        gb_v = gb_v + jnp.sum(grad_value.astype(F32), axis=0, keepdims=True)
        blank = jnp.zeros((256, HD), BF16)
        GC[part, QK] = grad_qk
        GVZ[part] = jnp.concatenate([grad_value, blank], axis=1)
        ATZ[part] = jnp.concatenate([blank, attended], axis=1)

    def rows_of(s):
        return pl.ds(pl.multiple_of(s * 256, 256), 256)

    out_core = []
    for i, s in enumerate((ox, xh)):
        part = rows_of(s)
        branch = dot_nt(GC[part, DN], columns_of(DN, 256)) + dot_nt(ATZ[part], columns_of(VO, 128))
        PO[s] = branch.astype(BF16).reshape(2, 128, 512)
        out_core.append(track(send(M_OUT + i, PO.at[s, oc], RO.at[s], core)))

    GS[:, :, :, QK] = dot_nn(NTR[...], GC[:, QK]).astype(BF16).reshape(4, 4, 32, 128)
    first_ring(2)
    grad_vo = dot_nn(NTR[...], GVZ[...]) + dot_nn(BTR[...], ATZ[...])
    GS[:, :, :, VO] = grad_vo.astype(BF16).reshape(4, 4, 32, 128)
    first_ring(3)

    def over_cores(s, own, received, total):
        total[s] = (own[s, c].astype(F32) + received[s].astype(F32)).astype(BF16)

    out_core[0].wait_recv()
    over_cores(ox, PO, RO, SO)
    out_across = track(send(M_OUT + 2, SO.at[ox], XO.at[0], dev(ox, c, ot)))

    totals = [jnp.zeros((1, 512), F32) for _ in range(4)]
    dx_core = []
    for i, s in enumerate((ox, xh)):
        part = rows_of(s)
        n = NRM[s]
        grad_mlp = dot_nt(GC[part, UP], columns_of(UP, 256))
        grad_normed = dot_nt(GC[part, QK], columns_of(QK, 128)) + dot_nt(GVZ[part], columns_of(VO, 128))
        for j, term in enumerate((grad_normed * n, grad_normed, grad_mlp * n, grad_mlp)):
            totals[j] = totals[j] + jnp.sum(term, axis=0, keepdims=True)
        joined = grad_normed * g1 + grad_mlp * g2
        mean_one = jnp.mean(joined, axis=1, keepdims=True)
        mean_two = jnp.mean(joined * n, axis=1, keepdims=True)
        term = RSQ[s][:, :1] * (joined - mean_one - n * mean_two)
        PD[s] = term.astype(BF16).reshape(2, 128, 512)
        dx_core.append(track(send(M_DX + i, PD.at[s, oc], RD.at[s], core)))

    up_rows = jnp.concatenate([gb_up[:, :128], gb_up[:, 128:]], axis=0)
    v_row = jnp.concatenate([gb_v, jnp.zeros((1, 128 - HD), F32)], axis=1)
    for zz in range(4):
        lanes = slice(zz * 128, (zz + 1) * 128)
        pieces = [total[:, lanes] for total in totals] + [bias_grad[:, lanes], gb_qk, v_row, up_rows]
        EG[zz] = jnp.concatenate(pieces + [jnp.zeros((7, 128), F32)], axis=0).astype(BF16)
    rse1 = [track(send(M_RSE1 + k - 1, EG, RE1.at[k - 1], ydev(k))) for k in (2, 1, 3)]

    dx_core[0].wait_recv()
    over_cores(ox, PD, RD, SD)
    parts_of_rows = (slice(0, 64), slice(64, 128))
    dx_across = [
        track(send(M_DX + 2 + i, SD.at[ox, part], XD.at[0, part], dev(ox, c, ot)))
        for i, part in enumerate(parts_of_rows)
    ]
    dx_core[1].wait_recv()
    over_cores(xh, PD, RD, SD)
    out_core[1].wait_recv()
    over_cores(xh, PO, RO, SO)

    def summed(own, received):
        total = own.astype(F32)
        for k in range(3):
            total = total + received[k].astype(F32)
        return total

    rs2 = []

    def second_ring(part):
        route, columns = PARTS[part]
        for copy in rs1[3 * part : 3 * part + 3]:
            copy.wait_recv()
        here = local(columns)
        if route == 0:
            SA[:, :, here] = summed(GS[:, y, :, columns], RA1[:, :, :, here]).astype(BF16)
        else:
            SB[:, :, here] = summed(GS[z, :, :, columns], RB1[:, :, :, here]).astype(BF16)
        for k in (2, 1, 3):
            src = (SA.at[(z + k) % 4, :, here], SB.at[(y + k) % 4, :, here])[route]
            dst = (RA2, RB2)[route].at[k - 1, :, here]
            rs2.append(track(send(M_RS2 + 3 * part + k - 1, src, dst, (zdev, ydev)[route](k))))

    second_ring(0)
    second_ring(1)
    out_across.wait_recv()
    TO[...] = (SO[xh].astype(F32) + XO[0].astype(F32)).astype(BF16)
    out_pair = track(send(M_OUT + 3, TO, XO.at[1], dev(xh, c, ot)))

    second_ring(2)
    second_ring(3)
    dx_pair = []
    for i, part in enumerate(parts_of_rows):
        dx_across[i].wait_recv()
        TD[part] = (SD[xh, part].astype(F32) + XD[0, part].astype(F32)).astype(BF16)
        dx_pair.append(track(send(M_DX + 4 + i, TD.at[part], XD.at[1, part], dev(xh, c, ot))))

    for copy in rse1:
        copy.wait_recv()
    SE[...] = summed(EG[...], RE1).astype(BF16)
    rse2 = [track(send(M_RSE2 + k - 1, SE.at[(z + k) % 4], RE2.at[k - 1], zdev(k))) for k in (2, 1, 3)]

    for copy in rs2:
        copy.wait_recv()
    FB[:, :, HALF[0]] = summed(SA[z], RA2).astype(BF16).reshape(2, 16, 384)
    FB[:, :, HALF[1]] = summed(SB[y], RB2).astype(BF16).reshape(2, 16, 384)
    fin = [
        track(send(M_FIN, FB.at[ox], XR.at[xh, c], dev(ox, c, t))),
        track(send(M_FIN + 1, FB.at[ox], XR.at[xh, c], dev(ox, oc, t))),
        track(send(M_FIN + 2, FB.at[xh], XR.at[xh, c], dev(xh, oc, t))),
    ]
    XR[xh, c] = FB[xh]
    for copy in rse2:
        copy.wait_recv()
    FE[...] = summed(SE[z], RE2).astype(BF16)
    fine = [track(send(M_FINE + i, FE, XF.at[t, xh, c], where)) for i, where in enumerate(group)]
    XF[t, xh, c] = FE[...]

    for copy in dx_pair:
        copy.wait_recv()
    gin_o[...] = CT[xh, c].astype(F32) + (TD[...].astype(F32) + XD[1].astype(F32))

    out_pair.wait_recv()
    total = TO[...].astype(F32) + XO[1].astype(F32)
    out_o[...] = (TK[xh, c].astype(F32) + (total + b_branch)).astype(BF16)

    for copy in fin:
        copy.wait_recv()
    for xx in range(2):
        both = [XR[xx, 0].astype(F32), XR[xx, 1].astype(F32)]
        lanes = slice(xx * 128, (xx + 1) * 128)
        low = iota((16, 128), 1) < HD

        def join(first, second):
            return jnp.where(low, first, pltpu.roll(second, HD, 1)), jnp.where(low, pltpu.roll(first, HD, 1), second)

        q_new, k_new = join(both[0][:, QK], both[1][:, QK])
        v_new, o_new = join(both[0][:, VO], both[1][:, VO])
        gqkvw_o[0, :, lanes] = q_new
        gqkvw_o[1, :, lanes] = k_new
        gqkvw_o[2, :, lanes] = v_new
        goutw_o[:, lanes] = o_new
        for cc in range(2):
            wide = slice((xx * 2 + cc) * 256, (xx * 2 + cc + 1) * 256)
            gupw_o[:, wide] = both[cc][:, UP]
            gdownw_o[:, wide] = both[cc][:, DN]

    for copy in fine:
        copy.wait_recv()
    tiles = [[[XF[tt, xx, cc].astype(F32) for cc in range(2)] for xx in range(2)] for tt in range(2)]
    whole = jnp.zeros((16, 128), F32)
    for tt in range(2):
        for xx in range(2):
            for cc in range(2):
                whole = whole + tiles[tt][xx][cc]
    whole = jnp.where(row16 == 4, tiles[0][0][0], whole)
    whole = pltpu.roll(whole, (128 - 16 * (y * 2 + xh)) % 128, 1)
    for row, ref in enumerate((gg1_o, gb1_o, gg2_o, gb2_o, gbias_o)):
        ref[...] = whole[row : row + 1, 0:16]
    j4, h4 = iota((2, 4), 0), iota((2, 4), 1)
    j16, h16 = iota((2, 16), 0), iota((2, 16), 1)
    new_qkv = [jnp.zeros((2, 4), F32) for _ in range(3)]
    new_up = jnp.zeros((2, 16), F32)
    for xx in range(2):
        for cc in range(2):
            head = xx * 2 + cc
            tile = jnp.where(t == 0, tiles[0][xx][cc], tiles[1][xx][cc])
            for j in range(2):
                low_col = jnp.sum(jnp.where(lane16 == 2 * place + j, tile, 0.0), axis=1, keepdims=True)
                high_col = jnp.sum(jnp.where(lane16 == HD + 2 * place + j, tile, 0.0), axis=1, keepdims=True)
                spot = (j4 == j) & (h4 == head)
                for which, item in enumerate((low_col[5:6], high_col[5:6], low_col[6:7])):
                    new_qkv[which] = jnp.where(spot, item, new_qkv[which])
                for u, item in enumerate((low_col[7:8], high_col[7:8], low_col[8:9], high_col[8:9])):
                    new_up = jnp.where((j16 == j) & (h16 == head * 4 + u), item, new_up)
    for which in range(3):
        gqkvb_o[which] = new_qkv[which]
    gupb_o[...] = new_up
    for copy in sent:
        copy.wait_send()


def place_results(*refs):
    ins, outs, sems = refs[:13], refs[13:27], refs[27]
    copies = [pltpu.make_async_copy(src, dst, sems.at[i]) for i, (src, dst) in enumerate(zip(ins + (ins[9],), outs))]
    for copy in copies:
        copy.start()
    for copy in copies:
        copy.wait()


def body(
    tokens, positions, cotangent, ln1_gain, ln1_bias, ln2_gain, ln2_bias, qkv_weight, qkv_bias, out_weight, out_bias,
    up_weight, up_bias, down_weight, down_bias,
):
    shape = jax.ShapeDtypeStruct
    row = shape((1, 16), F32)
    operands = (
        tokens, positions.reshape(1, 128), cotangent, ln1_gain, ln1_bias, ln2_gain, ln2_bias, qkv_weight[0],
        qkv_bias[0].transpose(0, 2, 1), out_weight[0].T, out_bias, up_weight[0], up_bias[0].T, down_weight[0].T,
        down_bias,
    )
    outs = (
        shape((128, 512), BF16), shape((128, 512), F32), row, row, row, row, shape((3, 16, 256), F32),
        shape((3, 2, 4), F32), shape((16, 256), F32), row, shape((16, 1024), F32), shape((2, 16), F32),
        shape((16, 1024), F32),
    )
    scratch = [
        *[((1, 16), BF16)] * 4, ((3, 16, 256), BF16), ((3, 2, 4), BF16), ((16, 256), BF16), ((1, 16), BF16),
        ((16, 1024), BF16), ((2, 16), BF16), ((16, 1024), BF16), ((1, 16), BF16),
        ((4, 4, 2, 16, 768), BF16), ((16, 768), BF16), ((4, 4, 16, 128), BF16), ((3, 16, 128), BF16),
        ((2, 2, 128, 512), BF16), ((2, 2, 128, 512), BF16), ((2, 2, 1, 128), jnp.int32), ((16, 128), F32),
        ((2, 256, 512), F32), ((2, 256, 128), F32), ((2, 256, 512), BF16), ((2, 256, 512), BF16),
        ((512, 512), BF16), ((512, 512), BF16), ((512, 512), BF16),
        ((2, 256, 128), F32), ((2, 256, 128), F32), ((2, 256, 128), F32),
        ((512, 768), BF16), ((512, 128), BF16), ((512, 128), BF16),
        ((2, 2, 128, 512), BF16), ((2, 128, 512), BF16), ((2, 128, 512), BF16), ((2, 128, 512), BF16),
        ((128, 512), BF16), ((2, 2, 128, 512), BF16), ((2, 128, 512), BF16), ((2, 128, 512), BF16),
        ((2, 128, 512), BF16), ((128, 512), BF16),
        ((4, 4, 32, 768), BF16), ((3, 4, 32, 384), BF16), ((3, 4, 32, 384), BF16), ((4, 32, 384), BF16),
        ((4, 32, 384), BF16), ((3, 32, 384), BF16), ((3, 32, 384), BF16),
        ((4, 16, 128), BF16), ((3, 4, 16, 128), BF16), ((4, 16, 128), BF16), ((3, 16, 128), BF16),
        ((2, 16, 768), BF16), ((2, 2, 16, 768), BF16), ((16, 128), BF16), ((2, 2, 2, 16, 128), BF16),
    ]
    results = pl.pallas_call(
        kernel,
        out_shape=outs,
        in_specs=[pl.BlockSpec(memory_space=pl.ANY)] * len(operands),
        out_specs=[pl.BlockSpec(memory_space=pltpu.VMEM)] * len(outs),
        scratch_shapes=[pltpu.VMEM(*item) for item in scratch]
        + [pltpu.SemaphoreType.DMA((M_ALL,)), pltpu.SemaphoreType.DMA((M_ALL,)), pltpu.SemaphoreType.DMA((15,))],
        compiler_params=pltpu.CompilerParams(
            collective_id=0, has_side_effects=True, vmem_limit_bytes=GRANT
        ),
    )(*operands)
    results = pl.pallas_call(
        place_results,
        out_shape=outs + (row,),
        in_specs=[pl.BlockSpec(memory_space=pltpu.VMEM)] * 13,
        out_specs=[pl.BlockSpec(memory_space=pl.ANY)] * 14,
        scratch_shapes=[pltpu.SemaphoreType.DMA((14,))],
        compiler_params=pltpu.CompilerParams(vmem_limit_bytes=GRANT),
    )(*results)
    (
        output, grad_input, grad_gain1, grad_shift1, grad_gain2, grad_shift2, grad_qkv, grad_qkv_bias, grad_out,
        grad_bias, grad_up, grad_up_bias, grad_down, grad_bias_again,
    ) = results
    return (
        output, grad_input, grad_gain1, grad_shift1, grad_gain2, grad_shift2, grad_qkv[None],
        grad_qkv_bias.transpose(0, 2, 1)[None], grad_out.T[None], grad_bias, grad_up[None], grad_up_bias.T[None],
        grad_down.T[None], grad_bias_again,
    )


def solution(mesh):
    row = P(None, "fsdp")
    tokens = P(("fsdp", "ctx"), None)
    qkv, qkv_bias = P(None, None, "fsdp", "tp"), P(None, None, "tp", "fsdp")
    fanned, spread = P(None, "tp", "fsdp"), P(None, "fsdp", "tp")
    in_specs = (
        tokens, P(("fsdp", "ctx")), tokens, row, row, row, row, qkv, qkv_bias, fanned, row, spread, fanned, fanned, row
    )
    out_specs = (
        tokens, tokens, row, row, row, row, qkv, qkv_bias, fanned, row, spread, fanned, fanned, row
    )
    return jax.shard_map(body, mesh=mesh, in_specs=in_specs, out_specs=out_specs, check_vma=False)
```

```python
import math

import jax
import jax.numpy as jnp
import numpy as np
from jax import lax
from jax.experimental import pallas as pl
from jax.experimental.pallas import tpu as pltpu
from jax.sharding import PartitionSpec as P

HD = 64
ROT = 16
EPS = 1e-05
BASE = 10000.0
MASKED = -1e30
SCALE = 1.0 / math.sqrt(HD)
INV_ROOT_TWO = 1.0 / math.sqrt(2.0)
INV_ROOT_TWO_PI = 1.0 / math.sqrt(2.0 * math.pi)
MESH = pl.DeviceIdType.MESH
F32 = jnp.float32
BF16 = jnp.bfloat16
GRANT = 40 * 1024 * 1024

UP = slice(0, 256)
QK = slice(256, 384)
DN = slice(384, 640)
VO = slice(640, 768)
HALF = (slice(0, 384), slice(384, 768))

PARTS = ((0, UP), (1, DN), (0, QK), (1, VO))

M_XW, M_XE = 0, 1
M_POS = 2
M_TOK = 5
M_COT = 8
M_AG1 = 12
M_AGE1 = 18
M_AG2 = 21
M_AGE2 = 33
M_OUT = 36
M_DX = 40
M_RS1 = 46
M_RSE1 = 58
M_RS2 = 61
M_RSE2 = 73
M_FIN = 76
M_FINE = 79
M_ALL = 86


def dot_nn(left, right):
    return lax.dot_general(left, right, (((1,), (0,)), ((), ())), preferred_element_type=F32)


def dot_nt(left, right):
    return lax.dot_general(left, right, (((1,), (1,)), ((), ())), preferred_element_type=F32)


def dot_tn(left, right):
    return lax.dot_general(left, right, (((0,), (0,)), ((), ())), preferred_element_type=F32)


def iota(shape, dim):
    return lax.broadcasted_iota(jnp.int32, shape, dim)


def turn_partner(pair):
    lane = iota(pair.shape, 1) % HD
    return jnp.where(
        lane < ROT // 2, pltpu.roll(pair, pair.shape[1] - ROT // 2, 1), pltpu.roll(pair, ROT // 2, 1)
    )


def kernel(
    tok_in, pos_in, cot_in, gain1_in, shift1_in, gain2_in, shift2_in, qkv_w_in, qkv_b_in, out_w_in, out_b_in, up_w_in,
    up_b_in, down_w_in, down_b_in,
    out_o, gin_o, gg1_o, gb1_o, gg2_o, gb2_o, gqkvw_o, gqkvb_o, goutw_o, gbias_o, gupw_o, gupb_o, gdownw_o,
    gain1, shift1, gain2, shift2, qkv_w, qkv_b, out_w, out_b, up_w, up_b, down_w, down_b,
    W, XS, E, XE, TK, CT, PS, SM,
    NRM, RSQ, NB, MB, NTR, MTR, BTR, COS, SIN, PCOL,
    GC, GVZ, ATZ, PO, RO, SO, XO, TO, PD, RD, SD, XD, TD,
    GS, RA1, RB1, SA, SB, RA2, RB2, EG, RE1, SE, RE2, FB, XR, FE, XF,
    ss, rs, ls,
):
    place = lax.axis_index("fsdp")
    z, y, xh = place // 8, (place // 2) % 4, place % 2
    c = lax.axis_index("ctx")
    t = lax.axis_index("tp")
    ox, oc, ot = 1 - xh, 1 - c, 1 - t

    def dev(xx, cc, tt, zz=z, yy=y):
        return {"fsdp": zz * 8 + yy * 2 + xx, "ctx": cc, "tp": tt}

    def zdev(k):
        return dev(xh, c, t, zz=(z + k) % 4)

    def ydev(k):
        return dev(xh, c, t, yy=(y + k) % 4)

    def send(number, src, dst, where):
        copy = pltpu.make_async_remote_copy(
            src_ref=src, dst_ref=dst, send_sem=ss.at[number], recv_sem=rs.at[number],
            device_id=where, device_id_type=MESH,
        )
        copy.start()
        return copy

    sent = []

    def track(copy):
        sent.append(copy)
        return copy

    barrier = pltpu.get_barrier_semaphore()
    group = [
        dev(xh, oc, t), dev(ox, c, t), dev(ox, c, ot), dev(ox, oc, t), dev(xh, c, ot), dev(xh, oc, ot), dev(ox, oc, ot)
    ]
    peers = group + [zdev(k) for k in (1, 2, 3)] + [ydev(k) for k in (1, 2, 3)]
    for peer in peers:
        pl.semaphore_signal(barrier, inc=1, device_id=peer, device_id_type=MESH)

    loads = []
    for i, (src, dst) in enumerate((
        (qkv_w_in, qkv_w), (out_w_in, out_w), (up_w_in, up_w), (down_w_in, down_w), (gain1_in, gain1),
        (shift1_in, shift1), (gain2_in, gain2), (shift2_in, shift2), (out_b_in, out_b), (down_b_in, down_b),
        (qkv_b_in, qkv_b), (up_b_in, up_b), (pos_in, PS.at[xh, c]), (tok_in, TK.at[xh, c]), (cot_in, CT.at[xh, c]),
    )):
        loads.append(pltpu.make_async_copy(src, dst, ls.at[i]))
        loads[-1].start()
    for load in loads[:4]:
        load.wait()

    def cut(xx):
        lanes = pl.ds(pl.multiple_of(xx * 128, 128), 128)
        q_pair, k_pair, v_pair, o_pair = (
            ref[:, lanes].astype(F32) for ref in (qkv_w.at[0], qkv_w.at[1], qkv_w.at[2], out_w)
        )
        low = iota((16, 128), 1) < HD
        first = c == 0

        def halves(a, b):
            a_low = jnp.where(first, a, pltpu.roll(a, HD, 1))
            b_high = jnp.where(first, pltpu.roll(b, HD, 1), b)
            return jnp.where(low, a_low, b_high).astype(BF16)

        wide = pl.ds(pl.multiple_of((xx * 2 + c) * 256, 256), 256)
        return up_w[:, wide], halves(q_pair, k_pair), down_w[:, wide], halves(v_pair, o_pair)

    for target, xx in ((XS, ox), (W.at[z, y, xh], xh)):
        up_cut, qk_cut, down_cut, vo_cut = cut(xx)
        target[:, UP] = up_cut
        target[:, QK] = qk_cut
        target[:, DN] = down_cut
        target[:, VO] = vo_cut

    for load in loads[4:12]:
        load.wait()
    SM[...] = jnp.zeros((16, 128), F32)
    for row, ref in enumerate((gain1, shift1, gain2, shift2, out_b, down_b)):
        SM[row : row + 1, 0:16] = ref[...].astype(F32)
    for which in range(3):
        SM[8 + 2 * which : 10 + 2 * which, 0:4] = qkv_b[which].astype(F32)
    SM[6:8, 0:16] = up_b[...].astype(F32)
    SM[14:16, 0:16] = up_b[...].astype(F32)

    row16, lane16 = iota((16, 128), 0), iota((16, 128), 1)

    def placed(xx):
        raw = SM[...]
        head = xx * 2 + c

        def column(lane):
            return jnp.sum(jnp.where(lane16 == lane, raw, 0.0), axis=1, keepdims=True)

        spread = pltpu.roll(raw, 16 * (y * 2 + xh), 1)
        low = lane16 < HD
        hit = (lane16 % HD) == 2 * place + row16 % 2
        qkv = jnp.where(low != ((row16 == 10) | (row16 == 11)), column(head), 0.0)
        up_first = jnp.where(low, column(4 * head), column(4 * head + 1))
        up_second = jnp.where(low, column(4 * head + 2), column(4 * head + 3))
        bias = jnp.where(row16 < 8, up_first, jnp.where(row16 < 14, qkv, up_second))
        return jnp.where(row16 < 6, spread, jnp.where(hit, bias, 0.0))

    XE[0] = placed(ox).astype(BF16)
    XE[1] = placed(xh).astype(BF16)

    pl.semaphore_wait(barrier, len(peers))

    xw = track(send(M_XW, XS, W.at[z, y, xh], dev(ox, c, t)))
    xe = track(send(M_XE, XE.at[0], XE.at[2], dev(ox, c, t)))
    across = dev(ox, c, ot)
    core = dev(xh, oc, t)
    tok_across = track(send(M_TOK, tok_in, TK.at[xh, c], across))
    tok_core = track(send(M_TOK + 1, tok_in, TK.at[xh, c], core))
    pos_copies = [
        track(send(M_POS + i, pos_in, PS.at[xh, c], where))
        for i, where in enumerate((core, dev(ox, c, t), dev(ox, oc, t)))
    ]
    cot_across = track(send(M_COT, cot_in, CT.at[xh, c], across))
    cot_core = track(send(M_COT + 1, cot_in, CT.at[xh, c], core))

    xw.wait_recv()
    ag1 = []
    for k in (2, 1, 3):
        here = W.at[z, y, :, :, HALF[0]]
        ag1.append(track(send(M_AG1 + k - 1, here, here, zdev(k))))
        here = W.at[z, y, :, :, HALF[1]]
        ag1.append(track(send(M_AG1 + 3 + k - 1, here, here, ydev(k))))
    xe.wait_recv()
    E[z, y] = (XE[1].astype(F32) + XE[2].astype(F32)).astype(BF16)
    for k in (2, 1, 3):
        ag1.append(track(send(M_AGE1 + k - 1, E.at[z, y], E.at[z, y], zdev(k))))
    tok_across.wait_recv()
    tok_pass = track(send(M_TOK + 2, TK.at[ox, c], TK.at[ox, c], core))
    for copy in ag1:
        copy.wait_recv()
    ag2 = []
    age2 = []
    for k in (2, 1, 3):
        age2.append(track(send(M_AGE2 + k - 1, E.at[:, y], E.at[:, y], ydev(k))))
    for part, (route, columns) in enumerate(PARTS):
        for k in (2, 1, 3):
            here = (W.at[:, y, :, :, columns], W.at[z, :, :, :, columns])[route]
            number = M_AG2 + 3 * part + k - 1
            ag2.append(track(send(number, here, here, (ydev, zdev)[route](k))))
    cot_across.wait_recv()
    cot_pass = track(send(M_COT + 2, CT.at[ox, c], CT.at[ox, c], core))
    for load in loads[12:]:
        load.wait()
    tok_core.wait_recv()
    tok_pass.wait_recv()

    for s in range(2):
        rows = TK[s].reshape(256, 512).astype(F32)
        centered = rows - jnp.mean(rows, axis=1, keepdims=True)
        moment = jnp.mean(centered * centered, axis=1, keepdims=True)
        rsq = lax.rsqrt(moment + EPS)
        NRM[s] = centered * rsq
        RSQ[s] = jnp.broadcast_to(rsq, (256, 128))

    for copy in pos_copies:
        copy.wait_recv()
    row8 = iota((8, 128), 0)
    inverse = jnp.zeros((8, 128), F32)
    for r in range(ROT // 2):
        inverse = jnp.where(row8 == r, float(np.float32(BASE ** (-2.0 * r / ROT))), inverse)
    ones, zeros = jnp.ones((48, 128), F32), jnp.zeros((48, 128), F32)
    for s in range(2):
        for b in range(2):
            places = PS[s, b].astype(F32)
            angle = jnp.broadcast_to(places, (8, 128)) * inverse
            cos, sin = jnp.cos(angle), jnp.sin(angle)
            part = pl.ds(b * 128, 128)
            COS[s, part] = jnp.concatenate([cos, cos, ones, cos, cos, ones], axis=0).T
            SIN[s, part] = jnp.concatenate([-sin, sin, zeros, -sin, sin, zeros], axis=0).T
            PCOL[s, part] = jnp.broadcast_to(places, (128, 128)).T

    cot_core.wait_recv()
    cot_pass.wait_recv()
    bias_grad = jnp.zeros((1, 512), F32)
    for s in range(2):
        grad = CT[s].reshape(256, 512)
        BTR[:, s * 256 : (s + 1) * 256] = grad.T
        bias_grad = bias_grad + jnp.sum(grad.astype(F32), axis=0, keepdims=True)

    for copy in age2:
        copy.wait_recv()
    per_z = []
    for zz in range(4):
        total = E[zz, 0].astype(F32)
        for yy in range(1, 4):
            total = total + E[zz, yy].astype(F32)
        per_z.append(total)
    vectors = jnp.concatenate(per_z, axis=1)
    all_z = per_z[0] + per_z[1] + per_z[2] + per_z[3]
    g1, b1, g2, b2 = (vectors[r : r + 1] for r in range(4))
    b_branch = vectors[4:5] + vectors[5:6]
    b_up = jnp.concatenate([all_z[6:7] + all_z[7:8], all_z[14:15] + all_z[15:16]], axis=1)
    b_qk = all_z[8:9] + all_z[9:10] + all_z[10:11] + all_z[11:12]
    b_v = (all_z[12:13] + all_z[13:14])[:, :HD]

    for s in range(2):
        n = NRM[s]
        normed = (n * g1 + b1).astype(BF16)
        mlp_input = (n * g2 + b2).astype(BF16)
        NB[s] = normed
        MB[s] = mlp_input
        NTR[:, s * 256 : (s + 1) * 256] = normed.T
        MTR[:, s * 256 : (s + 1) * 256] = mlp_input.T

    for copy in ag2[:6]:
        copy.wait_recv()

    def columns_of(columns, width):
        return W[:, :, :, :, columns].reshape(512, width)

    gb_up = jnp.zeros((1, 256), F32)
    for s in range(2):
        part = slice(s * 256, (s + 1) * 256)
        branch_grad = CT[s].reshape(256, 512)
        pre_act = dot_nn(MB[s], columns_of(UP, 256)) + b_up
        phi = 0.5 * (1.0 + lax.erf(pre_act * INV_ROOT_TWO))
        density = jnp.exp(-0.5 * pre_act * pre_act) * INV_ROOT_TWO_PI
        grad_hidden = dot_nn(branch_grad, columns_of(DN, 256))
        grad_pre = (grad_hidden * (phi + pre_act * density)).astype(BF16)
        gb_up = gb_up + jnp.sum(grad_pre.astype(F32), axis=0, keepdims=True)
        GC[part, UP] = grad_pre
        GC[part, DN] = (pre_act * phi).astype(BF16)

    rs1 = []

    def first_ring(part):
        route, columns = PARTS[part]
        for k in (2, 1, 3):
            src = (GS.at[:, (y + k) % 4, :, columns], GS.at[(z + k) % 4, :, :, columns])[route]
            dst = (RA1, RB1)[route].at[k - 1, :, :, local(columns)]
            rs1.append(track(send(M_RS1 + 3 * part + k - 1, src, dst, (ydev, zdev)[route](k))))

    def local(columns):
        return slice(columns.start % 384, (columns.stop - 1) % 384 + 1)

    GS[:, :, :, UP] = dot_nn(MTR[...], GC[:, UP]).astype(BF16).reshape(4, 4, 32, 256)
    first_ring(0)
    GS[:, :, :, DN] = dot_nn(BTR[...], GC[:, DN]).astype(BF16).reshape(4, 4, 32, 256)
    first_ring(1)

    for copy in ag2[6:]:
        copy.wait_recv()
    gb_qk = jnp.zeros((1, 128), F32)
    gb_v = jnp.zeros((1, HD), F32)
    for s in range(2):
        part = slice(s * 256, (s + 1) * 256)
        normed, branch_grad = NB[s], CT[s].reshape(256, 512)
        w_vo = columns_of(VO, 128)
        cos, sin = COS[s], SIN[s]
        qk = dot_nn(normed, columns_of(QK, 128)) + b_qk
        qk = (qk * cos + turn_partner(qk) * sin).astype(BF16)
        query, key = qk[:, :HD], qk[:, HD:]
        value = (dot_nn(normed, w_vo)[:, :HD] + b_v).astype(BF16)
        grad_att = dot_nn(branch_grad, w_vo)[:, HD:].astype(BF16)
        row, col = iota((256, 256), 0), iota((256, 256), 1)
        start = row.astype(F32) - jnp.concatenate([PCOL[s], PCOL[s]], axis=1)
        visible = (col <= row) & (col.astype(F32) >= start)
        scores = jnp.where(visible, dot_nt(query, key) * SCALE, MASKED)
        exps = jnp.exp(scores - jnp.max(scores, axis=1, keepdims=True))
        probs = exps / jnp.sum(exps, axis=1, keepdims=True)
        probs_low = probs.astype(BF16)
        attended = dot_nn(probs_low, value).astype(BF16)
        grad_probs = dot_nt(grad_att, value)
        row_dot = jnp.sum(probs * grad_probs, axis=1, keepdims=True)
        grad_scores = (probs * (grad_probs - row_dot)).astype(BF16)
        grad_query = dot_nn(grad_scores, key) * SCALE
        grad_key = dot_tn(grad_scores, query) * SCALE
        grad_value = dot_tn(probs_low, grad_att).astype(BF16)
        grad_qk = jnp.concatenate([grad_query, grad_key], axis=1)
        grad_qk = (grad_qk * cos - turn_partner(grad_qk) * sin).astype(BF16)
        gb_qk = gb_qk + jnp.sum(grad_qk.astype(F32), axis=0, keepdims=True)
        gb_v = gb_v + jnp.sum(grad_value.astype(F32), axis=0, keepdims=True)
        blank = jnp.zeros((256, HD), BF16)
        GC[part, QK] = grad_qk
        GVZ[part] = jnp.concatenate([grad_value, blank], axis=1)
        ATZ[part] = jnp.concatenate([blank, attended], axis=1)

    def rows_of(s):
        return pl.ds(pl.multiple_of(s * 256, 256), 256)

    out_core = []
    for i, s in enumerate((ox, xh)):
        part = rows_of(s)
        branch = dot_nt(GC[part, DN], columns_of(DN, 256)) + dot_nt(ATZ[part], columns_of(VO, 128))
        PO[s] = branch.astype(BF16).reshape(2, 128, 512)
        out_core.append(track(send(M_OUT + i, PO.at[s, oc], RO.at[s], core)))

    GS[:, :, :, QK] = dot_nn(NTR[...], GC[:, QK]).astype(BF16).reshape(4, 4, 32, 128)
    first_ring(2)
    grad_vo = dot_nn(NTR[...], GVZ[...]) + dot_nn(BTR[...], ATZ[...])
    GS[:, :, :, VO] = grad_vo.astype(BF16).reshape(4, 4, 32, 128)
    first_ring(3)

    def over_cores(s, own, received, total):
        total[s] = (own[s, c].astype(F32) + received[s].astype(F32)).astype(BF16)

    out_core[0].wait_recv()
    over_cores(ox, PO, RO, SO)
    out_across = track(send(M_OUT + 2, SO.at[ox], XO.at[0], dev(ox, c, ot)))

    totals = [jnp.zeros((1, 512), F32) for _ in range(4)]
    dx_core = []
    for i, s in enumerate((ox, xh)):
        part = rows_of(s)
        n = NRM[s]
        grad_mlp = dot_nt(GC[part, UP], columns_of(UP, 256))
        grad_normed = dot_nt(GC[part, QK], columns_of(QK, 128)) + dot_nt(GVZ[part], columns_of(VO, 128))
        for j, term in enumerate((grad_normed * n, grad_normed, grad_mlp * n, grad_mlp)):
            totals[j] = totals[j] + jnp.sum(term, axis=0, keepdims=True)
        joined = grad_normed * g1 + grad_mlp * g2
        mean_one = jnp.mean(joined, axis=1, keepdims=True)
        mean_two = jnp.mean(joined * n, axis=1, keepdims=True)
        term = RSQ[s][:, :1] * (joined - mean_one - n * mean_two)
        PD[s] = term.astype(BF16).reshape(2, 128, 512)
        dx_core.append(track(send(M_DX + i, PD.at[s, oc], RD.at[s], core)))

    up_rows = jnp.concatenate([gb_up[:, :128], gb_up[:, 128:]], axis=0)
    v_row = jnp.concatenate([gb_v, jnp.zeros((1, 128 - HD), F32)], axis=1)
    for zz in range(4):
        lanes = slice(zz * 128, (zz + 1) * 128)
        pieces = [total[:, lanes] for total in totals] + [bias_grad[:, lanes], gb_qk, v_row, up_rows]
        EG[zz] = jnp.concatenate(pieces + [jnp.zeros((7, 128), F32)], axis=0).astype(BF16)
    rse1 = [track(send(M_RSE1 + k - 1, EG, RE1.at[k - 1], ydev(k))) for k in (2, 1, 3)]

    dx_core[0].wait_recv()
    over_cores(ox, PD, RD, SD)
    parts_of_rows = (slice(0, 64), slice(64, 128))
    dx_across = [
        track(send(M_DX + 2 + i, SD.at[ox, part], XD.at[0, part], dev(ox, c, ot)))
        for i, part in enumerate(parts_of_rows)
    ]
    dx_core[1].wait_recv()
    over_cores(xh, PD, RD, SD)
    out_core[1].wait_recv()
    over_cores(xh, PO, RO, SO)

    def summed(own, received):
        total = own.astype(F32)
        for k in range(3):
            total = total + received[k].astype(F32)
        return total

    rs2 = []

    def second_ring(part):
        route, columns = PARTS[part]
        for copy in rs1[3 * part : 3 * part + 3]:
            copy.wait_recv()
        here = local(columns)
        if route == 0:
            SA[:, :, here] = summed(GS[:, y, :, columns], RA1[:, :, :, here]).astype(BF16)
        else:
            SB[:, :, here] = summed(GS[z, :, :, columns], RB1[:, :, :, here]).astype(BF16)
        for k in (2, 1, 3):
            src = (SA.at[(z + k) % 4, :, here], SB.at[(y + k) % 4, :, here])[route]
            dst = (RA2, RB2)[route].at[k - 1, :, here]
            rs2.append(track(send(M_RS2 + 3 * part + k - 1, src, dst, (zdev, ydev)[route](k))))

    second_ring(0)
    second_ring(1)
    out_across.wait_recv()
    TO[...] = (SO[xh].astype(F32) + XO[0].astype(F32)).astype(BF16)
    out_pair = track(send(M_OUT + 3, TO, XO.at[1], dev(xh, c, ot)))

    second_ring(2)
    second_ring(3)
    dx_pair = []
    for i, part in enumerate(parts_of_rows):
        dx_across[i].wait_recv()
        TD[part] = (SD[xh, part].astype(F32) + XD[0, part].astype(F32)).astype(BF16)
        dx_pair.append(track(send(M_DX + 4 + i, TD.at[part], XD.at[1, part], dev(xh, c, ot))))

    for copy in rse1:
        copy.wait_recv()
    SE[...] = summed(EG[...], RE1).astype(BF16)
    rse2 = [track(send(M_RSE2 + k - 1, SE.at[(z + k) % 4], RE2.at[k - 1], zdev(k))) for k in (2, 1, 3)]

    for copy in rs2:
        copy.wait_recv()
    FB[:, :, HALF[0]] = summed(SA[z], RA2).astype(BF16).reshape(2, 16, 384)
    FB[:, :, HALF[1]] = summed(SB[y], RB2).astype(BF16).reshape(2, 16, 384)
    fin = [
        track(send(M_FIN, FB.at[ox], XR.at[xh, c], dev(ox, c, t))),
        track(send(M_FIN + 1, FB.at[ox], XR.at[xh, c], dev(ox, oc, t))),
        track(send(M_FIN + 2, FB.at[xh], XR.at[xh, c], dev(xh, oc, t))),
    ]
    XR[xh, c] = FB[xh]
    for copy in rse2:
        copy.wait_recv()
    FE[...] = summed(SE[z], RE2).astype(BF16)
    fine = [track(send(M_FINE + i, FE, XF.at[t, xh, c], where)) for i, where in enumerate(group)]
    XF[t, xh, c] = FE[...]

    for copy in dx_pair:
        copy.wait_recv()
    gin_o[...] = CT[xh, c].astype(F32) + (TD[...].astype(F32) + XD[1].astype(F32))

    out_pair.wait_recv()
    total = TO[...].astype(F32) + XO[1].astype(F32)
    out_o[...] = (TK[xh, c].astype(F32) + (total + b_branch)).astype(BF16)

    for copy in fin:
        copy.wait_recv()
    for xx in range(2):
        both = [XR[xx, 0].astype(F32), XR[xx, 1].astype(F32)]
        lanes = slice(xx * 128, (xx + 1) * 128)
        low = iota((16, 128), 1) < HD

        def join(first, second):
            return jnp.where(low, first, pltpu.roll(second, HD, 1)), jnp.where(low, pltpu.roll(first, HD, 1), second)

        q_new, k_new = join(both[0][:, QK], both[1][:, QK])
        v_new, o_new = join(both[0][:, VO], both[1][:, VO])
        gqkvw_o[0, :, lanes] = q_new
        gqkvw_o[1, :, lanes] = k_new
        gqkvw_o[2, :, lanes] = v_new
        goutw_o[:, lanes] = o_new
        for cc in range(2):
            wide = slice((xx * 2 + cc) * 256, (xx * 2 + cc + 1) * 256)
            gupw_o[:, wide] = both[cc][:, UP]
            gdownw_o[:, wide] = both[cc][:, DN]

    for copy in fine:
        copy.wait_recv()
    tiles = [[[XF[tt, xx, cc].astype(F32) for cc in range(2)] for xx in range(2)] for tt in range(2)]
    whole = jnp.zeros((16, 128), F32)
    for tt in range(2):
        for xx in range(2):
            for cc in range(2):
                whole = whole + tiles[tt][xx][cc]
    whole = jnp.where(row16 == 4, tiles[0][0][0], whole)
    whole = pltpu.roll(whole, (128 - 16 * (y * 2 + xh)) % 128, 1)
    for row, ref in enumerate((gg1_o, gb1_o, gg2_o, gb2_o, gbias_o)):
        ref[...] = whole[row : row + 1, 0:16]
    j4, h4 = iota((2, 4), 0), iota((2, 4), 1)
    j16, h16 = iota((2, 16), 0), iota((2, 16), 1)
    new_qkv = [jnp.zeros((2, 4), F32) for _ in range(3)]
    new_up = jnp.zeros((2, 16), F32)
    for xx in range(2):
        for cc in range(2):
            head = xx * 2 + cc
            tile = jnp.where(t == 0, tiles[0][xx][cc], tiles[1][xx][cc])
            for j in range(2):
                low_col = jnp.sum(jnp.where(lane16 == 2 * place + j, tile, 0.0), axis=1, keepdims=True)
                high_col = jnp.sum(jnp.where(lane16 == HD + 2 * place + j, tile, 0.0), axis=1, keepdims=True)
                spot = (j4 == j) & (h4 == head)
                for which, item in enumerate((low_col[5:6], high_col[5:6], low_col[6:7])):
                    new_qkv[which] = jnp.where(spot, item, new_qkv[which])
                for u, item in enumerate((low_col[7:8], high_col[7:8], low_col[8:9], high_col[8:9])):
                    new_up = jnp.where((j16 == j) & (h16 == head * 4 + u), item, new_up)
    for which in range(3):
        gqkvb_o[which] = new_qkv[which]
    gupb_o[...] = new_up
    for copy in sent:
        copy.wait_send()


def place_results(*refs):
    ins, outs, sems = refs[:13], refs[13:27], refs[27]
    copies = [pltpu.make_async_copy(src, dst, sems.at[i]) for i, (src, dst) in enumerate(zip(ins + (ins[9],), outs))]
    for copy in copies:
        copy.start()
    for copy in copies:
        copy.wait()


def body(
    tokens, positions, cotangent, ln1_gain, ln1_bias, ln2_gain, ln2_bias, qkv_weight, qkv_bias, out_weight, out_bias,
    up_weight, up_bias, down_weight, down_bias,
):
    shape = jax.ShapeDtypeStruct
    row = shape((1, 16), F32)
    operands = (
        tokens, positions.reshape(1, 128), cotangent, ln1_gain, ln1_bias, ln2_gain, ln2_bias, qkv_weight[0],
        qkv_bias[0].transpose(0, 2, 1), out_weight[0].T, out_bias, up_weight[0], up_bias[0].T, down_weight[0].T,
        down_bias,
    )
    outs = (
        shape((128, 512), BF16), shape((128, 512), F32), row, row, row, row, shape((3, 16, 256), F32),
        shape((3, 2, 4), F32), shape((16, 256), F32), row, shape((16, 1024), F32), shape((2, 16), F32),
        shape((16, 1024), F32),
    )
    scratch = [
        *[((1, 16), BF16)] * 4, ((3, 16, 256), BF16), ((3, 2, 4), BF16), ((16, 256), BF16), ((1, 16), BF16),
        ((16, 1024), BF16), ((2, 16), BF16), ((16, 1024), BF16), ((1, 16), BF16),
        ((4, 4, 2, 16, 768), BF16), ((16, 768), BF16), ((4, 4, 16, 128), BF16), ((3, 16, 128), BF16),
        ((2, 2, 128, 512), BF16), ((2, 2, 128, 512), BF16), ((2, 2, 1, 128), jnp.int32), ((16, 128), F32),
        ((2, 256, 512), F32), ((2, 256, 128), F32), ((2, 256, 512), BF16), ((2, 256, 512), BF16),
        ((512, 512), BF16), ((512, 512), BF16), ((512, 512), BF16),
        ((2, 256, 128), F32), ((2, 256, 128), F32), ((2, 256, 128), F32),
        ((512, 768), BF16), ((512, 128), BF16), ((512, 128), BF16),
        ((2, 2, 128, 512), BF16), ((2, 128, 512), BF16), ((2, 128, 512), BF16), ((2, 128, 512), BF16),
        ((128, 512), BF16), ((2, 2, 128, 512), BF16), ((2, 128, 512), BF16), ((2, 128, 512), BF16),
        ((2, 128, 512), BF16), ((128, 512), BF16),
        ((4, 4, 32, 768), BF16), ((3, 4, 32, 384), BF16), ((3, 4, 32, 384), BF16), ((4, 32, 384), BF16),
        ((4, 32, 384), BF16), ((3, 32, 384), BF16), ((3, 32, 384), BF16),
        ((4, 16, 128), BF16), ((3, 4, 16, 128), BF16), ((4, 16, 128), BF16), ((3, 16, 128), BF16),
        ((2, 16, 768), BF16), ((2, 2, 16, 768), BF16), ((16, 128), BF16), ((2, 2, 2, 16, 128), BF16),
    ]
    results = pl.pallas_call(
        kernel,
        out_shape=outs,
        in_specs=[pl.BlockSpec(memory_space=pl.ANY)] * len(operands),
        out_specs=[pl.BlockSpec(memory_space=pltpu.VMEM)] * len(outs),
        scratch_shapes=[pltpu.VMEM(*item) for item in scratch]
        + [pltpu.SemaphoreType.DMA((M_ALL,)), pltpu.SemaphoreType.DMA((M_ALL,)), pltpu.SemaphoreType.DMA((15,))],
        compiler_params=pltpu.CompilerParams(
            collective_id=0, has_side_effects=True, vmem_limit_bytes=GRANT
        ),
    )(*(pltpu.with_memory_space_constraint(item, pltpu.HBM) for item in operands))
    results = pl.pallas_call(
        place_results,
        out_shape=outs + (row,),
        in_specs=[pl.BlockSpec(memory_space=pltpu.VMEM)] * 13,
        out_specs=[pl.BlockSpec(memory_space=pl.ANY)] * 14,
        scratch_shapes=[pltpu.SemaphoreType.DMA((14,))],
        compiler_params=pltpu.CompilerParams(vmem_limit_bytes=1024 * 1024),
    )(*results)
    (
        output, grad_input, grad_gain1, grad_shift1, grad_gain2, grad_shift2, grad_qkv, grad_qkv_bias, grad_out,
        grad_bias, grad_up, grad_up_bias, grad_down, grad_bias_again,
    ) = results
    return (
        output, grad_input, grad_gain1, grad_shift1, grad_gain2, grad_shift2, grad_qkv[None],
        grad_qkv_bias.transpose(0, 2, 1)[None], grad_out.T[None], grad_bias, grad_up[None], grad_up_bias.T[None],
        grad_down.T[None], grad_bias_again,
    )


def solution(mesh):
    row = P(None, "fsdp")
    tokens = P(("fsdp", "ctx"), None)
    qkv, qkv_bias = P(None, None, "fsdp", "tp"), P(None, None, "tp", "fsdp")
    fanned, spread = P(None, "tp", "fsdp"), P(None, "fsdp", "tp")
    in_specs = (
        tokens, P(("fsdp", "ctx")), tokens, row, row, row, row, qkv, qkv_bias, fanned, row, spread, fanned, fanned, row
    )
    out_specs = (
        tokens, tokens, row, row, row, row, qkv, qkv_bias, fanned, row, spread, fanned, fanned, row
    )
    return jax.shard_map(body, mesh=mesh, in_specs=in_specs, out_specs=out_specs, check_vma=False)
```

```python
import math

import jax
import jax.numpy as jnp
import numpy as np
from jax import lax
from jax.experimental import pallas as pl
from jax.experimental.pallas import tpu as pltpu
from jax.sharding import PartitionSpec as P

HD = 64
ROT = 16
EPS = 1e-05
BASE = 10000.0
MASKED = -1e30
SCALE = 1.0 / math.sqrt(HD)
INV_ROOT_TWO = 1.0 / math.sqrt(2.0)
INV_ROOT_TWO_PI = 1.0 / math.sqrt(2.0 * math.pi)
MESH = pl.DeviceIdType.MESH
F32 = jnp.float32
BF16 = jnp.bfloat16
GRANT = 40 * 1024 * 1024

UP = slice(0, 256)
QK = slice(256, 384)
DN = slice(384, 640)
VO = slice(640, 768)
HALF = (slice(0, 384), slice(384, 768))

PARTS = ((0, UP), (1, DN), (0, QK), (1, VO))

M_XW, M_XE = 0, 1
M_POS = 2
M_TOK = 5
M_COT = 8
M_AG1 = 12
M_AGE1 = 18
M_AG2 = 21
M_AGE2 = 33
M_OUT = 36
M_DX = 40
M_RS1 = 46
M_RSE1 = 58
M_RS2 = 61
M_RSE2 = 73
M_FIN = 76
M_FINE = 79
M_ALL = 86


def dot_nn(left, right):
    return lax.dot_general(left, right, (((1,), (0,)), ((), ())), preferred_element_type=F32)


def dot_nt(left, right):
    return lax.dot_general(left, right, (((1,), (1,)), ((), ())), preferred_element_type=F32)


def dot_tn(left, right):
    return lax.dot_general(left, right, (((0,), (0,)), ((), ())), preferred_element_type=F32)


def iota(shape, dim):
    return lax.broadcasted_iota(jnp.int32, shape, dim)


def turn_partner(pair):
    lane = iota(pair.shape, 1) % HD
    return jnp.where(
        lane < ROT // 2, pltpu.roll(pair, pair.shape[1] - ROT // 2, 1), pltpu.roll(pair, ROT // 2, 1)
    )


def kernel(
    tok_in, pos_in, cot_in, gain1_in, shift1_in, gain2_in, shift2_in, qkv_w_in, qkv_b_in, out_w_in, out_b_in, up_w_in,
    up_b_in, down_w_in, down_b_in,
    out_o, gin_o, gg1_o, gb1_o, gg2_o, gb2_o, gqkvw_o, gqkvb_o, goutw_o, gbias_o, gupw_o, gupb_o, gdownw_o,
    gain1, shift1, gain2, shift2, qkv_w, qkv_b, out_w, out_b, up_w, up_b, down_w, down_b,
    W, XS, E, XE, TK, CT, PS, SM,
    NRM, RSQ, NB, MB, NTR, MTR, BTR, COS, SIN, PCOL,
    GC, GVZ, ATZ, PO, RO, SO, XO, TO, PD, RD, SD, XD, TD,
    GS, RA1, RB1, SA, SB, RA2, RB2, EG, RE1, SE, RE2, FB, XR, FE, XF,
    ss, rs, ls,
):
    place = lax.axis_index("fsdp")
    z, y, xh = place // 8, (place // 2) % 4, place % 2
    c = lax.axis_index("ctx")
    t = lax.axis_index("tp")
    ox, oc, ot = 1 - xh, 1 - c, 1 - t

    def dev(xx, cc, tt, zz=z, yy=y):
        return {"fsdp": zz * 8 + yy * 2 + xx, "ctx": cc, "tp": tt}

    def zdev(k):
        return dev(xh, c, t, zz=(z + k) % 4)

    def ydev(k):
        return dev(xh, c, t, yy=(y + k) % 4)

    def send(number, src, dst, where):
        copy = pltpu.make_async_remote_copy(
            src_ref=src, dst_ref=dst, send_sem=ss.at[number], recv_sem=rs.at[number],
            device_id=where, device_id_type=MESH,
        )
        copy.start()
        return copy

    sent = []

    def track(copy):
        sent.append(copy)
        return copy

    barrier = pltpu.get_barrier_semaphore()
    group = [
        dev(xh, oc, t), dev(ox, c, t), dev(ox, c, ot), dev(ox, oc, t), dev(xh, c, ot), dev(xh, oc, ot), dev(ox, oc, ot)
    ]
    peers = group + [zdev(k) for k in (1, 2, 3)] + [ydev(k) for k in (1, 2, 3)]
    for peer in peers:
        pl.semaphore_signal(barrier, inc=1, device_id=peer, device_id_type=MESH)

    loads = []
    for i, (src, dst) in enumerate((
        (qkv_w_in, qkv_w), (out_w_in, out_w), (up_w_in, up_w), (down_w_in, down_w), (gain1_in, gain1),
        (shift1_in, shift1), (gain2_in, gain2), (shift2_in, shift2), (out_b_in, out_b), (down_b_in, down_b),
        (qkv_b_in, qkv_b), (up_b_in, up_b), (pos_in, PS.at[xh, c]), (tok_in, TK.at[xh, c]), (cot_in, CT.at[xh, c]),
    )):
        loads.append(pltpu.make_async_copy(src, dst, ls.at[i]))
        loads[-1].start()
    for load in loads[:4]:
        load.wait()

    def cut(xx):
        lanes = pl.ds(pl.multiple_of(xx * 128, 128), 128)
        q_pair, k_pair, v_pair, o_pair = (
            ref[:, lanes].astype(F32) for ref in (qkv_w.at[0], qkv_w.at[1], qkv_w.at[2], out_w)
        )
        low = iota((16, 128), 1) < HD
        first = c == 0

        def halves(a, b):
            a_low = jnp.where(first, a, pltpu.roll(a, HD, 1))
            b_high = jnp.where(first, pltpu.roll(b, HD, 1), b)
            return jnp.where(low, a_low, b_high).astype(BF16)

        wide = pl.ds(pl.multiple_of((xx * 2 + c) * 256, 256), 256)
        return up_w[:, wide], halves(q_pair, k_pair), down_w[:, wide], halves(v_pair, o_pair)

    for target, xx in ((XS, ox), (W.at[z, y, xh], xh)):
        up_cut, qk_cut, down_cut, vo_cut = cut(xx)
        target[:, UP] = up_cut
        target[:, QK] = qk_cut
        target[:, DN] = down_cut
        target[:, VO] = vo_cut

    for load in loads[4:12]:
        load.wait()
    SM[...] = jnp.zeros((16, 128), F32)
    for row, ref in enumerate((gain1, shift1, gain2, shift2, out_b, down_b)):
        SM[row : row + 1, 0:16] = ref[...].astype(F32)
    for which in range(3):
        SM[8 + 2 * which : 10 + 2 * which, 0:4] = qkv_b[which].astype(F32)
    SM[6:8, 0:16] = up_b[...].astype(F32)
    SM[14:16, 0:16] = up_b[...].astype(F32)

    row16, lane16 = iota((16, 128), 0), iota((16, 128), 1)

    def placed(xx):
        raw = SM[...]
        head = xx * 2 + c

        def column(lane):
            return jnp.sum(jnp.where(lane16 == lane, raw, 0.0), axis=1, keepdims=True)

        spread = pltpu.roll(raw, 16 * (y * 2 + xh), 1)
        low = lane16 < HD
        hit = (lane16 % HD) == 2 * place + row16 % 2
        qkv = jnp.where(low != ((row16 == 10) | (row16 == 11)), column(head), 0.0)
        up_first = jnp.where(low, column(4 * head), column(4 * head + 1))
        up_second = jnp.where(low, column(4 * head + 2), column(4 * head + 3))
        bias = jnp.where(row16 < 8, up_first, jnp.where(row16 < 14, qkv, up_second))
        return jnp.where(row16 < 6, spread, jnp.where(hit, bias, 0.0))

    XE[0] = placed(ox).astype(BF16)
    XE[1] = placed(xh).astype(BF16)

    pl.semaphore_wait(barrier, len(peers))

    xw = track(send(M_XW, XS, W.at[z, y, xh], dev(ox, c, t)))
    xe = track(send(M_XE, XE.at[0], XE.at[2], dev(ox, c, t)))
    across = dev(ox, c, ot)
    core = dev(xh, oc, t)
    tok_across = track(send(M_TOK, tok_in, TK.at[xh, c], across))
    tok_core = track(send(M_TOK + 1, tok_in, TK.at[xh, c], core))
    pos_copies = [
        track(send(M_POS + i, pos_in, PS.at[xh, c], where))
        for i, where in enumerate((core, dev(ox, c, t), dev(ox, oc, t)))
    ]
    cot_across = track(send(M_COT, cot_in, CT.at[xh, c], across))
    cot_core = track(send(M_COT + 1, cot_in, CT.at[xh, c], core))

    xw.wait_recv()
    ag1 = []
    for k in (2, 1, 3):
        here = W.at[z, y, :, :, HALF[0]]
        ag1.append(track(send(M_AG1 + k - 1, here, here, zdev(k))))
        here = W.at[z, y, :, :, HALF[1]]
        ag1.append(track(send(M_AG1 + 3 + k - 1, here, here, ydev(k))))
    xe.wait_recv()
    E[z, y] = (XE[1].astype(F32) + XE[2].astype(F32)).astype(BF16)
    for k in (2, 1, 3):
        ag1.append(track(send(M_AGE1 + k - 1, E.at[z, y], E.at[z, y], zdev(k))))
    tok_across.wait_recv()
    tok_pass = track(send(M_TOK + 2, TK.at[ox, c], TK.at[ox, c], core))
    for copy in ag1:
        copy.wait_recv()
    ag2 = []
    age2 = []
    for k in (2, 1, 3):
        age2.append(track(send(M_AGE2 + k - 1, E.at[:, y], E.at[:, y], ydev(k))))
    for part, (route, columns) in enumerate(PARTS):
        for k in (2, 1, 3):
            here = (W.at[:, y, :, :, columns], W.at[z, :, :, :, columns])[route]
            number = M_AG2 + 3 * part + k - 1
            ag2.append(track(send(number, here, here, (ydev, zdev)[route](k))))
    cot_across.wait_recv()
    cot_pass = track(send(M_COT + 2, CT.at[ox, c], CT.at[ox, c], core))
    for load in loads[12:]:
        load.wait()
    tok_core.wait_recv()
    tok_pass.wait_recv()

    for s in range(2):
        rows = TK[s].reshape(256, 512).astype(F32)
        centered = rows - jnp.mean(rows, axis=1, keepdims=True)
        moment = jnp.mean(centered * centered, axis=1, keepdims=True)
        rsq = lax.rsqrt(moment + EPS)
        NRM[s] = centered * rsq
        RSQ[s] = jnp.broadcast_to(rsq, (256, 128))

    for copy in pos_copies:
        copy.wait_recv()
    row8 = iota((8, 128), 0)
    inverse = jnp.zeros((8, 128), F32)
    for r in range(ROT // 2):
        inverse = jnp.where(row8 == r, float(np.float32(BASE ** (-2.0 * r / ROT))), inverse)
    ones, zeros = jnp.ones((48, 128), F32), jnp.zeros((48, 128), F32)
    for s in range(2):
        for b in range(2):
            places = PS[s, b].astype(F32)
            angle = jnp.broadcast_to(places, (8, 128)) * inverse
            cos, sin = jnp.cos(angle), jnp.sin(angle)
            part = pl.ds(b * 128, 128)
            COS[s, part] = jnp.concatenate([cos, cos, ones, cos, cos, ones], axis=0).T
            SIN[s, part] = jnp.concatenate([-sin, sin, zeros, -sin, sin, zeros], axis=0).T
            PCOL[s, part] = jnp.broadcast_to(places, (128, 128)).T

    cot_core.wait_recv()
    cot_pass.wait_recv()
    bias_grad = jnp.zeros((1, 512), F32)
    for s in range(2):
        grad = CT[s].reshape(256, 512)
        BTR[:, s * 256 : (s + 1) * 256] = grad.T
        bias_grad = bias_grad + jnp.sum(grad.astype(F32), axis=0, keepdims=True)

    for copy in age2:
        copy.wait_recv()
    per_z = []
    for zz in range(4):
        total = E[zz, 0].astype(F32)
        for yy in range(1, 4):
            total = total + E[zz, yy].astype(F32)
        per_z.append(total)
    vectors = jnp.concatenate(per_z, axis=1)
    all_z = per_z[0] + per_z[1] + per_z[2] + per_z[3]
    g1, b1, g2, b2 = (vectors[r : r + 1] for r in range(4))
    b_branch = vectors[4:5] + vectors[5:6]
    b_up = jnp.concatenate([all_z[6:7] + all_z[7:8], all_z[14:15] + all_z[15:16]], axis=1)
    b_qk = all_z[8:9] + all_z[9:10] + all_z[10:11] + all_z[11:12]
    b_v = (all_z[12:13] + all_z[13:14])[:, :HD]

    for s in range(2):
        n = NRM[s]
        normed = (n * g1 + b1).astype(BF16)
        mlp_input = (n * g2 + b2).astype(BF16)
        NB[s] = normed
        MB[s] = mlp_input
        NTR[:, s * 256 : (s + 1) * 256] = normed.T
        MTR[:, s * 256 : (s + 1) * 256] = mlp_input.T

    for copy in ag2[:6]:
        copy.wait_recv()

    def columns_of(columns, width):
        return W[:, :, :, :, columns].reshape(512, width)

    gb_up = jnp.zeros((1, 256), F32)
    for s in range(2):
        part = slice(s * 256, (s + 1) * 256)
        branch_grad = CT[s].reshape(256, 512)
        pre_act = dot_nn(MB[s], columns_of(UP, 256)) + b_up
        phi = 0.5 * (1.0 + lax.erf(pre_act * INV_ROOT_TWO))
        density = jnp.exp(-0.5 * pre_act * pre_act) * INV_ROOT_TWO_PI
        grad_hidden = dot_nn(branch_grad, columns_of(DN, 256))
        grad_pre = (grad_hidden * (phi + pre_act * density)).astype(BF16)
        gb_up = gb_up + jnp.sum(grad_pre.astype(F32), axis=0, keepdims=True)
        GC[part, UP] = grad_pre
        GC[part, DN] = (pre_act * phi).astype(BF16)

    rs1 = []

    def first_ring(part):
        route, columns = PARTS[part]
        for k in (2, 1, 3):
            src = (GS.at[:, (y + k) % 4, :, columns], GS.at[(z + k) % 4, :, :, columns])[route]
            dst = (RA1, RB1)[route].at[k - 1, :, :, local(columns)]
            rs1.append(track(send(M_RS1 + 3 * part + k - 1, src, dst, (ydev, zdev)[route](k))))

    def local(columns):
        return slice(columns.start % 384, (columns.stop - 1) % 384 + 1)

    GS[:, :, :, UP] = dot_nn(MTR[...], GC[:, UP]).astype(BF16).reshape(4, 4, 32, 256)
    first_ring(0)
    GS[:, :, :, DN] = dot_nn(BTR[...], GC[:, DN]).astype(BF16).reshape(4, 4, 32, 256)
    first_ring(1)

    for copy in ag2[6:]:
        copy.wait_recv()
    gb_qk = jnp.zeros((1, 128), F32)
    gb_v = jnp.zeros((1, HD), F32)
    for s in range(2):
        part = slice(s * 256, (s + 1) * 256)
        normed, branch_grad = NB[s], CT[s].reshape(256, 512)
        w_vo = columns_of(VO, 128)
        cos, sin = COS[s], SIN[s]
        qk = dot_nn(normed, columns_of(QK, 128)) + b_qk
        qk = (qk * cos + turn_partner(qk) * sin).astype(BF16)
        query, key = qk[:, :HD], qk[:, HD:]
        value = (dot_nn(normed, w_vo)[:, :HD] + b_v).astype(BF16)
        grad_att = dot_nn(branch_grad, w_vo)[:, HD:].astype(BF16)
        row, col = iota((256, 256), 0), iota((256, 256), 1)
        start = row.astype(F32) - jnp.concatenate([PCOL[s], PCOL[s]], axis=1)
        visible = (col <= row) & (col.astype(F32) >= start)
        scores = jnp.where(visible, dot_nt(query, key) * SCALE, MASKED)
        exps = jnp.exp(scores - jnp.max(scores, axis=1, keepdims=True))
        probs = exps / jnp.sum(exps, axis=1, keepdims=True)
        probs_low = probs.astype(BF16)
        attended = dot_nn(probs_low, value).astype(BF16)
        grad_probs = dot_nt(grad_att, value)
        row_dot = jnp.sum(probs * grad_probs, axis=1, keepdims=True)
        grad_scores = (probs * (grad_probs - row_dot)).astype(BF16)
        grad_query = dot_nn(grad_scores, key) * SCALE
        grad_key = dot_tn(grad_scores, query) * SCALE
        grad_value = dot_tn(probs_low, grad_att).astype(BF16)
        grad_qk = jnp.concatenate([grad_query, grad_key], axis=1)
        grad_qk = (grad_qk * cos - turn_partner(grad_qk) * sin).astype(BF16)
        gb_qk = gb_qk + jnp.sum(grad_qk.astype(F32), axis=0, keepdims=True)
        gb_v = gb_v + jnp.sum(grad_value.astype(F32), axis=0, keepdims=True)
        blank = jnp.zeros((256, HD), BF16)
        GC[part, QK] = grad_qk
        GVZ[part] = jnp.concatenate([grad_value, blank], axis=1)
        ATZ[part] = jnp.concatenate([blank, attended], axis=1)

    def rows_of(s):
        return pl.ds(pl.multiple_of(s * 256, 256), 256)

    out_core = []
    for i, s in enumerate((ox, xh)):
        part = rows_of(s)
        branch = dot_nt(GC[part, DN], columns_of(DN, 256)) + dot_nt(ATZ[part], columns_of(VO, 128))
        PO[s] = branch.astype(BF16).reshape(2, 128, 512)
        out_core.append(track(send(M_OUT + i, PO.at[s, oc], RO.at[s], core)))

    GS[:, :, :, QK] = dot_nn(NTR[...], GC[:, QK]).astype(BF16).reshape(4, 4, 32, 128)
    first_ring(2)
    grad_vo = dot_nn(NTR[...], GVZ[...]) + dot_nn(BTR[...], ATZ[...])
    GS[:, :, :, VO] = grad_vo.astype(BF16).reshape(4, 4, 32, 128)
    first_ring(3)

    def over_cores(s, own, received, total):
        total[s] = (own[s, c].astype(F32) + received[s].astype(F32)).astype(BF16)

    totals = [jnp.zeros((1, 512), F32) for _ in range(4)]
    dx_core = []
    for i, s in enumerate((ox, xh)):
        part = rows_of(s)
        n = NRM[s]
        grad_mlp = dot_nt(GC[part, UP], columns_of(UP, 256))
        grad_normed = dot_nt(GC[part, QK], columns_of(QK, 128)) + dot_nt(GVZ[part], columns_of(VO, 128))
        for j, term in enumerate((grad_normed * n, grad_normed, grad_mlp * n, grad_mlp)):
            totals[j] = totals[j] + jnp.sum(term, axis=0, keepdims=True)
        joined = grad_normed * g1 + grad_mlp * g2
        mean_one = jnp.mean(joined, axis=1, keepdims=True)
        mean_two = jnp.mean(joined * n, axis=1, keepdims=True)
        term = RSQ[s][:, :1] * (joined - mean_one - n * mean_two)
        PD[s] = term.astype(BF16).reshape(2, 128, 512)
        dx_core.append(track(send(M_DX + i, PD.at[s, oc], RD.at[s], core)))
        if i == 0:
            out_core[0].wait_recv()
            over_cores(ox, PO, RO, SO)
            out_across = track(send(M_OUT + 2, SO.at[ox], XO.at[0], dev(ox, c, ot)))

    up_rows = jnp.concatenate([gb_up[:, :128], gb_up[:, 128:]], axis=0)
    v_row = jnp.concatenate([gb_v, jnp.zeros((1, 128 - HD), F32)], axis=1)
    for zz in range(4):
        lanes = slice(zz * 128, (zz + 1) * 128)
        pieces = [total[:, lanes] for total in totals] + [bias_grad[:, lanes], gb_qk, v_row, up_rows]
        EG[zz] = jnp.concatenate(pieces + [jnp.zeros((7, 128), F32)], axis=0).astype(BF16)
    rse1 = [track(send(M_RSE1 + k - 1, EG, RE1.at[k - 1], ydev(k))) for k in (2, 1, 3)]

    dx_core[0].wait_recv()
    over_cores(ox, PD, RD, SD)
    parts_of_rows = (slice(0, 64), slice(64, 128))
    dx_across = [
        track(send(M_DX + 2 + i, SD.at[ox, part], XD.at[0, part], dev(ox, c, ot)))
        for i, part in enumerate(parts_of_rows)
    ]
    dx_core[1].wait_recv()
    over_cores(xh, PD, RD, SD)
    out_core[1].wait_recv()
    over_cores(xh, PO, RO, SO)

    def summed(own, received):
        total = own.astype(F32)
        for k in range(3):
            total = total + received[k].astype(F32)
        return total

    rs2 = []

    def second_ring(part):
        route, columns = PARTS[part]
        for copy in rs1[3 * part : 3 * part + 3]:
            copy.wait_recv()
        here = local(columns)
        if route == 0:
            SA[:, :, here] = summed(GS[:, y, :, columns], RA1[:, :, :, here]).astype(BF16)
        else:
            SB[:, :, here] = summed(GS[z, :, :, columns], RB1[:, :, :, here]).astype(BF16)
        for k in (2, 1, 3):
            src = (SA.at[(z + k) % 4, :, here], SB.at[(y + k) % 4, :, here])[route]
            dst = (RA2, RB2)[route].at[k - 1, :, here]
            rs2.append(track(send(M_RS2 + 3 * part + k - 1, src, dst, (zdev, ydev)[route](k))))

    second_ring(0)
    second_ring(1)
    second_ring(2)
    second_ring(3)
    out_across.wait_recv()
    TO[...] = (SO[xh].astype(F32) + XO[0].astype(F32)).astype(BF16)
    out_pair = track(send(M_OUT + 3, TO, XO.at[1], dev(xh, c, ot)))

    for copy in rse1:
        copy.wait_recv()
    SE[...] = summed(EG[...], RE1).astype(BF16)
    rse2 = [track(send(M_RSE2 + k - 1, SE.at[(z + k) % 4], RE2.at[k - 1], zdev(k))) for k in (2, 1, 3)]

    for copy in rs2:
        copy.wait_recv()
    FB[:, :, HALF[0]] = summed(SA[z], RA2).astype(BF16).reshape(2, 16, 384)
    FB[:, :, HALF[1]] = summed(SB[y], RB2).astype(BF16).reshape(2, 16, 384)
    fin = [
        track(send(M_FIN, FB.at[ox], XR.at[xh, c], dev(ox, c, t))),
        track(send(M_FIN + 1, FB.at[ox], XR.at[xh, c], dev(ox, oc, t))),
        track(send(M_FIN + 2, FB.at[xh], XR.at[xh, c], dev(xh, oc, t))),
    ]
    XR[xh, c] = FB[xh]
    for copy in rse2:
        copy.wait_recv()
    FE[...] = summed(SE[z], RE2).astype(BF16)
    fine = [track(send(M_FINE + i, FE, XF.at[t, xh, c], where)) for i, where in enumerate(group)]
    XF[t, xh, c] = FE[...]

    dx_pair = []
    for i, part in enumerate(parts_of_rows):
        dx_across[i].wait_recv()
        TD[part] = (SD[xh, part].astype(F32) + XD[0, part].astype(F32)).astype(BF16)
        dx_pair.append(track(send(M_DX + 4 + i, TD.at[part], XD.at[1, part], dev(xh, c, ot))))

    for copy in dx_pair:
        copy.wait_recv()
    gin_o[...] = CT[xh, c].astype(F32) + (TD[...].astype(F32) + XD[1].astype(F32))

    out_pair.wait_recv()
    total = TO[...].astype(F32) + XO[1].astype(F32)
    out_o[...] = (TK[xh, c].astype(F32) + (total + b_branch)).astype(BF16)

    for copy in fin:
        copy.wait_recv()
    for xx in range(2):
        both = [XR[xx, 0].astype(F32), XR[xx, 1].astype(F32)]
        lanes = slice(xx * 128, (xx + 1) * 128)
        low = iota((16, 128), 1) < HD

        def join(first, second):
            return jnp.where(low, first, pltpu.roll(second, HD, 1)), jnp.where(low, pltpu.roll(first, HD, 1), second)

        q_new, k_new = join(both[0][:, QK], both[1][:, QK])
        v_new, o_new = join(both[0][:, VO], both[1][:, VO])
        gqkvw_o[0, :, lanes] = q_new
        gqkvw_o[1, :, lanes] = k_new
        gqkvw_o[2, :, lanes] = v_new
        goutw_o[:, lanes] = o_new
        for cc in range(2):
            wide = slice((xx * 2 + cc) * 256, (xx * 2 + cc + 1) * 256)
            gupw_o[:, wide] = both[cc][:, UP]
            gdownw_o[:, wide] = both[cc][:, DN]

    for copy in fine:
        copy.wait_recv()
    tiles = [[[XF[tt, xx, cc].astype(F32) for cc in range(2)] for xx in range(2)] for tt in range(2)]
    whole = jnp.zeros((16, 128), F32)
    for tt in range(2):
        for xx in range(2):
            for cc in range(2):
                whole = whole + tiles[tt][xx][cc]
    whole = jnp.where(row16 == 4, tiles[0][0][0], whole)
    whole = pltpu.roll(whole, (128 - 16 * (y * 2 + xh)) % 128, 1)
    for row, ref in enumerate((gg1_o, gb1_o, gg2_o, gb2_o, gbias_o)):
        ref[...] = whole[row : row + 1, 0:16]
    j4, h4 = iota((2, 4), 0), iota((2, 4), 1)
    j16, h16 = iota((2, 16), 0), iota((2, 16), 1)
    new_qkv = [jnp.zeros((2, 4), F32) for _ in range(3)]
    new_up = jnp.zeros((2, 16), F32)
    for xx in range(2):
        for cc in range(2):
            head = xx * 2 + cc
            tile = jnp.where(t == 0, tiles[0][xx][cc], tiles[1][xx][cc])
            for j in range(2):
                low_col = jnp.sum(jnp.where(lane16 == 2 * place + j, tile, 0.0), axis=1, keepdims=True)
                high_col = jnp.sum(jnp.where(lane16 == HD + 2 * place + j, tile, 0.0), axis=1, keepdims=True)
                spot = (j4 == j) & (h4 == head)
                for which, item in enumerate((low_col[5:6], high_col[5:6], low_col[6:7])):
                    new_qkv[which] = jnp.where(spot, item, new_qkv[which])
                for u, item in enumerate((low_col[7:8], high_col[7:8], low_col[8:9], high_col[8:9])):
                    new_up = jnp.where((j16 == j) & (h16 == head * 4 + u), item, new_up)
    for which in range(3):
        gqkvb_o[which] = new_qkv[which]
    gupb_o[...] = new_up
    for copy in sent:
        copy.wait_send()


def place_results(*refs):
    ins, outs, sems = refs[:13], refs[13:27], refs[27]
    copies = [pltpu.make_async_copy(src, dst, sems.at[i]) for i, (src, dst) in enumerate(zip(ins + (ins[9],), outs))]
    for copy in copies:
        copy.start()
    for copy in copies:
        copy.wait()


def body(
    tokens, positions, cotangent, ln1_gain, ln1_bias, ln2_gain, ln2_bias, qkv_weight, qkv_bias, out_weight, out_bias,
    up_weight, up_bias, down_weight, down_bias,
):
    shape = jax.ShapeDtypeStruct
    row = shape((1, 16), F32)
    operands = (
        tokens, positions.reshape(1, 128), cotangent, ln1_gain, ln1_bias, ln2_gain, ln2_bias, qkv_weight[0],
        qkv_bias[0].transpose(0, 2, 1), out_weight[0].T, out_bias, up_weight[0], up_bias[0].T, down_weight[0].T,
        down_bias,
    )
    outs = (
        shape((128, 512), BF16), shape((128, 512), F32), row, row, row, row, shape((3, 16, 256), F32),
        shape((3, 2, 4), F32), shape((16, 256), F32), row, shape((16, 1024), F32), shape((2, 16), F32),
        shape((16, 1024), F32),
    )
    scratch = [
        *[((1, 16), BF16)] * 4, ((3, 16, 256), BF16), ((3, 2, 4), BF16), ((16, 256), BF16), ((1, 16), BF16),
        ((16, 1024), BF16), ((2, 16), BF16), ((16, 1024), BF16), ((1, 16), BF16),
        ((4, 4, 2, 16, 768), BF16), ((16, 768), BF16), ((4, 4, 16, 128), BF16), ((3, 16, 128), BF16),
        ((2, 2, 128, 512), BF16), ((2, 2, 128, 512), BF16), ((2, 2, 1, 128), jnp.int32), ((16, 128), F32),
        ((2, 256, 512), F32), ((2, 256, 128), F32), ((2, 256, 512), BF16), ((2, 256, 512), BF16),
        ((512, 512), BF16), ((512, 512), BF16), ((512, 512), BF16),
        ((2, 256, 128), F32), ((2, 256, 128), F32), ((2, 256, 128), F32),
        ((512, 768), BF16), ((512, 128), BF16), ((512, 128), BF16),
        ((2, 2, 128, 512), BF16), ((2, 128, 512), BF16), ((2, 128, 512), BF16), ((2, 128, 512), BF16),
        ((128, 512), BF16), ((2, 2, 128, 512), BF16), ((2, 128, 512), BF16), ((2, 128, 512), BF16),
        ((2, 128, 512), BF16), ((128, 512), BF16),
        ((4, 4, 32, 768), BF16), ((3, 4, 32, 384), BF16), ((3, 4, 32, 384), BF16), ((4, 32, 384), BF16),
        ((4, 32, 384), BF16), ((3, 32, 384), BF16), ((3, 32, 384), BF16),
        ((4, 16, 128), BF16), ((3, 4, 16, 128), BF16), ((4, 16, 128), BF16), ((3, 16, 128), BF16),
        ((2, 16, 768), BF16), ((2, 2, 16, 768), BF16), ((16, 128), BF16), ((2, 2, 2, 16, 128), BF16),
    ]
    results = pl.pallas_call(
        kernel,
        out_shape=outs,
        in_specs=[pl.BlockSpec(memory_space=pl.ANY)] * len(operands),
        out_specs=[pl.BlockSpec(memory_space=pltpu.VMEM)] * len(outs),
        scratch_shapes=[pltpu.VMEM(*item) for item in scratch]
        + [pltpu.SemaphoreType.DMA((M_ALL,)), pltpu.SemaphoreType.DMA((M_ALL,)), pltpu.SemaphoreType.DMA((15,))],
        compiler_params=pltpu.CompilerParams(
            collective_id=0, has_side_effects=True, vmem_limit_bytes=GRANT
        ),
    )(*(pltpu.with_memory_space_constraint(item, pltpu.HBM) for item in operands))
    results = pl.pallas_call(
        place_results,
        out_shape=outs + (row,),
        in_specs=[pl.BlockSpec(memory_space=pltpu.VMEM)] * 13,
        out_specs=[pl.BlockSpec(memory_space=pl.ANY)] * 14,
        scratch_shapes=[pltpu.SemaphoreType.DMA((14,))],
        compiler_params=pltpu.CompilerParams(vmem_limit_bytes=1024 * 1024),
    )(*results)
    (
        output, grad_input, grad_gain1, grad_shift1, grad_gain2, grad_shift2, grad_qkv, grad_qkv_bias, grad_out,
        grad_bias, grad_up, grad_up_bias, grad_down, grad_bias_again,
    ) = results
    return (
        output, grad_input, grad_gain1, grad_shift1, grad_gain2, grad_shift2, grad_qkv[None],
        grad_qkv_bias.transpose(0, 2, 1)[None], grad_out.T[None], grad_bias, grad_up[None], grad_up_bias.T[None],
        grad_down.T[None], grad_bias_again,
    )


def solution(mesh):
    row = P(None, "fsdp")
    tokens = P(("fsdp", "ctx"), None)
    qkv, qkv_bias = P(None, None, "fsdp", "tp"), P(None, None, "tp", "fsdp")
    fanned, spread = P(None, "tp", "fsdp"), P(None, "fsdp", "tp")
    in_specs = (
        tokens, P(("fsdp", "ctx")), tokens, row, row, row, row, qkv, qkv_bias, fanned, row, spread, fanned, fanned, row
    )
    out_specs = (
        tokens, tokens, row, row, row, row, qkv, qkv_bias, fanned, row, spread, fanned, fanned, row
    )
    return jax.shard_map(body, mesh=mesh, in_specs=in_specs, out_specs=out_specs, check_vma=False)
```

```python
import math

import jax
import jax.numpy as jnp
import numpy as np
from jax import lax
from jax.experimental import pallas as pl
from jax.experimental.pallas import tpu as pltpu
from jax.sharding import PartitionSpec as P

HD = 64
ROT = 16
EPS = 1e-05
BASE = 10000.0
MASKED = -1e30
SCALE = 1.0 / math.sqrt(HD)
INV_ROOT_TWO = 1.0 / math.sqrt(2.0)
INV_ROOT_TWO_PI = 1.0 / math.sqrt(2.0 * math.pi)
MESH = pl.DeviceIdType.MESH
F32 = jnp.float32
BF16 = jnp.bfloat16
GRANT = 40 * 1024 * 1024

UP = slice(0, 256)
QK = slice(256, 384)
DN = slice(384, 640)
VO = slice(640, 768)
HALF = (slice(0, 384), slice(384, 768))

PARTS = ((0, UP), (1, DN), (0, QK), (1, VO))

M_XW, M_XE = 0, 1
M_POS = 2
M_TOK = 5
M_COT = 8
M_AG1 = 12
M_AGE1 = 18
M_AG2 = 21
M_AGE2 = 33
M_OUT = 36
M_DX = 40
M_RS1 = 46
M_RSE1 = 58
M_RS2 = 61
M_RSE2 = 73
M_FIN = 76
M_FINE = 79
M_ALL = 86


def dot_nn(left, right):
    return lax.dot_general(left, right, (((1,), (0,)), ((), ())), preferred_element_type=F32)


def dot_nt(left, right):
    return lax.dot_general(left, right, (((1,), (1,)), ((), ())), preferred_element_type=F32)


def dot_tn(left, right):
    return lax.dot_general(left, right, (((0,), (0,)), ((), ())), preferred_element_type=F32)


def iota(shape, dim):
    return lax.broadcasted_iota(jnp.int32, shape, dim)


def turn_partner(pair):
    lane = iota(pair.shape, 1) % HD
    return jnp.where(
        lane < ROT // 2, pltpu.roll(pair, pair.shape[1] - ROT // 2, 1), pltpu.roll(pair, ROT // 2, 1)
    )


def kernel(
    tok_in, pos_in, cot_in, gain1_in, shift1_in, gain2_in, shift2_in, qkv_w_in, qkv_b_in, out_w_in, out_b_in, up_w_in,
    up_b_in, down_w_in, down_b_in,
    out_o, gin_o, gg1_o, gb1_o, gg2_o, gb2_o, gqkvw_o, gqkvb_o, goutw_o, gbias_o, gupw_o, gupb_o, gdownw_o,
    gain1, shift1, gain2, shift2, qkv_w, qkv_b, out_w, out_b, up_w, up_b, down_w, down_b,
    W, XS, E, XE, TK, CT, PS, SM,
    NRM, RSQ, NB, MB, NTR, MTR, BTR, COS, SIN, PCOL,
    GC, GVZ, ATZ, PO, RO, SO, XO, TO, PD, RD, SD, XD, TD,
    GS, RA1, RB1, SA, SB, RA2, RB2, EG, RE1, SE, RE2, FB, XR, FE, XF,
    ss, rs, ls,
):
    place = lax.axis_index("fsdp")
    z, y, xh = place // 8, (place // 2) % 4, place % 2
    c = lax.axis_index("ctx")
    t = lax.axis_index("tp")
    ox, oc, ot = 1 - xh, 1 - c, 1 - t

    def dev(xx, cc, tt, zz=z, yy=y):
        return {"fsdp": zz * 8 + yy * 2 + xx, "ctx": cc, "tp": tt}

    def zdev(k):
        return dev(xh, c, t, zz=(z + k) % 4)

    def ydev(k):
        return dev(xh, c, t, yy=(y + k) % 4)

    def send(number, src, dst, where):
        copy = pltpu.make_async_remote_copy(
            src_ref=src, dst_ref=dst, send_sem=ss.at[number], recv_sem=rs.at[number],
            device_id=where, device_id_type=MESH,
        )
        copy.start()
        return copy

    sent = []

    def track(copy):
        sent.append(copy)
        return copy

    barrier = pltpu.get_barrier_semaphore()
    group = [
        dev(xh, oc, t), dev(ox, c, t), dev(ox, c, ot), dev(ox, oc, t), dev(xh, c, ot), dev(xh, oc, ot), dev(ox, oc, ot)
    ]
    peers = group + [zdev(k) for k in (1, 2, 3)] + [ydev(k) for k in (1, 2, 3)]
    for peer in peers:
        pl.semaphore_signal(barrier, inc=1, device_id=peer, device_id_type=MESH)

    loads = []
    for i, (src, dst) in enumerate((
        (qkv_w_in, qkv_w), (out_w_in, out_w), (up_w_in, up_w), (down_w_in, down_w), (gain1_in, gain1),
        (shift1_in, shift1), (gain2_in, gain2), (shift2_in, shift2), (out_b_in, out_b), (down_b_in, down_b),
        (qkv_b_in, qkv_b), (up_b_in, up_b), (pos_in, PS.at[xh, c]), (tok_in, TK.at[xh, c]), (cot_in, CT.at[xh, c]),
    )):
        loads.append(pltpu.make_async_copy(src, dst, ls.at[i]))
        loads[-1].start()
    for load in loads[:4]:
        load.wait()

    def cut(xx):
        lanes = pl.ds(pl.multiple_of(xx * 128, 128), 128)
        q_pair, k_pair, v_pair, o_pair = (
            ref[:, lanes].astype(F32) for ref in (qkv_w.at[0], qkv_w.at[1], qkv_w.at[2], out_w)
        )
        low = iota((16, 128), 1) < HD
        first = c == 0

        def halves(a, b):
            a_low = jnp.where(first, a, pltpu.roll(a, HD, 1))
            b_high = jnp.where(first, pltpu.roll(b, HD, 1), b)
            return jnp.where(low, a_low, b_high).astype(BF16)

        wide = pl.ds(pl.multiple_of((xx * 2 + c) * 256, 256), 256)
        return up_w[:, wide], halves(q_pair, k_pair), down_w[:, wide], halves(v_pair, o_pair)

    for target, xx in ((XS, ox), (W.at[z, y, xh], xh)):
        up_cut, qk_cut, down_cut, vo_cut = cut(xx)
        target[:, UP] = up_cut
        target[:, QK] = qk_cut
        target[:, DN] = down_cut
        target[:, VO] = vo_cut

    pl.semaphore_wait(barrier, len(peers))

    xw = track(send(M_XW, XS, W.at[z, y, xh], dev(ox, c, t)))
    for load in loads[4:12]:
        load.wait()
    SM[...] = jnp.zeros((16, 128), F32)
    for row, ref in enumerate((gain1, shift1, gain2, shift2, out_b, down_b)):
        SM[row : row + 1, 0:16] = ref[...].astype(F32)
    for which in range(3):
        SM[8 + 2 * which : 10 + 2 * which, 0:4] = qkv_b[which].astype(F32)
    SM[6:8, 0:16] = up_b[...].astype(F32)
    SM[14:16, 0:16] = up_b[...].astype(F32)

    row16, lane16 = iota((16, 128), 0), iota((16, 128), 1)

    def placed(xx):
        raw = SM[...]
        head = xx * 2 + c

        def column(lane):
            return jnp.sum(jnp.where(lane16 == lane, raw, 0.0), axis=1, keepdims=True)

        spread = pltpu.roll(raw, 16 * (y * 2 + xh), 1)
        low = lane16 < HD
        hit = (lane16 % HD) == 2 * place + row16 % 2
        qkv = jnp.where(low != ((row16 == 10) | (row16 == 11)), column(head), 0.0)
        up_first = jnp.where(low, column(4 * head), column(4 * head + 1))
        up_second = jnp.where(low, column(4 * head + 2), column(4 * head + 3))
        bias = jnp.where(row16 < 8, up_first, jnp.where(row16 < 14, qkv, up_second))
        return jnp.where(row16 < 6, spread, jnp.where(hit, bias, 0.0))

    XE[0] = placed(ox).astype(BF16)
    xe = track(send(M_XE, XE.at[0], XE.at[2], dev(ox, c, t)))
    across = dev(ox, c, ot)
    core = dev(xh, oc, t)
    tok_across = track(send(M_TOK, tok_in, TK.at[xh, c], across))
    tok_core = track(send(M_TOK + 1, tok_in, TK.at[xh, c], core))
    pos_copies = [
        track(send(M_POS + i, pos_in, PS.at[xh, c], where))
        for i, where in enumerate((core, dev(ox, c, t), dev(ox, oc, t)))
    ]
    cot_across = track(send(M_COT, cot_in, CT.at[xh, c], across))
    cot_core = track(send(M_COT + 1, cot_in, CT.at[xh, c], core))

    XE[1] = placed(xh).astype(BF16)

    xw.wait_recv()
    ag1 = []
    for k in (2, 1, 3):
        here = W.at[z, y, :, :, HALF[0]]
        ag1.append(track(send(M_AG1 + k - 1, here, here, zdev(k))))
        here = W.at[z, y, :, :, HALF[1]]
        ag1.append(track(send(M_AG1 + 3 + k - 1, here, here, ydev(k))))
    xe.wait_recv()
    E[z, y] = (XE[1].astype(F32) + XE[2].astype(F32)).astype(BF16)
    for k in (2, 1, 3):
        ag1.append(track(send(M_AGE1 + k - 1, E.at[z, y], E.at[z, y], zdev(k))))
    tok_across.wait_recv()
    tok_pass = track(send(M_TOK + 2, TK.at[ox, c], TK.at[ox, c], core))
    for copy in ag1:
        copy.wait_recv()
    ag2 = []
    age2 = []
    for k in (2, 1, 3):
        age2.append(track(send(M_AGE2 + k - 1, E.at[:, y], E.at[:, y], ydev(k))))
    for part, (route, columns) in enumerate(PARTS):
        for k in (2, 1, 3):
            here = (W.at[:, y, :, :, columns], W.at[z, :, :, :, columns])[route]
            number = M_AG2 + 3 * part + k - 1
            ag2.append(track(send(number, here, here, (ydev, zdev)[route](k))))
    cot_across.wait_recv()
    cot_pass = track(send(M_COT + 2, CT.at[ox, c], CT.at[ox, c], core))
    for load in loads[12:]:
        load.wait()
    tok_core.wait_recv()
    tok_pass.wait_recv()

    for s in range(2):
        rows = TK[s].reshape(256, 512).astype(F32)
        centered = rows - jnp.mean(rows, axis=1, keepdims=True)
        moment = jnp.mean(centered * centered, axis=1, keepdims=True)
        rsq = lax.rsqrt(moment + EPS)
        NRM[s] = centered * rsq
        RSQ[s] = jnp.broadcast_to(rsq, (256, 128))

    for copy in pos_copies:
        copy.wait_recv()
    row8 = iota((8, 128), 0)
    inverse = jnp.zeros((8, 128), F32)
    for r in range(ROT // 2):
        inverse = jnp.where(row8 == r, float(np.float32(BASE ** (-2.0 * r / ROT))), inverse)
    ones, zeros = jnp.ones((48, 128), F32), jnp.zeros((48, 128), F32)
    for s in range(2):
        for b in range(2):
            places = PS[s, b].astype(F32)
            angle = jnp.broadcast_to(places, (8, 128)) * inverse
            cos, sin = jnp.cos(angle), jnp.sin(angle)
            part = pl.ds(b * 128, 128)
            COS[s, part] = jnp.concatenate([cos, cos, ones, cos, cos, ones], axis=0).T
            SIN[s, part] = jnp.concatenate([-sin, sin, zeros, -sin, sin, zeros], axis=0).T
            PCOL[s, part] = jnp.broadcast_to(places, (128, 128)).T

    cot_core.wait_recv()
    cot_pass.wait_recv()
    bias_grad = jnp.zeros((1, 512), F32)
    for s in range(2):
        grad = CT[s].reshape(256, 512)
        BTR[:, s * 256 : (s + 1) * 256] = grad.T
        bias_grad = bias_grad + jnp.sum(grad.astype(F32), axis=0, keepdims=True)

    for copy in age2:
        copy.wait_recv()
    per_z = []
    for zz in range(4):
        total = E[zz, 0].astype(F32)
        for yy in range(1, 4):
            total = total + E[zz, yy].astype(F32)
        per_z.append(total)
    vectors = jnp.concatenate(per_z, axis=1)
    all_z = per_z[0] + per_z[1] + per_z[2] + per_z[3]
    g1, b1, g2, b2 = (vectors[r : r + 1] for r in range(4))
    b_branch = vectors[4:5] + vectors[5:6]
    b_up = jnp.concatenate([all_z[6:7] + all_z[7:8], all_z[14:15] + all_z[15:16]], axis=1)
    b_qk = all_z[8:9] + all_z[9:10] + all_z[10:11] + all_z[11:12]
    b_v = (all_z[12:13] + all_z[13:14])[:, :HD]

    for s in range(2):
        n = NRM[s]
        normed = (n * g1 + b1).astype(BF16)
        mlp_input = (n * g2 + b2).astype(BF16)
        NB[s] = normed
        MB[s] = mlp_input
        NTR[:, s * 256 : (s + 1) * 256] = normed.T
        MTR[:, s * 256 : (s + 1) * 256] = mlp_input.T

    for copy in ag2[:6]:
        copy.wait_recv()

    def columns_of(columns, width):
        return W[:, :, :, :, columns].reshape(512, width)

    gb_up = jnp.zeros((1, 256), F32)
    for s in range(2):
        part = slice(s * 256, (s + 1) * 256)
        branch_grad = CT[s].reshape(256, 512)
        pre_act = dot_nn(MB[s], columns_of(UP, 256)) + b_up
        phi = 0.5 * (1.0 + lax.erf(pre_act * INV_ROOT_TWO))
        density = jnp.exp(-0.5 * pre_act * pre_act) * INV_ROOT_TWO_PI
        grad_hidden = dot_nn(branch_grad, columns_of(DN, 256))
        grad_pre = (grad_hidden * (phi + pre_act * density)).astype(BF16)
        gb_up = gb_up + jnp.sum(grad_pre.astype(F32), axis=0, keepdims=True)
        GC[part, UP] = grad_pre
        GC[part, DN] = (pre_act * phi).astype(BF16)

    rs1 = []

    def first_ring(part):
        route, columns = PARTS[part]
        for k in (2, 1, 3):
            src = (GS.at[:, (y + k) % 4, :, columns], GS.at[(z + k) % 4, :, :, columns])[route]
            dst = (RA1, RB1)[route].at[k - 1, :, :, local(columns)]
            rs1.append(track(send(M_RS1 + 3 * part + k - 1, src, dst, (ydev, zdev)[route](k))))

    def local(columns):
        return slice(columns.start % 384, (columns.stop - 1) % 384 + 1)

    GS[:, :, :, UP] = dot_nn(MTR[...], GC[:, UP]).astype(BF16).reshape(4, 4, 32, 256)
    first_ring(0)
    GS[:, :, :, DN] = dot_nn(BTR[...], GC[:, DN]).astype(BF16).reshape(4, 4, 32, 256)
    first_ring(1)

    for copy in ag2[6:]:
        copy.wait_recv()
    gb_qk = jnp.zeros((1, 128), F32)
    gb_v = jnp.zeros((1, HD), F32)
    for s in range(2):
        part = slice(s * 256, (s + 1) * 256)
        normed, branch_grad = NB[s], CT[s].reshape(256, 512)
        w_vo = columns_of(VO, 128)
        cos, sin = COS[s], SIN[s]
        qk = dot_nn(normed, columns_of(QK, 128)) + b_qk
        qk = (qk * cos + turn_partner(qk) * sin).astype(BF16)
        query, key = qk[:, :HD], qk[:, HD:]
        value = (dot_nn(normed, w_vo)[:, :HD] + b_v).astype(BF16)
        grad_att = dot_nn(branch_grad, w_vo)[:, HD:].astype(BF16)
        row, col = iota((256, 256), 0), iota((256, 256), 1)
        start = row.astype(F32) - jnp.concatenate([PCOL[s], PCOL[s]], axis=1)
        visible = (col <= row) & (col.astype(F32) >= start)
        scores = jnp.where(visible, dot_nt(query, key) * SCALE, MASKED)
        exps = jnp.exp(scores - jnp.max(scores, axis=1, keepdims=True))
        probs = exps / jnp.sum(exps, axis=1, keepdims=True)
        probs_low = probs.astype(BF16)
        attended = dot_nn(probs_low, value).astype(BF16)
        grad_probs = dot_nt(grad_att, value)
        row_dot = jnp.sum(probs * grad_probs, axis=1, keepdims=True)
        grad_scores = (probs * (grad_probs - row_dot)).astype(BF16)
        grad_query = dot_nn(grad_scores, key) * SCALE
        grad_key = dot_tn(grad_scores, query) * SCALE
        grad_value = dot_tn(probs_low, grad_att).astype(BF16)
        grad_qk = jnp.concatenate([grad_query, grad_key], axis=1)
        grad_qk = (grad_qk * cos - turn_partner(grad_qk) * sin).astype(BF16)
        gb_qk = gb_qk + jnp.sum(grad_qk.astype(F32), axis=0, keepdims=True)
        gb_v = gb_v + jnp.sum(grad_value.astype(F32), axis=0, keepdims=True)
        blank = jnp.zeros((256, HD), BF16)
        GC[part, QK] = grad_qk
        GVZ[part] = jnp.concatenate([grad_value, blank], axis=1)
        ATZ[part] = jnp.concatenate([blank, attended], axis=1)

    def rows_of(s):
        return pl.ds(pl.multiple_of(s * 256, 256), 256)

    out_core = []
    for i, s in enumerate((ox, xh)):
        part = rows_of(s)
        branch = dot_nt(GC[part, DN], columns_of(DN, 256)) + dot_nt(ATZ[part], columns_of(VO, 128))
        PO[s] = branch.astype(BF16).reshape(2, 128, 512)
        out_core.append(track(send(M_OUT + i, PO.at[s, oc], RO.at[s], core)))

    GS[:, :, :, QK] = dot_nn(NTR[...], GC[:, QK]).astype(BF16).reshape(4, 4, 32, 128)
    first_ring(2)
    grad_vo = dot_nn(NTR[...], GVZ[...]) + dot_nn(BTR[...], ATZ[...])
    GS[:, :, :, VO] = grad_vo.astype(BF16).reshape(4, 4, 32, 128)
    first_ring(3)

    def over_cores(s, own, received, total):
        total[s] = (own[s, c].astype(F32) + received[s].astype(F32)).astype(BF16)

    totals = [jnp.zeros((1, 512), F32) for _ in range(4)]
    dx_core = []
    for i, s in enumerate((ox, xh)):
        part = rows_of(s)
        n = NRM[s]
        grad_mlp = dot_nt(GC[part, UP], columns_of(UP, 256))
        grad_normed = dot_nt(GC[part, QK], columns_of(QK, 128)) + dot_nt(GVZ[part], columns_of(VO, 128))
        for j, term in enumerate((grad_normed * n, grad_normed, grad_mlp * n, grad_mlp)):
            totals[j] = totals[j] + jnp.sum(term, axis=0, keepdims=True)
        joined = grad_normed * g1 + grad_mlp * g2
        mean_one = jnp.mean(joined, axis=1, keepdims=True)
        mean_two = jnp.mean(joined * n, axis=1, keepdims=True)
        term = RSQ[s][:, :1] * (joined - mean_one - n * mean_two)
        PD[s] = term.astype(BF16).reshape(2, 128, 512)
        dx_core.append(track(send(M_DX + i, PD.at[s, oc], RD.at[s], core)))
        if i == 0:
            out_core[0].wait_recv()
            over_cores(ox, PO, RO, SO)
            out_across = track(send(M_OUT + 2, SO.at[ox], XO.at[0], dev(ox, c, ot)))

    dx_core[0].wait_recv()
    over_cores(ox, PD, RD, SD)
    parts_of_rows = (slice(0, 64), slice(64, 128))
    dx_across = [
        track(send(M_DX + 2 + i, SD.at[ox, part], XD.at[0, part], dev(ox, c, ot)))
        for i, part in enumerate(parts_of_rows)
    ]
    dx_core[1].wait_recv()
    over_cores(xh, PD, RD, SD)
    out_core[1].wait_recv()
    over_cores(xh, PO, RO, SO)

    up_rows = jnp.concatenate([gb_up[:, :128], gb_up[:, 128:]], axis=0)
    v_row = jnp.concatenate([gb_v, jnp.zeros((1, 128 - HD), F32)], axis=1)
    for zz in range(4):
        lanes = slice(zz * 128, (zz + 1) * 128)
        pieces = [total[:, lanes] for total in totals] + [bias_grad[:, lanes], gb_qk, v_row, up_rows]
        EG[zz] = jnp.concatenate(pieces + [jnp.zeros((7, 128), F32)], axis=0).astype(BF16)
    rse1 = [track(send(M_RSE1 + k - 1, EG, RE1.at[k - 1], ydev(k))) for k in (2, 1, 3)]

    def summed(own, received):
        total = own.astype(F32)
        for k in range(3):
            total = total + received[k].astype(F32)
        return total

    rs2 = []

    def second_ring(part):
        route, columns = PARTS[part]
        for copy in rs1[3 * part : 3 * part + 3]:
            copy.wait_recv()
        here = local(columns)
        if route == 0:
            SA[:, :, here] = summed(GS[:, y, :, columns], RA1[:, :, :, here]).astype(BF16)
        else:
            SB[:, :, here] = summed(GS[z, :, :, columns], RB1[:, :, :, here]).astype(BF16)
        for k in (2, 1, 3):
            src = (SA.at[(z + k) % 4, :, here], SB.at[(y + k) % 4, :, here])[route]
            dst = (RA2, RB2)[route].at[k - 1, :, here]
            rs2.append(track(send(M_RS2 + 3 * part + k - 1, src, dst, (zdev, ydev)[route](k))))

    second_ring(0)
    second_ring(1)
    second_ring(2)
    second_ring(3)
    out_across.wait_recv()
    TO[...] = (SO[xh].astype(F32) + XO[0].astype(F32)).astype(BF16)
    out_pair = track(send(M_OUT + 3, TO, XO.at[1], dev(xh, c, ot)))

    for copy in rse1:
        copy.wait_recv()
    SE[...] = summed(EG[...], RE1).astype(BF16)
    rse2 = [track(send(M_RSE2 + k - 1, SE.at[(z + k) % 4], RE2.at[k - 1], zdev(k))) for k in (2, 1, 3)]

    for copy in rs2:
        copy.wait_recv()
    FB[:, :, HALF[0]] = summed(SA[z], RA2).astype(BF16).reshape(2, 16, 384)
    FB[:, :, HALF[1]] = summed(SB[y], RB2).astype(BF16).reshape(2, 16, 384)
    fin = [
        track(send(M_FIN, FB.at[ox], XR.at[xh, c], dev(ox, c, t))),
        track(send(M_FIN + 1, FB.at[ox], XR.at[xh, c], dev(ox, oc, t))),
        track(send(M_FIN + 2, FB.at[xh], XR.at[xh, c], dev(xh, oc, t))),
    ]
    XR[xh, c] = FB[xh]
    for copy in rse2:
        copy.wait_recv()
    FE[...] = summed(SE[z], RE2).astype(BF16)
    fine = [track(send(M_FINE + i, FE, XF.at[t, xh, c], where)) for i, where in enumerate(group)]
    XF[t, xh, c] = FE[...]

    dx_pair = []
    for i, part in enumerate(parts_of_rows):
        dx_across[i].wait_recv()
        TD[part] = (SD[xh, part].astype(F32) + XD[0, part].astype(F32)).astype(BF16)
        dx_pair.append(track(send(M_DX + 4 + i, TD.at[part], XD.at[1, part], dev(xh, c, ot))))

    early = len(sent) - len(fin) - len(fine) - len(dx_pair)
    for copy in sent[:early]:
        copy.wait_send()

    out_pair.wait_recv()
    total = TO[...].astype(F32) + XO[1].astype(F32)
    out_o[...] = (TK[xh, c].astype(F32) + (total + b_branch)).astype(BF16)

    for copy in fin:
        copy.wait_recv()
    for xx in range(2):
        both = [XR[xx, 0].astype(F32), XR[xx, 1].astype(F32)]
        lanes = slice(xx * 128, (xx + 1) * 128)
        low = iota((16, 128), 1) < HD

        def join(first, second):
            return jnp.where(low, first, pltpu.roll(second, HD, 1)), jnp.where(low, pltpu.roll(first, HD, 1), second)

        q_new, k_new = join(both[0][:, QK], both[1][:, QK])
        v_new, o_new = join(both[0][:, VO], both[1][:, VO])
        gqkvw_o[0, :, lanes] = q_new
        gqkvw_o[1, :, lanes] = k_new
        gqkvw_o[2, :, lanes] = v_new
        goutw_o[:, lanes] = o_new
        for cc in range(2):
            wide = slice((xx * 2 + cc) * 256, (xx * 2 + cc + 1) * 256)
            gupw_o[:, wide] = both[cc][:, UP]
            gdownw_o[:, wide] = both[cc][:, DN]

    for copy in dx_pair:
        copy.wait_recv()
    gin_o[...] = CT[xh, c].astype(F32) + (TD[...].astype(F32) + XD[1].astype(F32))

    for copy in fine:
        copy.wait_recv()
    tiles = [[[XF[tt, xx, cc].astype(F32) for cc in range(2)] for xx in range(2)] for tt in range(2)]
    whole = jnp.zeros((16, 128), F32)
    for tt in range(2):
        for xx in range(2):
            for cc in range(2):
                whole = whole + tiles[tt][xx][cc]
    whole = jnp.where(row16 == 4, tiles[0][0][0], whole)
    whole = pltpu.roll(whole, (128 - 16 * (y * 2 + xh)) % 128, 1)
    for row, ref in enumerate((gg1_o, gb1_o, gg2_o, gb2_o, gbias_o)):
        ref[...] = whole[row : row + 1, 0:16]
    j4, h4 = iota((2, 4), 0), iota((2, 4), 1)
    j16, h16 = iota((2, 16), 0), iota((2, 16), 1)
    new_qkv = [jnp.zeros((2, 4), F32) for _ in range(3)]
    new_up = jnp.zeros((2, 16), F32)
    for xx in range(2):
        for cc in range(2):
            head = xx * 2 + cc
            tile = jnp.where(t == 0, tiles[0][xx][cc], tiles[1][xx][cc])
            for j in range(2):
                low_col = jnp.sum(jnp.where(lane16 == 2 * place + j, tile, 0.0), axis=1, keepdims=True)
                high_col = jnp.sum(jnp.where(lane16 == HD + 2 * place + j, tile, 0.0), axis=1, keepdims=True)
                spot = (j4 == j) & (h4 == head)
                for which, item in enumerate((low_col[5:6], high_col[5:6], low_col[6:7])):
                    new_qkv[which] = jnp.where(spot, item, new_qkv[which])
                for u, item in enumerate((low_col[7:8], high_col[7:8], low_col[8:9], high_col[8:9])):
                    new_up = jnp.where((j16 == j) & (h16 == head * 4 + u), item, new_up)
    for which in range(3):
        gqkvb_o[which] = new_qkv[which]
    gupb_o[...] = new_up
    for copy in sent[early:]:
        copy.wait_send()


def place_results(*refs):
    ins, outs, sems = refs[:13], refs[13:27], refs[27]
    copies = [pltpu.make_async_copy(src, dst, sems.at[i]) for i, (src, dst) in enumerate(zip(ins + (ins[9],), outs))]
    for copy in copies:
        copy.start()
    for copy in copies:
        copy.wait()


def body(
    tokens, positions, cotangent, ln1_gain, ln1_bias, ln2_gain, ln2_bias, qkv_weight, qkv_bias, out_weight, out_bias,
    up_weight, up_bias, down_weight, down_bias,
):
    shape = jax.ShapeDtypeStruct
    row = shape((1, 16), F32)
    operands = (
        tokens, positions.reshape(1, 128), cotangent, ln1_gain, ln1_bias, ln2_gain, ln2_bias, qkv_weight[0],
        qkv_bias[0].transpose(0, 2, 1), out_weight[0].T, out_bias, up_weight[0], up_bias[0].T, down_weight[0].T,
        down_bias,
    )
    outs = (
        shape((128, 512), BF16), shape((128, 512), F32), row, row, row, row, shape((3, 16, 256), F32),
        shape((3, 2, 4), F32), shape((16, 256), F32), row, shape((16, 1024), F32), shape((2, 16), F32),
        shape((16, 1024), F32),
    )
    scratch = [
        *[((1, 16), BF16)] * 4, ((3, 16, 256), BF16), ((3, 2, 4), BF16), ((16, 256), BF16), ((1, 16), BF16),
        ((16, 1024), BF16), ((2, 16), BF16), ((16, 1024), BF16), ((1, 16), BF16),
        ((4, 4, 2, 16, 768), BF16), ((16, 768), BF16), ((4, 4, 16, 128), BF16), ((3, 16, 128), BF16),
        ((2, 2, 128, 512), BF16), ((2, 2, 128, 512), BF16), ((2, 2, 1, 128), jnp.int32), ((16, 128), F32),
        ((2, 256, 512), F32), ((2, 256, 128), F32), ((2, 256, 512), BF16), ((2, 256, 512), BF16),
        ((512, 512), BF16), ((512, 512), BF16), ((512, 512), BF16),
        ((2, 256, 128), F32), ((2, 256, 128), F32), ((2, 256, 128), F32),
        ((512, 768), BF16), ((512, 128), BF16), ((512, 128), BF16),
        ((2, 2, 128, 512), BF16), ((2, 128, 512), BF16), ((2, 128, 512), BF16), ((2, 128, 512), BF16),
        ((128, 512), BF16), ((2, 2, 128, 512), BF16), ((2, 128, 512), BF16), ((2, 128, 512), BF16),
        ((2, 128, 512), BF16), ((128, 512), BF16),
        ((4, 4, 32, 768), BF16), ((3, 4, 32, 384), BF16), ((3, 4, 32, 384), BF16), ((4, 32, 384), BF16),
        ((4, 32, 384), BF16), ((3, 32, 384), BF16), ((3, 32, 384), BF16),
        ((4, 16, 128), BF16), ((3, 4, 16, 128), BF16), ((4, 16, 128), BF16), ((3, 16, 128), BF16),
        ((2, 16, 768), BF16), ((2, 2, 16, 768), BF16), ((16, 128), BF16), ((2, 2, 2, 16, 128), BF16),
    ]
    results = pl.pallas_call(
        kernel,
        out_shape=outs,
        in_specs=[pl.BlockSpec(memory_space=pl.ANY)] * len(operands),
        out_specs=[pl.BlockSpec(memory_space=pltpu.VMEM)] * len(outs),
        scratch_shapes=[pltpu.VMEM(*item) for item in scratch]
        + [pltpu.SemaphoreType.DMA((M_ALL,)), pltpu.SemaphoreType.DMA((M_ALL,)), pltpu.SemaphoreType.DMA((15,))],
        compiler_params=pltpu.CompilerParams(
            collective_id=0, has_side_effects=True, vmem_limit_bytes=GRANT
        ),
    )(*(pltpu.with_memory_space_constraint(item, pltpu.HBM) for item in operands))
    results = pl.pallas_call(
        place_results,
        out_shape=outs + (row,),
        in_specs=[pl.BlockSpec(memory_space=pltpu.VMEM)] * 13,
        out_specs=[pl.BlockSpec(memory_space=pl.ANY)] * 14,
        scratch_shapes=[pltpu.SemaphoreType.DMA((14,))],
        compiler_params=pltpu.CompilerParams(vmem_limit_bytes=1024 * 1024),
    )(*results)
    (
        output, grad_input, grad_gain1, grad_shift1, grad_gain2, grad_shift2, grad_qkv, grad_qkv_bias, grad_out,
        grad_bias, grad_up, grad_up_bias, grad_down, grad_bias_again,
    ) = results
    return (
        output, grad_input, grad_gain1, grad_shift1, grad_gain2, grad_shift2, grad_qkv[None],
        grad_qkv_bias.transpose(0, 2, 1)[None], grad_out.T[None], grad_bias, grad_up[None], grad_up_bias.T[None],
        grad_down.T[None], grad_bias_again,
    )


def solution(mesh):
    row = P(None, "fsdp")
    tokens = P(("fsdp", "ctx"), None)
    qkv, qkv_bias = P(None, None, "fsdp", "tp"), P(None, None, "tp", "fsdp")
    fanned, spread = P(None, "tp", "fsdp"), P(None, "fsdp", "tp")
    in_specs = (
        tokens, P(("fsdp", "ctx")), tokens, row, row, row, row, qkv, qkv_bias, fanned, row, spread, fanned, fanned, row
    )
    out_specs = (
        tokens, tokens, row, row, row, row, qkv, qkv_bias, fanned, row, spread, fanned, fanned, row
    )
    return jax.shard_map(body, mesh=mesh, in_specs=in_specs, out_specs=out_specs, check_vma=False)
```
